32 devices in a mesh: grp: 4 (over y, x), seq: 8 (over z, core).
Axes of the slice: x: 2, y: 2, z: 4, core: 2. Of those that a mesh axis runs over, the one named last changes fastest.
Arguments:
- tokens: bfloat16 [8192, 2048], P(('grp', 'seq')), may hold values from -6 to 6
- seq_lengths: int32 [4, 4], P('grp'), may hold values from 1 to 2045, as said below
- cotangent: bfloat16 [8192, 2048], P(('grp', 'seq')), may hold values from -6 to 6
- norm_gain: float32 [2048], replicated, may hold values from 0.5 to 1.5
- input_proj: bfloat16 [2048, 2048], P('seq'), may hold values from -0.125 to 0.125
- forget_proj: bfloat16 [2048, 2048], P('seq'), may hold values from -0.125 to 0.125
- forget_bias: float32 [2048], replicated, may hold values from -2 to 10
- gate_proj: bfloat16 [2048, 2048], P('seq'), may hold values from -0.125 to 0.125
- state_gain: float32 [2048], replicated, may hold values from 0.5 to 1.5
- out_proj: bfloat16 [2048, 2048], P('seq'), may hold values from -0.125 to 0.125
- mlp_gain: float32 [2048], replicated, may hold values from 0.5 to 1.5
- mlp_gate: bfloat16 [2048, 5632], P('seq'), may hold values from -0.125 to 0.125
- mlp_up: bfloat16 [2048, 5632], P('seq'), may hold values from -0.125 to 0.125
- mlp_down: bfloat16 [5632, 2048], P('seq'), may hold values from -0.078125 to 0.078125
Outputs:
- block_out: bfloat16 [8192, 2048], P(('grp', 'seq'))
- grad_tokens: float32 [8192, 2048], P(('grp', 'seq'))
- grad_norm_gain: float32 [2048], replicated
- grad_input_proj: float32 [2048, 2048], P('seq')
- grad_forget_proj: float32 [2048, 2048], P('seq')
- grad_forget_bias: float32 [2048], replicated
- grad_gate_proj: float32 [2048, 2048], P('seq')
- grad_state_gain: float32 [2048], replicated
- grad_out_proj: float32 [2048, 2048], P('seq')
- grad_mlp_gain: float32 [2048], replicated
- grad_mlp_gate: float32 [2048, 5632], P('seq')
- grad_mlp_up: float32 [2048, 5632], P('seq')
- grad_mlp_down: float32 [5632, 2048], P('seq')
The draws below stay inside these ranges and needn't reach their ends.
Inputs may be any that keep to these rules, and one draw needn't show every extreme that they name: `seq_lengths`: row g holds the lengths of the 4 sequences of group g in the order of its tokens; each row sums to 2048.
All inputs are finite; a program needn't handle non-finite values.
Results may differ from the reference program's by a relative error of at most 0.009.
Values may be sent and summed in bfloat16 or wider, within the bound.
No kernel may reach another device: no remote copies, remote signals or barrier semaphores. Data moves between devices by JAX's collectives and lax.ppermute only.
A program may use at most 512 MiB of HBM per device.

```python
from functools import partial
import jax
import jax.numpy as jnp
from jax import lax

D = 2048
FF = 5632
TOK_DEV = 256
SEQS = 4
GROUP_TOK = 2048
TOKENS = 8192
N_GRP = 4


def draw_seq_lengths(key, part):
    key = jax.random.fold_in(key, 11)
    long_key, short_key, group_key = jax.random.split(key, 3)
    longest = jax.random.randint(long_key, (N_GRP, 1), 0, SEQS)
    shorts = jax.random.randint(short_key, (N_GRP, SEQS), 1, TOK_DEV // SEQS + 1)
    tight_group = jax.random.randint(group_key, (), 0, N_GRP)
    groups = jnp.arange(N_GRP, dtype=jnp.int32)[:, None]
    shorts = jnp.where(groups == tight_group, 1, shorts)
    slots = jnp.arange(SEQS, dtype=jnp.int32)[None, :]
    shorts = jnp.where(slots == longest, 0, shorts)
    remain = GROUP_TOK - jnp.sum(shorts, axis=1, keepdims=True)
    return jnp.where(slots == longest, remain, shorts).astype(jnp.int32)


def draw_forget_bias(key, part):
    key = jax.random.fold_in(key, 23)
    return jax.random.uniform(key, (D,), jnp.float32, -2.0, 10.0)


def block_levels(own_key, shape, cuts, smallest, high):
    def one(axis_at, blocks):
        steps = jax.random.uniform(jax.random.fold_in(jax.random.fold_in(own_key, 6), axis_at), (blocks,), jnp.float32, smallest / len(cuts), high / len(cuts))
        return jnp.repeat(jnp.exp(steps), shape[axis_at] // blocks).reshape((-1,) + (1,) * (len(shape) - axis_at - 1))

    loudness = one(*cuts[0])
    for cut in cuts[1:]:
        loudness = loudness * one(*cut)
    return loudness


def normal_values(key, dims, scale, limit, pieces=(), kind=jnp.bfloat16):
    gain = block_levels(key, dims, pieces, -0.22, 0.18) if pieces else 1.0
    entries = jax.random.normal(key, dims, jnp.float32) * scale * gain
    return jnp.minimum(jnp.maximum(entries, -limit), limit).astype(kind)


def setup_inputs(seed: int = 0) -> dict:
    splits = jax.random.split(jax.random.key(seed), 15)
    return {
        "tokens": normal_values(splits[0], (TOKENS, D), 1.0, 6.0, ((0, 32),)),
        "seq_lengths": draw_seq_lengths(jax.random.fold_in(splits[14], 71), 0),
        "cotangent": normal_values(splits[2], (TOKENS, D), 1.0, 6.0, ((0, 32),)),
        "norm_gain": jnp.clip(1.0 + 0.1 * jax.random.normal(splits[3], (D,), jnp.float32), 0.5, 1.5),
        "input_proj": normal_values(splits[4], (D, D), D ** -0.5, 0.125, ((0, 8),)),
        "forget_proj": normal_values(splits[5], (D, D), D ** -0.5, 0.125, ((0, 8),)),
        "forget_bias": draw_forget_bias(jax.random.fold_in(splits[14], 71), 0),
        "gate_proj": normal_values(splits[7], (D, D), D ** -0.5, 0.125, ((0, 8),)),
        "state_gain": jnp.clip(1.0 + 0.1 * jax.random.normal(splits[8], (D,), jnp.float32), 0.5, 1.5),
        "out_proj": normal_values(splits[9], (D, D), D ** -0.5, 0.125, ((0, 8),)),
        "mlp_gain": jnp.clip(1.0 + 0.1 * jax.random.normal(splits[10], (D,), jnp.float32), 0.5, 1.5),
        "mlp_gate": normal_values(splits[11], (D, FF), D ** -0.5, 0.125, ((0, 8),)),
        "mlp_up": normal_values(splits[12], (D, FF), D ** -0.5, 0.125, ((0, 8),)),
        "mlp_down": normal_values(splits[13], (FF, D), FF ** -0.5, 0.078125, ((0, 8),)),
    }


LOWER = 0.9
EPSILON = 1e-06

@jax.custom_vjp
def low(v):
    return lax.optimization_barrier(v.astype(jnp.bfloat16)).astype(jnp.float32)

@jax.custom_vjp
def low_back(v):
    return v

def low_keep(v):
    return (low(v), None)

def low_pass(kept, grad):
    return (grad,)

def back_keep(v):
    return (v, None)

def back_low(kept, grad):
    return (low(grad),)
low.defvjp(low_keep, low_pass)
low_back.defvjp(back_keep, back_low)

def hdot(lhs_arr, rhs_arr):
    return jnp.dot(lhs_arr, rhs_arr, precision=lax.Precision.HIGHEST, preferred_element_type=jnp.float32)

def rms_scale(values, weights):
    return values * lax.rsqrt(lax.optimization_barrier(jnp.mean(values * values, axis=1, keepdims=True)) + EPSILON) * weights

def gates(keeping, proj_input, proj_forget, bias_term):
    forget = LOWER + (1.0 - LOWER) * jax.nn.sigmoid(proj_forget + bias_term)
    return (forget * keeping, jax.nn.silu(proj_input) * (1.0 - forget))

def carry_join(earlier, later):
    return (earlier[0] * later[0], later[0] * earlier[1] + later[1])

def forward(keeping, inputs, norm_gain, input_proj, forget_proj, forget_bias, gate_proj, state_gain, out_proj, mlp_gain, mlp_gate, mlp_up, mlp_down):
    normed = low(rms_scale(inputs, norm_gain))
    proj_input = low_back(hdot(normed, input_proj))
    proj_forget = low_back(hdot(normed, forget_proj))
    proj_gate = low_back(hdot(normed, gate_proj))
    decay, income = gates(keeping, proj_input, proj_forget, forget_bias)
    width = inputs.shape[1]
    decay_grp = decay.reshape(N_GRP, GROUP_TOK, width)
    income_grp = income.reshape(N_GRP, GROUP_TOK, width)
    states = lax.associative_scan(carry_join, (decay_grp, income_grp), axis=1)[1].reshape(TOKENS, width)
    gated = low(rms_scale(states, state_gain) * jax.nn.silu(proj_gate))
    mixed = low_back(hdot(gated, out_proj))
    middle = inputs + mixed
    normed_mid = low(rms_scale(middle, mlp_gain))
    gate_vals = low_back(hdot(normed_mid, mlp_gate))
    up_vals = low_back(hdot(normed_mid, mlp_up))
    hidden = low(jax.nn.silu(gate_vals) * up_vals)
    return middle + hdot(hidden, mlp_down)

def reference(tokens, seq_lengths, cotangent, norm_gain, input_proj, forget_proj, forget_bias, gate_proj, state_gain, out_proj, mlp_gain, mlp_gate, mlp_up, mlp_down):
    starts = (jnp.cumsum(seq_lengths, axis=1) - seq_lengths).astype(jnp.int32)
    positions = jnp.arange(GROUP_TOK, dtype=jnp.int32)
    hits = lax.optimization_barrier(jnp.sum((positions[None, :, None] == starts[:, None, :]).astype(jnp.float32), axis=2))
    keeping = (1.0 - hits).reshape(TOKENS, 1)
    result, pullback = jax.vjp(partial(forward, keeping), tokens.astype(jnp.float32), norm_gain.astype(jnp.float32), input_proj.astype(jnp.float32), forget_proj.astype(jnp.float32), forget_bias.astype(jnp.float32), gate_proj.astype(jnp.float32), state_gain.astype(jnp.float32), out_proj.astype(jnp.float32), mlp_gain.astype(jnp.float32), mlp_gate.astype(jnp.float32), mlp_up.astype(jnp.float32), mlp_down.astype(jnp.float32))
    grads = pullback(cotangent.astype(jnp.float32))
    return (result.astype(jnp.bfloat16), grads[0], grads[1], grads[2], grads[3], grads[4], grads[5], grads[6], grads[7], grads[8], grads[9], grads[10], grads[11])
```

```python
from functools import partial

import jax
import jax.numpy as jnp
from jax import lax
from jax.experimental import pallas as pl
from jax.experimental.pallas import tpu as pltpu
from jax.sharding import PartitionSpec as P

LOWER = 0.9
EPSILON = 1e-06
GRP = 4
LANE = 128
ROWS = 8
F32 = jnp.float32
BF16 = jnp.bfloat16
SWAP_X = [(0, 1), (1, 0), (2, 3), (3, 2)]
SWAP_Y = [(0, 2), (2, 0), (1, 3), (3, 1)]
SLOT = ((0, 1), (4, 3), (2, 6), (5, 7))
VMEM_LIMIT = 56 * 1024 * 1024


def matmul(lhs_arr, rhs_arr, out=F32):
    return jnp.dot(lhs_arr, rhs_arr, preferred_element_type=F32).astype(out)


def matmul_back(lhs_arr, rhs_arr, out=F32):
    return lax.dot_general(
        lhs_arr, rhs_arr, (((1,), (1,)), ((), ())), preferred_element_type=F32
    ).astype(out)


def outer_sum(lhs_arr, rhs_arr, out=BF16):
    return lax.dot_general(
        lhs_arr, rhs_arr, (((0,), (0,)), ((), ())), preferred_element_type=F32
    ).astype(out)


def rms_parts(values):
    return lax.rsqrt(jnp.mean(values * values, axis=1, keepdims=True) + EPSILON)


def rms_back(values, scale, weights, grad):
    weighted = values * grad
    inner = jnp.mean(weighted * weights, axis=1, keepdims=True)
    return scale * weights * grad - values * (scale * scale * scale * inner), jnp.sum(
        weighted * scale, axis=0
    )


def exchange(own):
    half = own.shape[0] // 2
    top, low = own[:half], own[half:]
    from_x = lax.ppermute(top, "grp", SWAP_X)
    from_y = lax.ppermute(low, "grp", SWAP_Y)
    tops = lax.ppermute(jnp.concatenate([top, from_x]), "grp", SWAP_Y)
    lows = lax.ppermute(jnp.concatenate([low, from_y]), "grp", SWAP_X)
    return top, low, from_x, from_y, tops[:half], tops[half:], lows[:half], lows[half:]


def gather_rows(own):
    top, low, from_x, from_y, y_top, across_top, x_low, across_low = exchange(own)
    return jnp.concatenate([top, low, y_top, x_low, from_x, across_top, from_y, across_low])


def gather_blocks(own):
    top, low, from_x, from_y, y_top, across_top, x_low, across_low = exchange(own)
    return jnp.concatenate(
        [top, low, from_x, x_low, y_top, from_y, across_top, across_low]
    ).reshape((GRP,) + own.shape)


def scatter_rows(multiply, rows):
    quarter = rows.shape[0] // 8
    to_x = multiply(rows[4 * quarter : 6 * quarter])
    to_y = multiply(rows[6 * quarter :])
    by_x = lax.ppermute(to_x.astype(BF16), "grp", SWAP_X)
    by_y = lax.ppermute(to_y.astype(BF16), "grp", SWAP_Y)
    kept = multiply(rows[: 4 * quarter])
    for_y = (kept[2 * quarter : 3 * quarter] + by_x[quarter:].astype(F32)).astype(BF16)
    for_x = (kept[3 * quarter :] + by_y[quarter:].astype(F32)).astype(BF16)
    last_y = lax.ppermute(for_y, "grp", SWAP_Y)
    last_x = lax.ppermute(for_x, "grp", SWAP_X)
    top = kept[:quarter] + by_x[:quarter].astype(F32) + last_y.astype(F32)
    low = kept[quarter : 2 * quarter] + by_y[:quarter].astype(F32) + last_x.astype(F32)
    return jnp.concatenate([top, low])


def by_relation(values, mine):
    values = jnp.where(mine % 2 == 1, values[jnp.array([1, 0, 3, 2])], values)
    return jnp.where(mine // 2 == 1, values[jnp.array([2, 3, 0, 1])], values)


def pick_columns(mine, matrices, parts, spread):
    rows, wide = matrices[0].shape
    piece = wide // (GRP * parts)
    own = wide // GRP
    count = len(matrices)
    step = min(rows, 64)

    def body(mine_ref, *refs):
        out_ref = refs[-1]
        for index, ref in enumerate(refs[:-1]):
            for which in range(GRP):

                @pl.when(mine_ref[0] == which)
                def _(index=index, ref=ref, which=which):
                    whole = ref[...].astype(F32)
                    picked = jnp.concatenate(
                        [
                            whole[:, (part * GRP + which) * piece : (part * GRP + which + 1) * piece]
                            for part in range(parts)
                        ],
                        axis=1,
                    ).astype(BF16)
                    if not spread:
                        out_ref[:, index * own : (index + 1) * own] = picked
                    else:
                        for turn in range(own // LANE):
                            at = (turn * count + index) * LANE
                            out_ref[:, at : at + LANE] = picked[:, turn * LANE : (turn + 1) * LANE]

    return pl.pallas_call(
        body,
        grid=(rows // step,),
        in_specs=[pl.BlockSpec(memory_space=pltpu.SMEM)]
        + [pl.BlockSpec((step, wide), lambda i: (i, 0))] * count,
        out_specs=pl.BlockSpec((step, own * count), lambda i: (i, 0)),
        out_shape=jax.ShapeDtypeStruct((rows, own * count), BF16),
        compiler_params=pltpu.CompilerParams(vmem_limit_bytes=VMEM_LIMIT),
        name="pick_columns",
    )(mine.reshape(1), *matrices)


def place_columns(mine, blocks, parts, count, spread):
    _, rows, wide = blocks.shape
    own = wide // count
    piece = own // parts
    step = min(rows, 32)

    def body(mine_ref, blocks_ref, *out_refs):
        for which in range(GRP):
            block = blocks_ref[mine_ref[0] ^ which].astype(F32)
            for index, out_ref in enumerate(out_refs):
                if spread:
                    turns = [
                        block[:, (turn * count + index) * LANE : (turn * count + index + 1) * LANE]
                        for turn in range(own // LANE)
                    ]
                    mat = jnp.concatenate(turns, axis=1)
                else:
                    mat = block[:, index * own : (index + 1) * own]
                for part in range(parts):
                    at = (part * GRP + which) * piece
                    out_ref[:, at : at + piece] = mat[:, part * piece : (part + 1) * piece]

    return pl.pallas_call(
        body,
        grid=(rows // step,),
        in_specs=[
            pl.BlockSpec(memory_space=pltpu.SMEM),
            pl.BlockSpec((GRP, step, wide), lambda i: (0, i, 0)),
        ],
        out_specs=[pl.BlockSpec((step, own * GRP), lambda i: (i, 0))] * count,
        out_shape=[jax.ShapeDtypeStruct((rows, own * GRP), F32)] * count,
        compiler_params=pltpu.CompilerParams(vmem_limit_bytes=VMEM_LIMIT),
        name="place_columns",
    )(mine.reshape(1), blocks)


def keep_rows(info_ref, owner, first, count):
    place = info_ref[0] + first + lax.broadcasted_iota(jnp.int32, (count, LANE), 0)
    keep = jnp.ones((count, LANE), F32)
    for one in range(GRP):
        keep = jnp.where(place == info_ref[2 + owner * GRP + one], 0.0, keep)
    return keep


def scan_forward(info, proj, bias):
    _, half, wide = proj.shape
    own = wide // 3
    tiles = half // ROWS

    def body(info_ref, proj_ref, bias_ref, prod_ref, state_ref, ends_ref):
        row = lax.broadcasted_iota(jnp.int32, (ROWS, LANE), 0)
        bias_row = bias_ref[...]

        def tile(part, step, carry):
            out = []
            for owner in range(GRP):
                slot = SLOT[owner][part]
                at = pl.ds(pl.multiple_of(step * ROWS, ROWS), ROWS)
                both = proj_ref[slot, at, : 2 * LANE]
                enter = both[:, :LANE]
                forget = LOWER + (1.0 - LOWER) * jax.nn.sigmoid(both[:, LANE:] + bias_row)
                decay = forget * keep_rows(info_ref, owner, part * half + step * ROWS, ROWS)
                income = enter * jax.nn.sigmoid(enter) * (1.0 - forget)
                for shift in (1, 2, 4):
                    fits = row >= shift
                    before = jnp.where(fits, pltpu.roll(income, shift, 0), 0.0)
                    factor = jnp.where(fits, pltpu.roll(decay, shift, 0), 1.0)
                    income = income + decay * before
                    decay = decay * factor
                prod, state = carry[owner]
                state_now = income + decay * state
                prod_now = decay * prod
                prod_ref[slot, at, :] = prod_now
                state_ref[slot, at, :] = state_now
                out.append((prod_now[ROWS - 1 :], state_now[ROWS - 1 :]))
            return tuple(out)

        carry = tuple(
            (jnp.ones((1, LANE), F32), jnp.zeros((1, LANE), F32)) for owner in range(GRP)
        )
        for part in range(2):
            carry = lax.fori_loop(0, tiles, partial(tile, part), carry)
        for owner in range(GRP):
            ends_ref[owner : owner + 1, :] = carry[owner][0]
            ends_ref[GRP + owner : GRP + owner + 1, :] = carry[owner][1]

    block = pl.BlockSpec((8, half, LANE), lambda j: (0, 0, j))
    return pl.pallas_call(
        body,
        grid=(own // LANE,),
        in_specs=[
            pl.BlockSpec(memory_space=pltpu.SMEM),
            pl.BlockSpec((8, half, 3 * LANE), lambda j: (0, 0, j)),
            pl.BlockSpec((1, LANE), lambda j: (0, j)),
        ],
        out_specs=[block, block, pl.BlockSpec((2 * GRP, LANE), lambda j: (0, j))],
        out_shape=[
            jax.ShapeDtypeStruct((8, half, own), F32),
            jax.ShapeDtypeStruct((8, half, own), F32),
            jax.ShapeDtypeStruct((2 * GRP, own), F32),
        ],
        compiler_params=pltpu.CompilerParams(vmem_limit_bytes=VMEM_LIMIT),
        name="scan_forward",
    )(info, proj, bias)


def entering_state(info_ref, ends_ref, count, backward):
    state = jnp.zeros((GRP, LANE), F32)
    order = range(count - 1, 0, -1) if backward else range(count - 1)
    for place in order:
        longer = ends_ref[place, GRP:, :] + ends_ref[place, :GRP, :] * state
        reached = place > info_ref[1] if backward else place < info_ref[1]
        state = jnp.where(reached, longer, state)
    return state


def finish_forward(info, ends, prod, state, proj, gain):
    _, half, own = prod.shape
    count = ends.shape[0]

    def body(info_ref, ends_ref, prod_ref, state_ref, proj_ref, gain_ref, states_ref, mix_ref, squares_ref, enter_ref):
        entering = entering_state(info_ref, ends_ref, count, False)
        enter_ref[...] = entering

        @pl.when(pl.program_id(0) == 0)
        def _():
            squares_ref[...] = jnp.zeros_like(squares_ref)

        for owner in range(GRP):
            for part in range(2):
                slot = SLOT[owner][part]
                states = state_ref[slot] + prod_ref[slot] * entering[owner : owner + 1]
                states_ref[slot] = states
                gate = proj_ref[slot]
                mix_ref[slot] = (states * gain_ref[...] * (gate * jax.nn.sigmoid(gate))).astype(BF16)
                squares_ref[slot] += jnp.sum(states * states, axis=1, keepdims=True)

    block = pl.BlockSpec((8, half, LANE), lambda j: (0, 0, j))
    return pl.pallas_call(
        body,
        grid=(own // LANE,),
        in_specs=[
            pl.BlockSpec(memory_space=pltpu.SMEM),
            pl.BlockSpec((count, 2 * GRP, LANE), lambda j: (0, 0, j)),
            block,
            block,
            pl.BlockSpec((8, half, LANE), lambda j: (0, 0, 3 * j + 2)),
            pl.BlockSpec((1, LANE), lambda j: (0, j)),
        ],
        out_specs=[
            block,
            block,
            pl.BlockSpec((8, half, 1), lambda j: (0, 0, 0)),
            pl.BlockSpec((GRP, LANE), lambda j: (0, j)),
        ],
        out_shape=[
            jax.ShapeDtypeStruct((8, half, own), F32),
            jax.ShapeDtypeStruct((8, half, own), BF16),
            jax.ShapeDtypeStruct((8, half, 1), F32),
            jax.ShapeDtypeStruct((GRP, own), F32),
        ],
        compiler_params=pltpu.CompilerParams(vmem_limit_bytes=VMEM_LIMIT),
        name="finish_forward",
    )(info, ends, prod, state, proj, gain)


def scan_backward(info, proj, bias, gain, states, back, coupling):
    _, half, wide = proj.shape
    own = wide // 3
    tiles = half // ROWS

    def body(info_ref, proj_ref, bias_ref, gain_ref, states_ref, back_ref, coupling_ref, prod_ref, grad_ref, ends_ref):
        row = lax.broadcasted_iota(jnp.int32, (ROWS, LANE), 0)
        bias_row = bias_ref[...]
        gain_row = gain_ref[...]

        def tile(part, turn, carry):
            step = tiles - 1 - turn
            out = []
            for owner in range(GRP):
                slot = SLOT[owner][part]
                at = pl.ds(pl.multiple_of(step * ROWS, ROWS), ROWS)
                both = proj_ref[slot, at, LANE:]
                gate = both[:, LANE:]
                forget = LOWER + (1.0 - LOWER) * jax.nn.sigmoid(both[:, :LANE] + bias_row)
                decay = forget * keep_rows(info_ref, owner, part * half + step * ROWS, ROWS)
                direct = (
                    gain_row * (gate * jax.nn.sigmoid(gate)) * back_ref[slot, at, :]
                    - states_ref[slot, at, :] * coupling_ref[slot, at, :]
                )
                flow = decay * direct
                for shift in (1, 2, 4):
                    fits = row < ROWS - shift
                    after = jnp.where(fits, pltpu.roll(flow, ROWS - shift, 0), 0.0)
                    factor = jnp.where(fits, pltpu.roll(decay, ROWS - shift, 0), 1.0)
                    flow = flow + decay * after
                    decay = decay * factor
                prod, grad = carry[owner]
                flow = flow + decay * grad
                decay = decay * prod
                last = row == ROWS - 1
                grad_ref[slot, at, :] = direct + jnp.where(last, grad, pltpu.roll(flow, ROWS - 1, 0))
                prod_ref[slot, at, :] = jnp.where(last, prod, pltpu.roll(decay, ROWS - 1, 0))
                out.append((decay[:1], flow[:1]))
            return tuple(out)

        carry = tuple(
            (jnp.ones((1, LANE), F32), jnp.zeros((1, LANE), F32)) for owner in range(GRP)
        )
        for part in (1, 0):
            carry = lax.fori_loop(0, tiles, partial(tile, part), carry)
        for owner in range(GRP):
            ends_ref[owner : owner + 1, :] = carry[owner][0]
            ends_ref[GRP + owner : GRP + owner + 1, :] = carry[owner][1]

    block = pl.BlockSpec((8, half, LANE), lambda j: (0, 0, j))
    vector = pl.BlockSpec((1, LANE), lambda j: (0, j))
    return pl.pallas_call(
        body,
        grid=(own // LANE,),
        in_specs=[
            pl.BlockSpec(memory_space=pltpu.SMEM),
            pl.BlockSpec((8, half, 3 * LANE), lambda j: (0, 0, j)),
            vector,
            vector,
            block,
            block,
            pl.BlockSpec((8, half, 1), lambda j: (0, 0, 0)),
        ],
        out_specs=[block, block, pl.BlockSpec((2 * GRP, LANE), lambda j: (0, j))],
        out_shape=[
            jax.ShapeDtypeStruct((8, half, own), F32),
            jax.ShapeDtypeStruct((8, half, own), F32),
            jax.ShapeDtypeStruct((2 * GRP, own), F32),
        ],
        compiler_params=pltpu.CompilerParams(vmem_limit_bytes=VMEM_LIMIT),
        name="scan_backward",
    )(info, proj, bias, gain, states, back, coupling)


def finish_backward(info, ends, prod, grad, proj, bias, gain, states, enter, back):
    _, half, own = prod.shape
    count = ends.shape[0]

    def body(info_ref, ends_ref, prod_ref, grad_ref, proj_ref, bias_ref, gain_ref, states_ref, enter_ref, back_ref, out_ref, sums_ref):
        entering = entering_state(info_ref, ends_ref, count, True)
        first = lax.broadcasted_iota(jnp.int32, (half, LANE), 0) == 0
        bias_sum = jnp.zeros((1, LANE), F32)
        gain_sum = jnp.zeros((1, LANE), F32)
        for owner in range(GRP):
            before = enter_ref[owner : owner + 1, :]
            for part in range(2):
                slot = SLOT[owner][part]
                states = states_ref[slot]
                previous = jnp.where(first, before, pltpu.roll(states, 1, 0))
                before = states[half - 1 :]
                total = grad_ref[slot] + prod_ref[slot] * entering[owner : owner + 1]
                enter = proj_ref[slot, :, :LANE]
                gate = proj_ref[slot, :, 2 * LANE :]
                sig = jax.nn.sigmoid(proj_ref[slot, :, LANE : 2 * LANE] + bias_ref[...])
                enter_sig = jax.nn.sigmoid(enter)
                gate_sig = jax.nn.sigmoid(gate)
                keep = keep_rows(info_ref, owner, part * half, half)
                grad_forget = total * (previous * keep - enter * enter_sig)
                grad_proj = grad_forget * ((1.0 - LOWER) * sig * (1.0 - sig))
                forget = LOWER + (1.0 - LOWER) * sig
                pull = back_ref[slot] * states
                out_ref[slot, :, :LANE] = (
                    total * (1.0 - forget) * (enter_sig * (1.0 + enter * (1.0 - enter_sig)))
                ).astype(BF16)
                out_ref[slot, :, LANE : 2 * LANE] = grad_proj.astype(BF16)
                out_ref[slot, :, 2 * LANE :] = (
                    pull * gain_ref[...] * (gate_sig * (1.0 + gate * (1.0 - gate_sig)))
                ).astype(BF16)
                bias_sum = bias_sum + jnp.sum(grad_proj, axis=0, keepdims=True)
                gain_sum = gain_sum + jnp.sum(pull * (gate * gate_sig), axis=0, keepdims=True)
        sums_ref[0:1, :] = bias_sum
        sums_ref[1:2, :] = gain_sum

    block = pl.BlockSpec((8, half, LANE), lambda j: (0, 0, j))
    wide = pl.BlockSpec((8, half, 3 * LANE), lambda j: (0, 0, j))
    vector = pl.BlockSpec((1, LANE), lambda j: (0, j))
    return pl.pallas_call(
        body,
        grid=(own // LANE,),
        in_specs=[
            pl.BlockSpec(memory_space=pltpu.SMEM),
            pl.BlockSpec((count, 2 * GRP, LANE), lambda j: (0, 0, j)),
            block,
            block,
            wide,
            vector,
            vector,
            block,
            pl.BlockSpec((GRP, LANE), lambda j: (0, j)),
            block,
        ],
        out_specs=[wide, pl.BlockSpec((2, LANE), lambda j: (0, j))],
        out_shape=[
            jax.ShapeDtypeStruct((8, half, 3 * own), BF16),
            jax.ShapeDtypeStruct((2, own), F32),
        ],
        compiler_params=pltpu.CompilerParams(vmem_limit_bytes=VMEM_LIMIT),
        name="finish_backward",
    )(info, ends, prod, grad, proj, bias, gain, states, enter, back)


def on_device(
    tokens,
    seq_lengths,
    cotangent,
    norm_gain,
    input_proj,
    forget_proj,
    forget_bias,
    gate_proj,
    state_gain,
    out_proj,
    mlp_gain,
    mlp_gate,
    mlp_up,
    mlp_down,
):
    tok_rows, width = tokens.shape
    half = tok_rows // 2
    parts = lax.axis_size("seq")
    mine, place = lax.axis_index("grp"), lax.axis_index("seq")
    own = width // GRP
    ff_own = mlp_gate.shape[1] // GRP

    def own_rows(matrix):
        count = matrix.shape[0] // GRP
        return lax.dynamic_slice_in_dim(matrix, mine * count, count, 0)

    def own_features(vector):
        cut = vector.reshape(parts, GRP, -1)
        return lax.dynamic_index_in_dim(cut, mine, 1, False).reshape(1, -1)

    def all_features(vector):
        cut = vector.reshape(parts, 1, -1)
        spread = jnp.where(jnp.arange(GRP)[None, :, None] == mine, cut, 0.0)
        return spread.reshape(-1)

    def whole(rows):
        return lax.all_gather(rows, "seq", axis=0, tiled=True)

    def reduced(grads):
        return lax.psum_scatter(grads, "seq", scatter_dimension=0, tiled=True)

    w_proj = whole(pick_columns(mine, (input_proj, forget_proj, gate_proj), parts, True))
    w_out = whole(own_rows(out_proj))
    w_ff = whole(pick_columns(mine, (mlp_gate, mlp_up), parts, False))
    w_down = whole(own_rows(mlp_down))

    lengths = lax.all_gather(seq_lengths, "grp", axis=0, tiled=True)
    starts = by_relation(jnp.cumsum(lengths, axis=1) - lengths, mine)
    info = jnp.concatenate([jnp.stack([place * tok_rows, place]), starts.reshape(-1)]).astype(jnp.int32)
    bias = own_features(forget_bias)
    gain = own_features(state_gain)

    inputs = tokens.astype(F32)
    scale_in = rms_parts(inputs)
    normed = gather_rows((inputs * scale_in * norm_gain).astype(BF16))
    cot = gather_rows(cotangent)

    proj = matmul(normed, w_proj).reshape(8, half, 3 * own)
    prod, state, ends = scan_forward(info, proj, bias)
    ends = lax.all_gather(ends, "seq")
    states, mix, squares, enter = finish_forward(info, ends, prod, state, proj, gain)
    mix = mix.reshape(GRP * tok_rows, own)
    squares = jnp.stack(
        [jnp.concatenate([squares[SLOT[k][0], :, 0], squares[SLOT[k][1], :, 0]]) for k in range(GRP)]
    )
    squares = lax.psum(by_relation(squares, mine), "grp")
    squares = lax.dynamic_index_in_dim(squares, mine, 0, False)
    scale_state = lax.rsqrt(squares / width + EPSILON)[:, None]

    raw = scatter_rows(partial(matmul, rhs_arr=w_out), mix)
    middle = inputs + raw * scale_state
    scale_mid = rms_parts(middle)
    normed_mid = gather_rows((middle * scale_mid * mlp_gain).astype(BF16))

    gate_vals = matmul(normed_mid, w_ff[:, :ff_own])
    up_vals = matmul(normed_mid, w_ff[:, ff_own:])
    gate_sig = jax.nn.sigmoid(gate_vals)
    gate_act = gate_vals * gate_sig
    hidden = (gate_act * up_vals).astype(BF16)
    block_out = (middle + scatter_rows(partial(matmul, rhs_arr=w_down), hidden)).astype(BF16)
    sum_down = reduced(outer_sum(hidden, cot))

    grad_hidden = matmul_back(cot, w_down)
    grad_gate = grad_hidden * up_vals * (gate_sig * (1.0 + gate_vals * (1.0 - gate_sig)))
    grad_up = grad_hidden * gate_act
    grad_ff = jnp.concatenate([grad_gate.astype(BF16), grad_up.astype(BF16)], axis=1)
    grad_normed_mid = scatter_rows(partial(matmul_back, rhs_arr=w_ff), grad_ff)
    sum_ff = reduced(outer_sum(normed_mid, grad_ff))

    back_mid, grad_mlp_gain = rms_back(middle, scale_mid, mlp_gain, grad_normed_mid)
    grad_middle = cotangent.astype(F32) + back_mid
    scaled_mix = (grad_middle * scale_state).astype(BF16)
    coupling = (
        scale_state[:, 0] * scale_state[:, 0] * scale_state[:, 0] * jnp.mean(raw * grad_middle, axis=1)
    )
    grad_mix = gather_rows(scaled_mix)
    coupling = by_relation(lax.all_gather(coupling, "grp"), mine).reshape(GRP, 2, half)
    order = [(k, h) for slot in range(8) for k in range(GRP) for h in range(2) if SLOT[k][h] == slot]
    coupling = jnp.stack([coupling[k, h] for k, h in order])[:, :, None]

    back = matmul_back(grad_mix, w_out).reshape(8, half, own)
    sum_out = reduced(outer_sum(mix, grad_mix))
    after, local, ends_back = scan_backward(info, proj, bias, gain, states, back, coupling)
    ends_back = lax.all_gather(ends_back, "seq")
    grad_proj, sums = finish_backward(
        info, ends_back, after, local, proj, bias, gain, states, enter, back
    )
    grad_proj = grad_proj.reshape(GRP * tok_rows, 3 * own)
    grad_normed = scatter_rows(partial(matmul_back, rhs_arr=w_proj), grad_proj)
    sum_proj = reduced(outer_sum(normed, grad_proj))
    back_in, grad_norm_gain = rms_back(inputs, scale_in, norm_gain, grad_normed)
    grad_tokens = grad_middle + back_in

    vectors = jnp.stack([grad_norm_gain, all_features(sums[0]), all_features(sums[1]), grad_mlp_gain])
    vectors = lax.psum(vectors, ("grp", "seq"))

    def whole_rows(summed):
        blocks = by_relation(gather_blocks(summed), mine)
        return blocks.reshape(-1, summed.shape[1]).astype(F32)

    grad_down = whole_rows(sum_down)
    grad_out = whole_rows(sum_out)
    grad_mlp_gate, grad_mlp_up = place_columns(mine, gather_blocks(sum_ff), parts, 2, False)
    grad_input, grad_forget, grad_gate_proj = place_columns(
        mine, gather_blocks(sum_proj), parts, 3, True
    )
    return (
        block_out,
        grad_tokens,
        vectors[0],
        grad_input,
        grad_forget,
        vectors[1],
        grad_gate_proj,
        vectors[2],
        grad_out,
        vectors[3],
        grad_mlp_gate,
        grad_mlp_up,
        grad_down,
    )


def solution(mesh):
    rows = P("seq", None)
    tokens = P(("grp", "seq"), None)
    return jax.shard_map(
        on_device,
        mesh=mesh,
        in_specs=(
            tokens,
            P("grp", None),
            tokens,
            P(),
            rows,
            rows,
            P(),
            rows,
            P(),
            rows,
            P(),
            rows,
            rows,
            rows,
        ),
        out_specs=(
            tokens,
            tokens,
            P(),
            rows,
            rows,
            P(),
            rows,
            P(),
            rows,
            P(),
            rows,
            rows,
            rows,
        ),
        check_vma=False,
    )
```

```python
from functools import partial

import jax
import jax.numpy as jnp
from jax import lax
from jax.experimental import pallas as pl
from jax.experimental.pallas import tpu as pltpu
from jax.sharding import PartitionSpec as P

LOWER = 0.9
EPSILON = 1e-06
GRP = 4
LANE = 128
ROWS = 8
F32 = jnp.float32
BF16 = jnp.bfloat16
SWAP_X = [(0, 1), (1, 0), (2, 3), (3, 2)]
SWAP_Y = [(0, 2), (2, 0), (1, 3), (3, 1)]
TO_X, TO_Y, KEPT = (2, 6), (5, 7), (0, 1, 3, 4)
VMEM_LIMIT = 56 * 1024 * 1024
NN = (((1,), (0,)), ((), ()))
NT = (((1,), (1,)), ((), ()))
TN = (((0,), (0,)), ((), ()))
COSTS = {"finish_mid": 200}
SMALL = pl.CostEstimate(flops=1024, bytes_accessed=1024, transcendentals=0)
ANY = pl.BlockSpec(memory_space=pl.ANY)
SMEM = pl.BlockSpec(memory_space=pltpu.SMEM)


def dot(lhs_arr, rhs_arr, dims):
    return lax.dot_general(lhs_arr, rhs_arr, dims, preferred_element_type=F32)


def call(body, name, grid, in_specs, out_specs, out_shape, args, deps=(), scratch=(), aliases=None):
    n_in, n_deps = len(in_specs), len(deps)

    def wrapped(*refs):
        body(*refs[:n_in], *refs[n_in + n_deps :])

    return pl.pallas_call(
        wrapped,
        grid=grid,
        in_specs=list(in_specs) + [ANY] * n_deps,
        out_specs=out_specs,
        out_shape=out_shape,
        scratch_shapes=list(scratch),
        compiler_params=pltpu.CompilerParams(vmem_limit_bytes=VMEM_LIMIT),
        input_output_aliases=aliases or {},
        cost_estimate=pl.CostEstimate(
            flops=COSTS.get(name, 1) * 1_000_000_000, bytes_accessed=1024, transcendentals=0
        ),
        name=name,
    )(*args, *deps)


def shape(dims, dtype):
    return jax.ShapeDtypeStruct(tuple(dims), dtype)


def whole_block(array):
    return pl.BlockSpec(array.shape, lambda *i: (0,) * len(array.shape))


def product(name, lhs_arr, rhs_arr, depth, first, wide, step, deps=()):
    rows = lhs_arr.shape[0]

    def body(lhs_ref, rhs_ref, out_ref):
        out_ref[...] = dot(lhs_ref[...], rhs_ref[...], NN)

    return call(
        body,
        name,
        (wide // step,),
        [
            pl.BlockSpec((rows, depth), lambda j: (0, 0)),
            pl.BlockSpec((depth, step), lambda j: (0, first // step + j)),
        ],
        pl.BlockSpec((rows, step), lambda j: (0, j)),
        shape((rows, wide), F32),
        (lhs_arr, rhs_arr),
        deps,
    )


def product_back(name, lhs_arr, rhs_arr, step, deps=()):
    rows = lhs_arr.shape[0]
    wide, depth = rhs_arr.shape

    def body(lhs_ref, rest_ref, rhs_ref, out_ref, sum_ref):
        out_ref[...] = dot(lhs_ref[...], rhs_ref[...], NT)

        @pl.when(pl.program_id(0) == 0)
        def _():
            sum_ref[...] = jnp.broadcast_to(join(rest_ref[...]), (rows, LANE))

    return call(
        body,
        name,
        (wide // step,),
        [
            pl.BlockSpec((rows, depth), lambda j: (0, 0)),
            pl.BlockSpec((rows, LANE), lambda j: (0, depth // LANE)),
            pl.BlockSpec((step, depth), lambda j: (j, 0)),
        ],
        [pl.BlockSpec((rows, step), lambda j: (0, j)), pl.BlockSpec((rows, LANE), lambda j: (0, 0))],
        [shape((rows, wide), F32), shape((rows, LANE), F32)],
        (lhs_arr, lhs_arr, rhs_arr),
        deps,
    )


def outer_sum(name, lhs_arr, rhs_arr, rows, wide, step, deps=()):
    depth = lhs_arr.shape[0]
    by_rows = step > 0
    step = abs(step)

    def body(lhs_ref, rhs_ref, out_ref):
        out_ref[...] = dot(lhs_ref[...], rhs_ref[...], TN).astype(BF16)

    if by_rows:
        grid = (rows // step,)
        specs = [
            pl.BlockSpec((depth, step), lambda j: (0, j)),
            pl.BlockSpec((depth, wide), lambda j: (0, 0)),
        ]
        out_spec = pl.BlockSpec((step, wide), lambda j: (j, 0))
    else:
        grid = (wide // step,)
        specs = [
            pl.BlockSpec((depth, rows), lambda j: (0, 0)),
            pl.BlockSpec((depth, step), lambda j: (0, j)),
        ]
        out_spec = pl.BlockSpec((rows, step), lambda j: (0, j))
    return call(body, name, grid, specs, out_spec, shape((rows, wide), BF16), (lhs_arr, rhs_arr), deps)


def outer_gate_out(normed, grad_gate, mix, grad_mix, parts, wide, deps=()):
    depth, own = mix.shape
    count = own // parts
    turns = wide // own

    def right(lhs_ref, rhs_ref, out_ref):
        out_ref[...] = dot(lhs_ref[...], rhs_ref[...], TN).astype(BF16).reshape(parts, count, own)

    half_done = call(
        right,
        "part_out",
        (turns,),
        [
            pl.BlockSpec((depth, own), lambda j: (0, 0)),
            pl.BlockSpec((depth, own), lambda j: (0, j)),
        ],
        pl.BlockSpec((parts, count, own), lambda j: (0, j, 1)),
        shape((parts, turns * count, 2 * own), BF16),
        (mix, grad_mix),
        deps,
    ).reshape(wide, 2 * own)

    def left(lhs_ref, rhs_ref, _, out_ref):
        out_ref[...] = dot(lhs_ref[...], rhs_ref[...], TN).astype(BF16)

    return call(
        left,
        "part_gate",
        (turns,),
        [
            pl.BlockSpec((depth, own), lambda j: (0, j)),
            pl.BlockSpec((depth, own), lambda j: (0, 0)),
            ANY,
        ],
        pl.BlockSpec((own, own), lambda j: (j, 0)),
        shape((wide, 2 * own), BF16),
        (normed, grad_gate, half_done),
        aliases={2: 0},
    )


def after(value, *events):
    return lax.optimization_barrier((value, events))[0]


def send_x(value):
    return lax.ppermute(value, "grp", SWAP_X)


def send_y(value):
    return lax.ppermute(value, "grp", SWAP_Y)


def lay(pieces, deps=()):
    if any(piece.shape[0] % 16 for piece in pieces):
        return jnp.concatenate(pieces)
    wide = pieces[0].shape[1]
    at = [0]
    for piece in pieces:
        at.append(at[-1] + piece.shape[0])
    deps = tuple(deps)

    def body(*refs):
        out_ref, sems = refs[-2], refs[-1]
        copies = [
            pltpu.make_async_copy(
                ref, out_ref.at[pl.ds(at[index], pieces[index].shape[0])], sems.at[index]
            )
            for index, ref in enumerate(refs[: len(pieces)])
        ]
        for copy in copies:
            copy.start()
        for copy in copies:
            copy.wait()

    return call(
        body,
        "lay",
        (),
        [pl.BlockSpec(memory_space=pltpu.VMEM)] * len(pieces),
        ANY,
        shape((at[-1], wide), pieces[0].dtype),
        tuple(pieces),
        deps,
        [pltpu.SemaphoreType.DMA((len(pieces),))],
    )


def start_gather(own):
    half = own.shape[0] // 2 if own.shape[0] % 16 else (own.shape[0] + 16) // 32 * 16
    top, low = own[:half], own[half:]
    x_top, y_low = send_x(top), send_y(low)
    x_low, y_top = send_x(low), send_y(top)
    return (top, low, x_top, x_low, y_top, y_low), x_top


def end_gather(held, deps=(), hold=()):
    top, low, x_top, x_low, y_top, y_low = held
    x_on, y_on = (x_top, y_low) if not hold else after((x_top, y_low), hold)
    across_top, across_low = send_y(x_on), send_x(y_on)
    return lay((top, low, x_top, x_low, y_top, y_low, across_top, across_low), deps)


def gather_rows(own, deps=(), hold=()):
    return end_gather(start_gather(own)[0], deps, hold)


def sum_everywhere(value):
    value = value + send_x(value)
    value = value + send_y(value)
    count = lax.axis_size("seq")
    step = 1
    while step < count:
        value = value + lax.ppermute(value, "seq", [(one, one ^ step) for one in range(count)])
        step *= 2
    return value


def gather_blocks(own, deps=(), hold=()):
    held, came = start_gather(own)
    return end_gather(held, deps, hold).reshape((GRP,) + own.shape), came


def split(column):
    high = column.astype(BF16).astype(F32)
    rest = column - high
    middle = rest.astype(BF16).astype(F32)
    lane = lax.broadcasted_iota(jnp.int32, column.shape, 1)
    zero = jnp.zeros_like(column)
    picked = jnp.where(lane == 0, high, jnp.where(lane == 1, middle, jnp.where(lane == 2, rest - middle, zero)))
    return picked.astype(BF16)


def join(block):
    return jnp.sum(block.astype(F32), axis=1, keepdims=True)


def partial_sums(name, dims, rows, weights, step, column=None, deps=(), stacked=None, firsts=(0, 0)):
    half = rows[0].shape[0] // 8
    pairs = len(rows)
    if stacked is not None:
        wide, parts, first = stacked
        own = rows[0].shape[1]
        specs = [pl.BlockSpec((parts, own // parts, step), lambda j: (0, j, first // step))]
    elif dims is NN:
        wide = weights[0].shape[1]
        specs = [pl.BlockSpec((one.shape[1], step), lambda j: (0, j)) for one in rows]
    else:
        wide = weights[0].shape[0]
        specs = [
            pl.BlockSpec((step, one.shape[1]), lambda j, at=at // one.shape[1]: (j, at))
            for one, at in zip(rows, firsts)
        ]
    extra = 0 if column is None else LANE
    columns = () if column is None else (column,)

    def pick(value, slots):
        return jnp.concatenate([value[slot * half : (slot + 1) * half] for slot in slots])

    def body(*refs):
        x_ref, y_ref, kept_ref = refs[-3:]
        at = pl.ds(pl.multiple_of(pl.program_id(0) * step, LANE), step)
        sums = None
        for rows_ref, weights_ref in zip(refs[:pairs], refs[pairs : 2 * pairs]):
            block = weights_ref[...]
            if stacked is not None:
                block = block.reshape(own, step)
            term = dot(rows_ref[...], block, dims)
            sums = term if sums is None else sums + term
        x_ref[:, at] = pick(sums, TO_X).astype(BF16)
        y_ref[:, at] = pick(sums, TO_Y).astype(BF16)
        kept_ref[...] = pick(sums, KEPT)
        if column is not None:

            @pl.when(pl.program_id(0) == 0)
            def _():
                x_ref[:, wide:] = split(pick(refs[-4], TO_X))
                y_ref[:, wide:] = split(pick(refs[-4], TO_Y))

    sent = shape((2 * half, wide + extra), BF16)
    return call(
        body,
        name,
        (wide // step,),
        [whole_block(one) for one in rows] + specs + [whole_block(one) for one in columns],
        [whole_block(sent), whole_block(sent), pl.BlockSpec((4 * half, step), lambda j: (0, j))],
        [sent, sent, shape((4 * half, wide), F32)],
        tuple(rows) + tuple(weights) + columns,
        deps,
    )


def merge(name, kept, by_x, by_y, column=None, deps=()):
    half = kept.shape[0] // 4
    wide = kept.shape[1]
    extra = 0 if column is None else LANE
    columns = () if column is None else (column,)

    def body(kept_ref, by_x_ref, by_y_ref, *refs):
        for_y_ref, for_x_ref = refs[-2:]
        for_y_ref[:, :wide] = (kept_ref[half:, :] + by_x_ref[:, :wide].astype(F32)).astype(BF16)
        for_x_ref[:, :wide] = (kept_ref[:half, :] + by_y_ref[:, :wide].astype(F32)).astype(BF16)
        if column is not None:
            for_y_ref[:, wide:] = split(refs[0][4 * half : 5 * half] + join(by_x_ref[:, wide:]))
            for_x_ref[:, wide:] = split(refs[0][3 * half : 4 * half] + join(by_y_ref[:, wide:]))

    again = shape((half, wide + extra), BF16)
    return call(
        body,
        name,
        (1,),
        [
            pl.BlockSpec((2 * half, wide), lambda j: (1, 0)),
            pl.BlockSpec((half, wide + extra), lambda j: (1, 0)),
            pl.BlockSpec((half, wide + extra), lambda j: (1, 0)),
        ]
        + [whole_block(one) for one in columns],
        [whole_block(again), whole_block(again)],
        [again, again],
        (kept, by_x, by_y) + columns,
        deps,
    )


def scattered_specs(pieces, step, turn=None):
    kept, by_x, by_y, last_y, last_x = pieces[:5]
    half = last_y.shape[0]
    count = half // step
    wide = by_x.shape[1]
    received = pl.BlockSpec((step, wide), lambda h, i: (i, 0))
    specs = [
        pl.BlockSpec((step, kept.shape[1]), lambda h, i: (h * count + i, 0)),
        received,
        received,
        received,
        received,
    ]
    if len(pieces) > 5:
        specs.append(pl.BlockSpec((step, LANE), lambda h, i: (h * count + i, 0)))
    return specs


def scattered_sum(refs, wide):
    top = pl.program_id(0) == 0
    first = jnp.where(top, refs[1][...].astype(F32), refs[2][...].astype(F32))
    second = jnp.where(top, refs[3][...].astype(F32), refs[4][...].astype(F32))
    came = first + second
    total = refs[0][...] + came[:, :wide]
    if len(refs) == 5:
        return total, None
    return total, refs[5][:, :1] + jnp.sum(came[:, wide:], axis=1, keepdims=True)


def own_block(step, count, wide):
    return pl.BlockSpec((step, wide), lambda h, i: (h * count + i, 0))


def finish_mix(pieces, tokens, gain, width):
    rows = tokens.shape[0]
    half = rows // 2
    step = min(half, 64)
    count = half // step

    def body(*refs):
        tokens_ref, gain_ref, middle_ref, normed_ref, raw_ref, scale_ref, scale_mid_ref = refs[-7:]
        raw, squares = scattered_sum(refs[:-7], width)
        scale = lax.rsqrt(squares / width + EPSILON)
        middle = tokens_ref[...].astype(F32) + raw * scale
        scale_mid = lax.rsqrt(jnp.mean(middle * middle, axis=1, keepdims=True) + EPSILON)
        middle_ref[...] = middle
        raw_ref[...] = raw
        normed_ref[...] = (middle * scale_mid * gain_ref[...]).astype(BF16)
        scale_ref[...] = scale
        scale_mid_ref[...] = scale_mid

    block = own_block(step, count, width)
    thin = own_block(step, count, 1)
    return call(
        body,
        "finish_mix",
        (2, count),
        scattered_specs(pieces, step) + [block, pl.BlockSpec((1, width), lambda h, i: (0, 0))],
        [block, block, block, thin, thin],
        [
            shape((rows, width), F32),
            shape((rows, width), BF16),
            shape((rows, width), F32),
            shape((rows, 1), F32),
            shape((rows, 1), F32),
        ],
        tuple(pieces) + (tokens, gain),
    )


def add_scattered(pieces, middle, out, width, deps=()):
    rows = middle.shape[0]
    half = rows // 2
    step = min(half, 64)
    count = half // step

    def body(*refs):
        middle_ref, out_ref = refs[-2:]
        out_ref[...] = (middle_ref[...] + scattered_sum(refs[:-2], width)[0]).astype(out)

    block = own_block(step, count, width)
    return call(
        body,
        "add_scattered",
        (2, count),
        scattered_specs(pieces, step) + [block],
        block,
        shape((rows, width), out),
        tuple(pieces) + (middle,),
        deps,
    )


def norm_back(values, scale, gain, grad):
    weighted = values * grad
    inner = jnp.mean(weighted * gain, axis=1, keepdims=True)
    back = scale * gain * grad - values * (scale * scale * scale * inner)
    return back, jnp.sum(weighted * scale, axis=0, keepdims=True)


def finish_mid(pieces, middle, cotangent, raw, scale, scale_mid, gain, width):
    rows = middle.shape[0]
    half = rows // 2
    step = min(half, 64)
    count = half // step

    def body(*refs):
        middle_ref, cot_ref, raw_ref, scale_ref, scale_mid_ref, gain_ref, grad_ref, send_ref, sum_ref = refs[-9:]
        grad, _ = scattered_sum(refs[:-9], width)
        back, gain_part = norm_back(middle_ref[...], scale_mid_ref[...], gain_ref[...], grad)
        grad_middle = cot_ref[...].astype(F32) + back
        scale = scale_ref[...]
        coupling = scale * scale * scale * jnp.mean(raw_ref[...] * grad_middle, axis=1, keepdims=True)
        grad_ref[...] = grad_middle
        send_ref[:, :width] = (grad_middle * scale).astype(BF16)
        send_ref[:, width:] = split(jnp.broadcast_to(coupling, (step, LANE)))

        @pl.when((pl.program_id(0) == 0) & (pl.program_id(1) == 0))
        def _():
            sum_ref[...] = jnp.zeros_like(sum_ref)

        sum_ref[...] += gain_part

    block = own_block(step, count, width)
    thin = own_block(step, count, 1)
    row = pl.BlockSpec((1, width), lambda h, i: (0, 0))
    return call(
        body,
        "finish_mid",
        (2, count),
        scattered_specs(pieces, step) + [block, block, block, thin, thin, row],
        [block, own_block(step, count, width + LANE), row],
        [shape((rows, width), F32), shape((rows, width + LANE), BF16), shape((1, width), F32)],
        tuple(pieces) + (middle, cotangent, raw, scale, scale_mid, gain),
    )


def finish_in(pieces, tokens, grad_middle, gain, width, deps=()):
    rows = tokens.shape[0]
    half = rows // 2
    step = min(half, 64)
    count = half // step

    def body(*refs):
        tokens_ref, middle_ref, gain_ref, out_ref, sum_ref = refs[-5:]
        grad, _ = scattered_sum(refs[:-5], width)
        values = tokens_ref[...].astype(F32)
        scale = lax.rsqrt(jnp.mean(values * values, axis=1, keepdims=True) + EPSILON)
        back, gain_part = norm_back(values, scale, gain_ref[...], grad)
        out_ref[...] = middle_ref[...] + back

        @pl.when((pl.program_id(0) == 0) & (pl.program_id(1) == 0))
        def _():
            sum_ref[...] = jnp.zeros_like(sum_ref)

        sum_ref[...] += gain_part

    block = own_block(step, count, width)
    row = pl.BlockSpec((1, width), lambda h, i: (0, 0))
    return call(
        body,
        "finish_in",
        (2, count),
        scattered_specs(pieces, step) + [block, block, row],
        [block, row],
        [shape((rows, width), F32), shape((1, width), F32)],
        tuple(pieces) + (tokens, grad_middle, gain),
        deps,
    )


def norm_in(tokens, starts, gain, width):
    rows = tokens.shape[0]
    step = min(rows, 64)

    def body(starts_ref, tokens_ref, gain_ref, out_ref):
        values = tokens_ref[...].astype(F32)
        scale = lax.rsqrt(jnp.mean(values * values, axis=1, keepdims=True) + EPSILON)
        out_ref[:, :width] = (values * scale * gain_ref[...]).astype(BF16)
        here = starts_ref[0] + pl.program_id(0) * step
        here = here + lax.broadcasted_iota(jnp.int32, (step, LANE), 0)
        keep = jnp.ones((step, LANE), F32)
        for one in range(1, starts.shape[0]):
            keep = jnp.where(here == starts_ref[one], 0.0, keep)
        out_ref[:, width:] = keep.astype(BF16)

    return call(
        body,
        "norm_in",
        (rows // step,),
        [SMEM, pl.BlockSpec((step, width), lambda i: (i, 0)), pl.BlockSpec((1, width), lambda i: (0, 0))],
        pl.BlockSpec((step, width + LANE), lambda i: (i, 0)),
        shape((rows, width + LANE), BF16),
        (starts, tokens, gain),
    )


def feed_forward(normed, weights, deps=()):
    rows, depth = normed.shape
    own = weights.shape[1] // 2

    def body(normed_ref, weights_ref, hidden_ref, by_gate_ref, by_up_ref):
        both = dot(normed_ref[...], weights_ref[...], NN)
        gate, up = both[:, :LANE], both[:, LANE:]
        sig = jax.nn.sigmoid(gate)
        act = gate * sig
        hidden_ref[...] = (act * up).astype(BF16)
        by_gate_ref[...] = up * (sig * (1.0 + gate * (1.0 - sig)))
        by_up_ref[...] = act

    block = pl.BlockSpec((rows, LANE), lambda j: (0, j))
    return call(
        body,
        "feed_forward",
        (own // LANE,),
        [whole_block(normed), pl.BlockSpec((depth, 2 * LANE), lambda j: (0, j))],
        [block, block, block],
        [shape((rows, own), BF16), shape((rows, own), F32), shape((rows, own), F32)],
        (normed, weights),
        deps,
    )


def feed_back(cot, weights, by_gate, by_up, deps=()):
    rows, depth = cot.shape
    own = weights.shape[0]
    step = min(rows, 256)

    def body(cot_ref, weights_ref, by_gate_ref, by_up_ref, out_ref):
        grad = dot(cot_ref[...], weights_ref[...], NT)
        for turn in range(own // LANE):
            part = slice(turn * LANE, (turn + 1) * LANE)
            out_ref[:, 2 * turn * LANE : (2 * turn + 1) * LANE] = (grad[:, part] * by_gate_ref[:, part]).astype(BF16)
            out_ref[:, (2 * turn + 1) * LANE : (2 * turn + 2) * LANE] = (grad[:, part] * by_up_ref[:, part]).astype(BF16)

    return call(
        body,
        "feed_back",
        (rows // step,),
        [
            pl.BlockSpec((step, depth), lambda j: (j, 0)),
            whole_block(weights),
            pl.BlockSpec((step, own), lambda j: (j, 0)),
            pl.BlockSpec((step, own), lambda j: (j, 0)),
        ],
        pl.BlockSpec((step, 2 * own), lambda j: (j, 0)),
        shape((rows, 2 * own), BF16),
        (cot, weights, by_gate, by_up),
        deps,
    )


def by_relation(values, mine):
    values = jnp.where(mine % 2 == 1, values[jnp.array([1, 0, 3, 2])], values)
    return jnp.where(mine // 2 == 1, values[jnp.array([2, 3, 0, 1])], values)


def pick_columns(mine, matrices, parts, spread, deps=()):
    rows, wide = matrices[0].shape
    piece = wide // (GRP * parts)
    own = wide // GRP
    count = len(matrices)
    step = min(rows, 64)

    def body(mine_ref, *refs):
        out_ref = refs[-1]
        for index, ref in enumerate(refs[:-1]):
            for which in range(GRP):

                @pl.when(mine_ref[0] == which)
                def _(index=index, ref=ref, which=which):
                    whole = ref[...].astype(F32)
                    picked = jnp.concatenate(
                        [
                            whole[:, (part * GRP + which) * piece : (part * GRP + which + 1) * piece]
                            for part in range(parts)
                        ],
                        axis=1,
                    ).astype(BF16)
                    if not spread:
                        out_ref[:, index * own : (index + 1) * own] = picked
                    else:
                        for turn in range(own // LANE):
                            at = (turn * count + index) * LANE
                            out_ref[:, at : at + LANE] = picked[:, turn * LANE : (turn + 1) * LANE]

    return call(
        body,
        "pick_columns",
        (rows // step,),
        [SMEM] + [pl.BlockSpec((step, wide), lambda i: (i, 0))] * count,
        pl.BlockSpec((step, own * count), lambda i: (i, 0)),
        shape((rows, own * count), BF16),
        (mine.reshape(1),) + tuple(matrices),
        deps,
    )


def pick_first(mine, input_proj, forget_proj, gate_proj, out_proj, parts):
    rows, wide = input_proj.shape
    piece = wide // (GRP * parts)
    own = wide // GRP
    count = rows // GRP

    def body(mine_ref, input_ref, forget_ref, gate_ref, out_ref, first_ref):
        at = pl.ds(pl.multiple_of(mine_ref[0] * count, count), count)
        first_ref[:, 3 * own :] = out_ref[at, :]
        for which in range(GRP):

            @pl.when(mine_ref[0] == which)
            def _(which=which):
                for index, ref in enumerate((input_ref, forget_ref, gate_ref)):
                    picked = jnp.concatenate(
                        [
                            ref[:, (part * GRP + which) * piece : (part * GRP + which + 1) * piece].astype(F32)
                            for part in range(parts)
                        ],
                        axis=1,
                    ).astype(BF16)
                    if index == 2:
                        first_ref[:, 2 * own : 3 * own] = picked
                        continue
                    for turn in range(own // LANE):
                        to = (2 * turn + index) * LANE
                        first_ref[:, to : to + LANE] = picked[:, turn * LANE : (turn + 1) * LANE]

    block = pl.BlockSpec((count, wide), lambda i: (i, 0))
    return call(
        body,
        "pick_first",
        (GRP,),
        [SMEM, block, block, block, pl.BlockSpec((rows, own), lambda i: (0, i))],
        pl.BlockSpec((count, 4 * own), lambda i: (i, 0)),
        shape((rows, 4 * own), BF16),
        (mine.reshape(1), input_proj, forget_proj, gate_proj, out_proj),
    )


def place_columns(mine, blocks, parts, count, own, spread):
    _, rows, _ = blocks.shape
    piece = own // parts
    step = min(rows, 32)

    def body(mine_ref, blocks_ref, *out_refs):
        for which in range(GRP):
            block = blocks_ref[mine_ref[0] ^ which].astype(F32)
            for index, out_ref in enumerate(out_refs):
                if spread:
                    turns = [
                        block[:, (turn * count + index) * LANE : (turn * count + index + 1) * LANE]
                        for turn in range(own // LANE)
                    ]
                    mat = jnp.concatenate(turns, axis=1)
                else:
                    mat = block[:, index * own : (index + 1) * own]
                for part in range(parts):
                    at = (part * GRP + which) * piece
                    out_ref[:, at : at + piece] = mat[:, part * piece : (part + 1) * piece]

    return pl.pallas_call(
        body,
        grid=(rows // step,),
        in_specs=[
            pl.BlockSpec(memory_space=pltpu.SMEM),
            pl.BlockSpec((GRP, step, own * count), lambda i: (0, i, 0)),
        ],
        out_specs=[pl.BlockSpec((step, own * GRP), lambda i: (i, 0))] * count,
        out_shape=[jax.ShapeDtypeStruct((rows, own * GRP), F32)] * count,
        compiler_params=pltpu.CompilerParams(vmem_limit_bytes=VMEM_LIMIT),
        cost_estimate=SMALL,
        name="place_columns",
    )(mine.reshape(1), blocks)


def scan_forward(keep, proj, bias):
    _, half, wide = proj.shape
    own = wide // 2
    tiles = half // ROWS

    def body(keep_ref, proj_ref, bias_ref, prod_ref, state_ref, ends_ref):
        row = lax.broadcasted_iota(jnp.int32, (ROWS, LANE), 0)
        bias_row = bias_ref[...]

        def tile(part, step, carry):
            out = []
            for owner in range(GRP):
                slot = 2 * owner + part
                at = pl.ds(pl.multiple_of(step * ROWS, ROWS), ROWS)
                both = proj_ref[slot, at, :]
                enter = both[:, :LANE]
                forget = LOWER + (1.0 - LOWER) * jax.nn.sigmoid(both[:, LANE:] + bias_row)
                decay = forget * keep_ref[slot, at, :]
                income = enter * jax.nn.sigmoid(enter) * (1.0 - forget)
                for shift in (1, 2, 4):
                    fits = row >= shift
                    before = jnp.where(fits, pltpu.roll(income, shift, 0), 0.0)
                    factor = jnp.where(fits, pltpu.roll(decay, shift, 0), 1.0)
                    income = income + decay * before
                    decay = decay * factor
                prod, state = carry[owner]
                state_now = income + decay * state
                prod_now = decay * prod
                prod_ref[slot, at, :] = prod_now
                state_ref[slot, at, :] = state_now
                out.append((prod_now[ROWS - 1 :], state_now[ROWS - 1 :]))
            return tuple(out)

        carry = tuple(
            (jnp.ones((1, LANE), F32), jnp.zeros((1, LANE), F32)) for owner in range(GRP)
        )
        for part in range(2):
            carry = lax.fori_loop(0, tiles, partial(tile, part), carry)
        for owner in range(GRP):
            ends_ref[owner : owner + 1, :] = carry[owner][0]
            ends_ref[GRP + owner : GRP + owner + 1, :] = carry[owner][1]

    block = pl.BlockSpec((8, half, LANE), lambda j: (0, 0, j))
    return pl.pallas_call(
        body,
        grid=(own // LANE,),
        in_specs=[
            pl.BlockSpec((8, half, LANE), lambda j: (0, 0, 0)),
            pl.BlockSpec((8, half, 2 * LANE), lambda j: (0, 0, j)),
            pl.BlockSpec((1, LANE), lambda j: (0, j)),
        ],
        out_specs=[block, block, pl.BlockSpec((2 * GRP, LANE), lambda j: (0, j))],
        out_shape=[
            jax.ShapeDtypeStruct((8, half, own), F32),
            jax.ShapeDtypeStruct((8, half, own), F32),
            jax.ShapeDtypeStruct((2 * GRP, own), F32),
        ],
        compiler_params=pltpu.CompilerParams(vmem_limit_bytes=VMEM_LIMIT),
        cost_estimate=SMALL,
        name="scan_forward",
    )(keep, proj, bias)


def entering_state(info_ref, ends_ref, parts, backward):
    here = info_ref[0]
    state = jnp.zeros((GRP, LANE), F32)
    for place in range(parts - 1, 0, -1) if backward else range(parts - 1):
        longer = ends_ref[place, GRP:, :] + ends_ref[place, :GRP, :] * state
        state = jnp.where(place > here if backward else place < here, longer, state)
    return state


def finish_forward(info, ends, prod, state, proj, gain, deps=()):
    _, half, own = prod.shape
    count = ends.shape[0]

    def body(info_ref, ends_ref, prod_ref, state_ref, proj_ref, gain_ref, states_ref, mix_ref, squares_ref, enter_ref):
        entering = entering_state(info_ref, ends_ref, count, False)
        enter_ref[...] = entering

        @pl.when(pl.program_id(0) == 0)
        def _():
            squares_ref[...] = jnp.zeros_like(squares_ref)

        for owner in range(GRP):
            for part in range(2):
                slot = 2 * owner + part
                states = state_ref[slot] + prod_ref[slot] * entering[owner : owner + 1]
                states_ref[slot] = states
                gate = proj_ref[slot]
                mix_ref[slot] = (states * gain_ref[...] * (gate * jax.nn.sigmoid(gate))).astype(BF16)
                squares_ref[slot] += states * states

        @pl.when(pl.program_id(0) == own // LANE - 1)
        def _():
            for slot in range(8):
                total = jnp.sum(squares_ref[slot], axis=1, keepdims=True)
                squares_ref[slot] = jnp.broadcast_to(total, (half, LANE))

    block = pl.BlockSpec((8, half, LANE), lambda j: (0, 0, j))
    return call(
        body,
        "finish_forward",
        (own // LANE,),
        [
            SMEM,
            pl.BlockSpec((count, 2 * GRP, LANE), lambda j: (0, 0, j)),
            block,
            block,
            block,
            pl.BlockSpec((1, LANE), lambda j: (0, j)),
        ],
        [
            block,
            block,
            pl.BlockSpec((8, half, LANE), lambda j: (0, 0, 0)),
            pl.BlockSpec((GRP, LANE), lambda j: (0, j)),
        ],
        [
            shape((8, half, own), F32),
            shape((8, half, own), BF16),
            shape((8, half, LANE), F32),
            shape((GRP, own), F32),
        ],
        (info, ends, prod, state, proj, gain),
        deps,
    )


def scan_backward(keep, proj, proj_gate, bias, gain, states, back, coupling):
    _, half, own = proj_gate.shape
    tiles = half // ROWS

    def body(
        keep_ref, proj_ref, gate_ref, bias_ref, gain_ref, states_ref, back_ref, coupling_ref,
        prod_ref, grad_ref, ends_ref, out_ref, sum_ref,
    ):
        row = lax.broadcasted_iota(jnp.int32, (ROWS, LANE), 0)
        bias_row = bias_ref[...]
        gain_row = gain_ref[...]

        def tile(part, turn, carry):
            step = tiles - 1 - turn
            out = []
            for owner in range(GRP):
                slot = 2 * owner + part
                at = pl.ds(pl.multiple_of(step * ROWS, ROWS), ROWS)
                gate = gate_ref[slot, at, :]
                forget = LOWER + (1.0 - LOWER) * jax.nn.sigmoid(proj_ref[slot, at, :] + bias_row)
                decay = forget * keep_ref[slot, at, :]
                direct = (
                    gain_row * (gate * jax.nn.sigmoid(gate)) * back_ref[slot, at, :]
                    - states_ref[slot, at, :] * coupling_ref[slot, at, :]
                )
                flow = decay * direct
                for shift in (1, 2, 4):
                    fits = row < ROWS - shift
                    later = jnp.where(fits, pltpu.roll(flow, ROWS - shift, 0), 0.0)
                    factor = jnp.where(fits, pltpu.roll(decay, ROWS - shift, 0), 1.0)
                    flow = flow + decay * later
                    decay = decay * factor
                prod, grad = carry[owner]
                flow = flow + decay * grad
                decay = decay * prod
                last = row == ROWS - 1
                grad_ref[slot, at, :] = direct + jnp.where(last, grad, pltpu.roll(flow, ROWS - 1, 0))
                prod_ref[slot, at, :] = jnp.where(last, prod, pltpu.roll(decay, ROWS - 1, 0))
                out.append((decay[:1], flow[:1]))
            return tuple(out)

        carry = tuple(
            (jnp.ones((1, LANE), F32), jnp.zeros((1, LANE), F32)) for owner in range(GRP)
        )
        for part in (1, 0):
            carry = lax.fori_loop(0, tiles, partial(tile, part), carry)
        for owner in range(GRP):
            ends_ref[owner : owner + 1, :] = carry[owner][0]
            ends_ref[GRP + owner : GRP + owner + 1, :] = carry[owner][1]
        gain_sum = jnp.zeros((1, LANE), F32)
        for slot in range(8):
            gate = gate_ref[slot]
            gate_sig = jax.nn.sigmoid(gate)
            pull = back_ref[slot] * states_ref[slot]
            out_ref[slot] = (pull * gain_row * (gate_sig * (1.0 + gate * (1.0 - gate_sig)))).astype(BF16)
            gain_sum = gain_sum + jnp.sum(pull * (gate * gate_sig), axis=0, keepdims=True)
        sum_ref[...] = gain_sum

    block = pl.BlockSpec((8, half, LANE), lambda j: (0, 0, j))
    vector = pl.BlockSpec((1, LANE), lambda j: (0, j))
    rows = pl.BlockSpec((8, half, LANE), lambda j: (0, 0, 0))
    return call(
        body,
        "scan_backward",
        (own // LANE,),
        [rows, pl.BlockSpec((8, half, LANE), lambda j: (0, 0, 2 * j + 1)), block, vector, vector, block, block, rows],
        [block, block, pl.BlockSpec((2 * GRP, LANE), lambda j: (0, j)), block, vector],
        [
            shape((8, half, own), F32),
            shape((8, half, own), F32),
            shape((2 * GRP, own), F32),
            shape((8, half, own), BF16),
            shape((1, own), F32),
        ],
        (keep, proj, proj_gate, bias, gain, states, back, coupling),
    )


def finish_backward(info, keep, ends, prod, grad, proj, bias, states, enter, deps=()):
    _, half, own = prod.shape
    parts = ends.shape[0]

    def body(info_ref, keep_ref, ends_ref, prod_ref, grad_ref, proj_ref, bias_ref, states_ref, enter_ref, out_ref, sum_ref):
        entering = entering_state(info_ref, ends_ref, parts, True)
        first = lax.broadcasted_iota(jnp.int32, (half, LANE), 0) == 0
        bias_sum = jnp.zeros((1, LANE), F32)
        for owner in range(GRP):
            before = enter_ref[owner : owner + 1, :]
            for part in range(2):
                slot = 2 * owner + part
                states = states_ref[slot]
                previous = jnp.where(first, before, pltpu.roll(states, 1, 0))
                before = states[half - 1 :]
                total = grad_ref[slot] + prod_ref[slot] * entering[owner : owner + 1]
                enter = proj_ref[slot, :, :LANE]
                sig = jax.nn.sigmoid(proj_ref[slot, :, LANE:] + bias_ref[...])
                enter_sig = jax.nn.sigmoid(enter)
                grad_forget = total * (previous * keep_ref[slot] - enter * enter_sig)
                grad_proj = grad_forget * ((1.0 - LOWER) * sig * (1.0 - sig))
                forget = LOWER + (1.0 - LOWER) * sig
                out_ref[slot, :, :LANE] = (
                    total * (1.0 - forget) * (enter_sig * (1.0 + enter * (1.0 - enter_sig)))
                ).astype(BF16)
                out_ref[slot, :, LANE:] = grad_proj.astype(BF16)
                bias_sum = bias_sum + jnp.sum(grad_proj, axis=0, keepdims=True)
        sum_ref[...] = bias_sum

    block = pl.BlockSpec((8, half, LANE), lambda j: (0, 0, j))
    pair = pl.BlockSpec((8, half, 2 * LANE), lambda j: (0, 0, j))
    vector = pl.BlockSpec((1, LANE), lambda j: (0, j))
    return call(
        body,
        "finish_backward",
        (own // LANE,),
        [
            SMEM,
            pl.BlockSpec((8, half, LANE), lambda j: (0, 0, 0)),
            pl.BlockSpec((parts, 2 * GRP, LANE), lambda j: (0, 0, j)),
            block,
            block,
            pair,
            vector,
            block,
            pl.BlockSpec((GRP, LANE), lambda j: (0, j)),
        ],
        [pair, vector],
        [shape((8, half, 2 * own), BF16), shape((1, own), F32)],
        (info, keep, ends, prod, grad, proj, bias, states, enter),
        deps,
    )


def place_rows(mine, blocks, deps=()):
    _, rows, wide = blocks.shape

    def body(mine_ref, blocks_ref, out_ref):
        out_ref[0] = blocks_ref[mine_ref[0] ^ pl.program_id(0)].astype(F32)

    return call(
        body,
        "place_rows",
        (GRP,),
        [SMEM, whole_block(blocks)],
        pl.BlockSpec((1, rows, wide), lambda j: (j, 0, 0)),
        shape((GRP, rows, wide), F32),
        (mine.reshape(1), blocks),
        deps,
    ).reshape(GRP * rows, wide)


def place_stacked(mine, blocks, first, own):
    _, rows, wide = blocks.shape
    count = rows // GRP

    def body(mine_ref, blocks_ref, out_ref):
        for which in range(GRP):
            out_ref[which * count : (which + 1) * count, :] = blocks_ref[mine_ref[0] ^ which].astype(F32)

    return call(
        body,
        "place_stacked",
        (GRP,),
        [SMEM, pl.BlockSpec((GRP, count, own), lambda j: (0, j, first // own))],
        pl.BlockSpec((rows, own), lambda j: (0, j)),
        shape((rows, GRP * own), F32),
        (mine.reshape(1), blocks),
    )


def on_device(
    tokens,
    seq_lengths,
    cotangent,
    norm_gain,
    input_proj,
    forget_proj,
    forget_bias,
    gate_proj,
    state_gain,
    out_proj,
    mlp_gain,
    mlp_gate,
    mlp_up,
    mlp_down,
):
    tok_rows, width = tokens.shape
    half = tok_rows // 2
    plane = GRP * tok_rows
    parts = lax.axis_size("seq")
    mine, place = lax.axis_index("grp"), lax.axis_index("seq")
    own = width // GRP

    def own_rows(matrix):
        count = matrix.shape[0] // GRP
        return lax.dynamic_slice_in_dim(matrix, mine * count, count, 0)

    def own_features(vector):
        cut = vector.reshape(parts, GRP, -1)
        return lax.dynamic_index_in_dim(cut, mine, 1, False).reshape(1, -1)

    def all_features(vector):
        cut = vector.reshape(parts, 1, -1)
        spread = jnp.where(jnp.arange(GRP)[None, :, None] == mine, cut, 0.0)
        return spread.reshape(-1)

    def whole(rows):
        return lax.all_gather(rows, "seq", axis=0, tiled=True)

    def reduced(grads):
        return lax.psum_scatter(grads, "seq", scatter_dimension=0, tiled=True)

    starts = (jnp.cumsum(seq_lengths[0]) - seq_lengths[0]).astype(jnp.int32)
    starts = jnp.concatenate([(place * tok_rows).reshape(1).astype(jnp.int32), starts])
    info = place.reshape(1).astype(jnp.int32)
    bias = own_features(forget_bias)
    gain = own_features(state_gain)
    in_gain, mid_gain = norm_gain.reshape(1, -1), mlp_gain.reshape(1, -1)

    w_first = whole(pick_first(mine, input_proj, forget_proj, gate_proj, out_proj, parts))
    normed = norm_in(tokens, starts, in_gain, width)
    normed = gather_rows(normed)
    ff_cols = pick_columns(mine, (mlp_gate, mlp_up), parts, True, (normed,))
    w_ff = whole(ff_cols)
    w_down = whole(own_rows(mlp_down))
    cot = gather_rows(after(cotangent, normed), deps=(ff_cols,))
    keep = normed[:, width:].astype(F32).reshape(8, half, LANE)

    proj = product("proj_pair", normed, w_first, width, 0, 2 * own, 256, (cot,)).reshape(8, half, 2 * own)
    prod, state, ends = scan_forward(keep, proj, bias)
    ends = lax.all_gather(ends, "seq")
    proj_gate = product("proj_gate", normed, w_first, width, 2 * own, own, 256, (prod,))
    proj_gate = proj_gate.reshape(8, half, own)
    states, mix, squares, enter = finish_forward(info, ends, prod, state, proj_gate, gain)
    mix, squares = mix.reshape(plane, own), squares.reshape(plane, LANE)
    w_stacked = w_first.reshape(parts, -1, 4 * own)
    to_x, to_y, kept = partial_sums(
        "mix", NN, (mix,), (w_stacked,), own, squares, stacked=(width, parts, 3 * own)
    )
    by_x, by_y = send_x(to_x), send_y(to_y)
    for_y, for_x = merge("mix_merge", kept, by_x, by_y, squares)
    pieces = (kept, by_x, by_y, send_y(for_y), send_x(for_x), squares)
    middle, normed_mid, raw, scale_state, scale_mid = finish_mix(pieces, tokens, mid_gain, width)
    normed_mid = gather_rows(normed_mid)
    w_out = w_stacked[:, :, 3 * own :].reshape(parts, GRP, -1, own).transpose(0, 2, 1, 3)
    w_out = w_out.reshape(own, width)

    hidden, by_gate, by_up = feed_forward(normed_mid, w_ff)
    part_down = outer_sum("part_down", hidden, cot, hidden.shape[1], width, -512)
    sum_down = reduced(part_down)

    to_x, to_y, kept_out = partial_sums("down", NN, (hidden,), (w_down,), 256, deps=(part_down,))
    by_x_out, by_y_out = send_x(to_x), send_y(to_y)
    grad_ff = feed_back(cot, w_down, by_gate, by_up, (to_x,))
    to_x, to_y, kept = partial_sums("grad_mid", NT, (grad_ff,), (w_ff,), 256)
    by_x, by_y = send_x(to_x), send_y(to_y)
    out_for_y, out_for_x = merge("down_merge", kept_out, by_x_out, by_y_out, deps=(to_x,))
    out_last_y, out_last_x = send_y(out_for_y), send_x(out_for_x)
    part_ff = outer_sum("part_ff", normed_mid, grad_ff, width, grad_ff.shape[1], 256, (out_for_y,))
    sum_ff = reduced(part_ff)
    for_y, for_x = merge("grad_mid_merge", kept, by_x, by_y, deps=(part_ff,))
    pieces = (kept, by_x, by_y, send_y(for_y), send_x(for_x))
    grad_middle, scaled_mix, grad_mlp_gain = finish_mid(
        pieces, middle, cotangent, raw, scale_state, scale_mid, mid_gain, width
    )
    pieces_out = (kept_out, by_x_out, by_y_out, out_last_y, out_last_x)
    grad_mix = gather_rows(scaled_mix)

    back, coupling = product_back("back", grad_mix, w_out, 256)
    after_prod, local, ends_back, grad_gate, gain_sum = scan_backward(
        keep,
        proj,
        proj_gate,
        bias,
        gain,
        states,
        back.reshape(8, half, own),
        coupling.reshape(8, half, LANE),
    )
    ends_back = lax.all_gather(ends_back, "seq")
    blocks_down, _ = gather_blocks(after(sum_down, grad_mix), (ends_back,), (after_prod,))
    block_out = add_scattered(pieces_out, middle, BF16, width, (blocks_down,))
    grad_gate = grad_gate.reshape(plane, own)
    part_gate_out = outer_gate_out(normed, grad_gate, mix, grad_mix, parts, width, (block_out,))
    sum_gate_out = reduced(part_gate_out)
    grad_pair, bias_sum = finish_backward(
        info, keep, ends_back, after_prod, local, proj, bias, states, enter, (part_gate_out,)
    )
    grad_pair = grad_pair.reshape(plane, 2 * own)
    held, came_ff = start_gather(after(sum_ff, blocks_down))
    part_pair = outer_sum("part_pair", normed, grad_pair, width, 2 * own, 256, (came_ff,))
    sum_pair = reduced(part_pair)
    to_x, to_y, kept = partial_sums(
        "grad_in",
        NT,
        (grad_pair, grad_gate),
        (w_first, w_first),
        256,
        deps=(part_pair,),
        firsts=(0, 2 * own),
    )
    by_x, by_y = send_x(to_x), send_y(to_y)
    blocks_ff = end_gather(held, (to_x,), (grad_pair,)).reshape((GRP,) + sum_ff.shape)
    grad_down = place_rows(mine, blocks_down, (to_x,))
    for_y, for_x = merge("grad_in_merge", kept, by_x, by_y, deps=(grad_down, blocks_ff))
    last_y, last_x = send_y(for_y), send_x(for_x)
    pieces = (kept, by_x, by_y, last_y, last_x)
    grad_tokens, grad_norm_gain = finish_in(pieces, tokens, grad_middle, in_gain, width)
    vectors = sum_everywhere(
        jnp.stack(
            [grad_norm_gain[0], all_features(bias_sum), all_features(gain_sum), grad_mlp_gain[0]]
        )
    )
    blocks_gate_out, came = gather_blocks(after(sum_gate_out, by_y))
    grad_mlp_gate, grad_mlp_up = place_columns(mine, blocks_ff, parts, 2, w_ff.shape[1] // 2, True)
    (grad_gate_proj,) = place_columns(mine, blocks_gate_out, parts, 1, own, True)
    grad_out = place_stacked(mine, blocks_gate_out, own, own)
    blocks_pair, _ = gather_blocks(after(sum_pair, came), (grad_mlp_gate, grad_gate_proj, grad_out))
    grad_input, grad_forget = place_columns(mine, blocks_pair, parts, 2, own, True)
    return (
        block_out,
        grad_tokens,
        vectors[0],
        grad_input,
        grad_forget,
        vectors[1],
        grad_gate_proj,
        vectors[2],
        grad_out,
        vectors[3],
        grad_mlp_gate,
        grad_mlp_up,
        grad_down,
    )


def solution(mesh):
    rows = P("seq", None)
    tokens = P(("grp", "seq"), None)
    return jax.shard_map(
        on_device,
        mesh=mesh,
        in_specs=(
            tokens,
            P("grp", None),
            tokens,
            P(),
            rows,
            rows,
            P(),
            rows,
            P(),
            rows,
            P(),
            rows,
            rows,
            rows,
        ),
        out_specs=(
            tokens,
            tokens,
            P(),
            rows,
            rows,
            P(),
            rows,
            P(),
            rows,
            P(),
            rows,
            rows,
            rows,
        ),
        check_vma=False,
    )
```

```python
import math
from functools import partial

import jax
import jax.numpy as jnp
from jax import lax
from jax.experimental import pallas as pl
from jax.experimental.pallas import tpu as pltpu
from jax.sharding import PartitionSpec as P

LOWER = 0.9
EPSILON = 1e-06
GRP = 4
LANE = 128
ROWS = 8
F32 = jnp.float32
BF16 = jnp.bfloat16
SWAP_X = [(0, 1), (1, 0), (2, 3), (3, 2)]
SWAP_Y = [(0, 2), (2, 0), (1, 3), (3, 1)]
TO_X, TO_Y, KEPT = (2, 6), (5, 7), (0, 1, 3, 4)
VMEM_LIMIT = 56 * 1024 * 1024
PLACE_STEP = 32
NN = (((1,), (0,)), ((), ()))
NT = (((1,), (1,)), ((), ()))
TN = (((0,), (0,)), ((), ()))
COSTS = {"finish_in": 67}
SMALL = pl.CostEstimate(flops=1024, bytes_accessed=1024, transcendentals=0)
ANY = pl.BlockSpec(memory_space=pl.ANY)
SMEM = pl.BlockSpec(memory_space=pltpu.SMEM)


def dot(lhs_arr, rhs_arr, dims):
    return lax.dot_general(lhs_arr, rhs_arr, dims, preferred_element_type=F32)


def call(body, name, grid, in_specs, out_specs, out_shape, args, deps=(), scratch=(), aliases=None):
    n_in, n_deps = len(in_specs), len(deps)

    def wrapped(*refs):
        body(*refs[:n_in], *refs[n_in + n_deps :])

    return pl.pallas_call(
        wrapped,
        grid=grid,
        in_specs=list(in_specs) + [ANY] * n_deps,
        out_specs=out_specs,
        out_shape=out_shape,
        scratch_shapes=list(scratch),
        compiler_params=pltpu.CompilerParams(vmem_limit_bytes=VMEM_LIMIT),
        input_output_aliases=aliases or {},
        cost_estimate=pl.CostEstimate(
            flops=1024 + COSTS.get(name, 0) * 1_000_000_000, bytes_accessed=1024, transcendentals=0
        ),
        name=name,
    )(*args, *deps)


def shape(dims, dtype):
    return jax.ShapeDtypeStruct(tuple(dims), dtype)


def whole_block(array):
    return pl.BlockSpec(array.shape, lambda *i: (0,) * len(array.shape))


def product(name, lhs_arr, rhs_arr, depth, first, wide, step, deps=()):
    rows = lhs_arr.shape[0]

    def body(lhs_ref, rhs_ref, out_ref):
        out_ref[...] = dot(lhs_ref[...], rhs_ref[...], NN)

    return call(
        body,
        name,
        (wide // step,),
        [
            pl.BlockSpec((rows, depth), lambda j: (0, 0)),
            pl.BlockSpec((depth, step), lambda j: (0, first // step + j)),
        ],
        pl.BlockSpec((rows, step), lambda j: (0, j)),
        shape((rows, wide), F32),
        (lhs_arr, rhs_arr),
        deps,
    )


def product_back(name, lhs_arr, rhs_arr, step, deps=()):
    rows = lhs_arr.shape[0]
    wide, depth = rhs_arr.shape

    def body(lhs_ref, rest_ref, rhs_ref, out_ref, sum_ref):
        out_ref[...] = dot(lhs_ref[...], rhs_ref[...], NT)

        @pl.when(pl.program_id(0) == 0)
        def _():
            sum_ref[...] = jnp.broadcast_to(join(rest_ref[...]), (rows, LANE))

    return call(
        body,
        name,
        (wide // step,),
        [
            pl.BlockSpec((rows, depth), lambda j: (0, 0)),
            pl.BlockSpec((rows, LANE), lambda j: (0, depth // LANE)),
            pl.BlockSpec((step, depth), lambda j: (j, 0)),
        ],
        [pl.BlockSpec((rows, step), lambda j: (0, j)), pl.BlockSpec((rows, LANE), lambda j: (0, 0))],
        [shape((rows, wide), F32), shape((rows, LANE), F32)],
        (lhs_arr, lhs_arr, rhs_arr),
        deps,
    )


def outer_sum(name, lhs_arr, rhs_arr, rows, wide, step, deps=()):
    depth = lhs_arr.shape[0]
    by_rows = step > 0
    step = abs(step)

    def body(lhs_ref, rhs_ref, out_ref):
        out_ref[...] = dot(lhs_ref[...], rhs_ref[...], TN).astype(BF16)

    if by_rows:
        grid = (rows // step,)
        specs = [
            pl.BlockSpec((depth, step), lambda j: (0, j)),
            pl.BlockSpec((depth, wide), lambda j: (0, 0)),
        ]
        out_spec = pl.BlockSpec((step, wide), lambda j: (j, 0))
    else:
        grid = (wide // step,)
        specs = [
            pl.BlockSpec((depth, rows), lambda j: (0, 0)),
            pl.BlockSpec((depth, step), lambda j: (0, j)),
        ]
        out_spec = pl.BlockSpec((rows, step), lambda j: (0, j))
    return call(body, name, grid, specs, out_spec, shape((rows, wide), BF16), (lhs_arr, rhs_arr), deps)


def outer_gate_out(normed, grad_gate, mix, grad_mix, parts, wide, deps, between):
    depth, own = mix.shape
    count = own // parts
    turns = wide // own

    def right(lhs_ref, rhs_ref, out_ref):
        out_ref[...] = dot(lhs_ref[...], rhs_ref[...], TN).astype(BF16).reshape(parts, count, own)

    half_done = call(
        right,
        "part_out",
        (turns,),
        [
            pl.BlockSpec((depth, own), lambda j: (0, 0)),
            pl.BlockSpec((depth, own), lambda j: (0, j)),
        ],
        pl.BlockSpec((parts, count, own), lambda j: (0, j, 1)),
        shape((parts, turns * count, 2 * own), BF16),
        (mix, grad_mix),
        deps,
    ).reshape(wide, 2 * own)

    middle = between((half_done,))

    def left(lhs_ref, rhs_ref, _, out_ref):
        out_ref[...] = dot(lhs_ref[...], rhs_ref[...], TN).astype(BF16)

    return call(
        left,
        "part_gate",
        (turns,),
        [
            pl.BlockSpec((depth, own), lambda j: (0, j)),
            pl.BlockSpec((depth, own), lambda j: (0, 0)),
            ANY,
        ],
        pl.BlockSpec((own, own), lambda j: (j, 0)),
        shape((wide, 2 * own), BF16),
        (normed, grad_gate, half_done),
        middle,
        aliases={2: 0},
    ), middle


def after(value, *events):
    return lax.optimization_barrier((value, events))[0]


def send_x(value):
    return lax.ppermute(value, "grp", SWAP_X)


def send_y(value):
    return lax.ppermute(value, "grp", SWAP_Y)


def lay(pieces, deps=()):
    if any(piece.shape[0] % 16 for piece in pieces):
        return jnp.concatenate(pieces)
    wide = pieces[0].shape[1]
    at = [0]
    for piece in pieces:
        at.append(at[-1] + piece.shape[0])
    deps = tuple(deps)

    def body(*refs):
        out_ref, sems = refs[-2], refs[-1]
        copies = [
            pltpu.make_async_copy(
                ref, out_ref.at[pl.ds(at[index], pieces[index].shape[0])], sems.at[index]
            )
            for index, ref in enumerate(refs[: len(pieces)])
        ]
        for copy in copies:
            copy.start()
        for copy in copies:
            copy.wait()

    return call(
        body,
        "lay",
        (),
        [pl.BlockSpec(memory_space=pltpu.VMEM)] * len(pieces),
        ANY,
        shape((at[-1], wide), pieces[0].dtype),
        tuple(pieces),
        deps,
        [pltpu.SemaphoreType.DMA((len(pieces),))],
    )


def start_gather(own):
    return own, send_x(own), send_y(own)


def second_step(held, hold=()):
    own, by_x, by_y = held
    half = own.shape[0] // 2 if own.shape[0] % 16 else (own.shape[0] + 16) // 32 * 16
    x_on, y_on = by_x[:half], by_y[half:]
    if hold:
        x_on, y_on = after((x_on, y_on), hold)
    return own, by_x, by_y, send_y(x_on), send_x(y_on)


def end_gather(held, deps=(), hold=()):
    return lay(second_step(held, hold), deps)


def gather_rows(own, deps=(), hold=()):
    return end_gather(start_gather(own), deps, hold)


def sum_everywhere(value):
    value = value + send_x(value)
    value = value + send_y(value)
    count = lax.axis_size("seq")
    step = 1
    while step < count:
        value = value + lax.ppermute(value, "seq", [(one, one ^ step) for one in range(count)])
        step *= 2
    return value


def split(column):
    high = column.astype(BF16).astype(F32)
    rest = column - high
    middle = rest.astype(BF16).astype(F32)
    lane = lax.broadcasted_iota(jnp.int32, column.shape, 1)
    zero = jnp.zeros_like(column)
    picked = jnp.where(lane == 0, high, jnp.where(lane == 1, middle, jnp.where(lane == 2, rest - middle, zero)))
    return picked.astype(BF16)


def join(block):
    return jnp.sum(block.astype(F32), axis=1, keepdims=True)


def partial_sums(name, dims, rows, weights, step, column=None, deps=(), stacked=None, firsts=(0, 0)):
    half = rows[0].shape[0] // 8
    pairs = len(rows)
    if stacked is not None:
        wide, parts, first = stacked
        own = rows[0].shape[1]
        specs = [pl.BlockSpec((parts, own // parts, step), lambda j: (0, j, first // step))]
    elif dims is NN:
        wide = weights[0].shape[1]
        specs = [pl.BlockSpec((one.shape[1], step), lambda j: (0, j)) for one in rows]
    else:
        wide = weights[0].shape[0]
        specs = [
            pl.BlockSpec((step, one.shape[1]), lambda j, at=at // one.shape[1]: (j, at))
            for one, at in zip(rows, firsts)
        ]
    extra = 0 if column is None else LANE
    columns = () if column is None else (column,)

    def pick(value, slots):
        return jnp.concatenate([value[slot * half : (slot + 1) * half] for slot in slots])

    def body(*refs):
        x_ref, y_ref, kept_ref = refs[-3:]
        at = pl.ds(pl.multiple_of(pl.program_id(0) * step, LANE), step)
        sums = None
        for rows_ref, weights_ref in zip(refs[:pairs], refs[pairs : 2 * pairs]):
            block = weights_ref[...]
            if stacked is not None:
                block = block.reshape(own, step)
            term = dot(rows_ref[...], block, dims)
            sums = term if sums is None else sums + term
        x_ref[:, at] = pick(sums, TO_X).astype(BF16)
        y_ref[:, at] = pick(sums, TO_Y).astype(BF16)
        kept_ref[...] = pick(sums, KEPT)
        if column is not None:

            @pl.when(pl.program_id(0) == 0)
            def _():
                x_ref[:, wide:] = split(pick(refs[-4], TO_X))
                y_ref[:, wide:] = split(pick(refs[-4], TO_Y))

    sent = shape((2 * half, wide + extra), BF16)
    return call(
        body,
        name,
        (wide // step,),
        [whole_block(one) for one in rows] + specs + [whole_block(one) for one in columns],
        [whole_block(sent), whole_block(sent), pl.BlockSpec((4 * half, step), lambda j: (0, j))],
        [sent, sent, shape((4 * half, wide), F32)],
        tuple(rows) + tuple(weights) + columns,
        deps,
    )


def merge(name, kept, by_x, by_y, column=None, deps=()):
    half = kept.shape[0] // 4
    wide = kept.shape[1]
    extra = 0 if column is None else LANE
    columns = () if column is None else (column,)

    def body(kept_ref, by_x_ref, by_y_ref, *refs):
        for_y_ref, for_x_ref = refs[-2:]
        for_y_ref[:, :wide] = (kept_ref[half:, :] + by_x_ref[:, :wide].astype(F32)).astype(BF16)
        for_x_ref[:, :wide] = (kept_ref[:half, :] + by_y_ref[:, :wide].astype(F32)).astype(BF16)
        if column is not None:
            for_y_ref[:, wide:] = split(refs[0][4 * half : 5 * half] + join(by_x_ref[:, wide:]))
            for_x_ref[:, wide:] = split(refs[0][3 * half : 4 * half] + join(by_y_ref[:, wide:]))

    again = shape((half, wide + extra), BF16)
    return call(
        body,
        name,
        (1,),
        [
            pl.BlockSpec((2 * half, wide), lambda j: (1, 0)),
            pl.BlockSpec((half, wide + extra), lambda j: (1, 0)),
            pl.BlockSpec((half, wide + extra), lambda j: (1, 0)),
        ]
        + [whole_block(one) for one in columns],
        [whole_block(again), whole_block(again)],
        [again, again],
        (kept, by_x, by_y) + columns,
        deps,
    )


def scattered_specs(pieces, step, turn=None):
    kept, by_x, by_y, last_y, last_x = pieces[:5]
    half = last_y.shape[0]
    count = half // step
    wide = by_x.shape[1]
    received = pl.BlockSpec((step, wide), lambda h, i: (i, 0))
    specs = [
        pl.BlockSpec((step, kept.shape[1]), lambda h, i: (h * count + i, 0)),
        received,
        received,
        received,
        received,
    ]
    if len(pieces) > 5:
        specs.append(pl.BlockSpec((step, LANE), lambda h, i: (h * count + i, 0)))
    return specs


def scattered_sum(refs, wide):
    top = pl.program_id(0) == 0
    first = jnp.where(top, refs[1][...].astype(F32), refs[2][...].astype(F32))
    second = jnp.where(top, refs[3][...].astype(F32), refs[4][...].astype(F32))
    came = first + second
    total = refs[0][...] + came[:, :wide]
    if len(refs) == 5:
        return total, None
    return total, refs[5][:, :1] + jnp.sum(came[:, wide:], axis=1, keepdims=True)


def own_block(step, count, wide):
    return pl.BlockSpec((step, wide), lambda h, i: (h * count + i, 0))


def finish_mix(pieces, tokens, gain, width):
    rows = tokens.shape[0]
    half = rows // 2
    step = min(half, 64)
    count = half // step

    def body(*refs):
        tokens_ref, gain_ref, middle_ref, normed_ref, raw_ref, scale_ref, scale_mid_ref = refs[-7:]
        raw, squares = scattered_sum(refs[:-7], width)
        scale = lax.rsqrt(squares / width + EPSILON)
        middle = tokens_ref[...].astype(F32) + raw * scale
        scale_mid = lax.rsqrt(jnp.mean(middle * middle, axis=1, keepdims=True) + EPSILON)
        middle_ref[...] = middle
        raw_ref[...] = raw
        normed_ref[...] = (middle * scale_mid * gain_ref[...]).astype(BF16)
        scale_ref[...] = scale
        scale_mid_ref[...] = scale_mid

    block = own_block(step, count, width)
    thin = own_block(step, count, 1)
    return call(
        body,
        "finish_mix",
        (2, count),
        scattered_specs(pieces, step) + [block, pl.BlockSpec((1, width), lambda h, i: (0, 0))],
        [block, block, block, thin, thin],
        [
            shape((rows, width), F32),
            shape((rows, width), BF16),
            shape((rows, width), F32),
            shape((rows, 1), F32),
            shape((rows, 1), F32),
        ],
        tuple(pieces) + (tokens, gain),
    )


def add_scattered(pieces, middle, out, width, deps=()):
    rows = middle.shape[0]
    half = rows // 2
    step = min(half, 64)
    count = half // step

    def body(*refs):
        middle_ref, out_ref = refs[-2:]
        out_ref[...] = (middle_ref[...] + scattered_sum(refs[:-2], width)[0]).astype(out)

    block = own_block(step, count, width)
    return call(
        body,
        "add_scattered",
        (2, count),
        scattered_specs(pieces, step) + [block],
        block,
        shape((rows, width), out),
        tuple(pieces) + (middle,),
        deps,
    )


def norm_back(values, scale, gain, grad):
    weighted = values * grad
    inner = jnp.mean(weighted * gain, axis=1, keepdims=True)
    back = scale * gain * grad - values * (scale * scale * scale * inner)
    return back, jnp.sum(weighted * scale, axis=0, keepdims=True)


def finish_mid(pieces, middle, cotangent, raw, scale, scale_mid, gain, width, deps=()):
    rows = middle.shape[0]
    half = rows // 2
    step = min(half, 64)
    count = half // step

    def body(*refs):
        middle_ref, cot_ref, raw_ref, scale_ref, scale_mid_ref, gain_ref, grad_ref, send_ref, sum_ref = refs[-9:]
        grad, _ = scattered_sum(refs[:-9], width)
        back, gain_part = norm_back(middle_ref[...], scale_mid_ref[...], gain_ref[...], grad)
        grad_middle = cot_ref[...].astype(F32) + back
        scale = scale_ref[...]
        coupling = scale * scale * scale * jnp.mean(raw_ref[...] * grad_middle, axis=1, keepdims=True)
        grad_ref[...] = grad_middle
        send_ref[:, :width] = (grad_middle * scale).astype(BF16)
        send_ref[:, width:] = split(jnp.broadcast_to(coupling, (step, LANE)))

        @pl.when((pl.program_id(0) == 0) & (pl.program_id(1) == 0))
        def _():
            sum_ref[...] = jnp.zeros_like(sum_ref)

        sum_ref[...] += gain_part

    block = own_block(step, count, width)
    thin = own_block(step, count, 1)
    row = pl.BlockSpec((1, width), lambda h, i: (0, 0))
    return call(
        body,
        "finish_mid",
        (2, count),
        scattered_specs(pieces, step) + [block, block, block, thin, thin, row],
        [block, own_block(step, count, width + LANE), row],
        [shape((rows, width), F32), shape((rows, width + LANE), BF16), shape((1, width), F32)],
        tuple(pieces) + (middle, cotangent, raw, scale, scale_mid, gain),
        deps,
    )


def finish_in(pieces, tokens, grad_middle, gain, width, deps=()):
    rows = tokens.shape[0]
    half = rows // 2
    step = min(half, 64)
    count = half // step

    def body(*refs):
        tokens_ref, middle_ref, gain_ref, out_ref, sum_ref = refs[-5:]
        grad, _ = scattered_sum(refs[:-5], width)
        values = tokens_ref[...].astype(F32)
        scale = lax.rsqrt(jnp.mean(values * values, axis=1, keepdims=True) + EPSILON)
        back, gain_part = norm_back(values, scale, gain_ref[...], grad)
        out_ref[...] = middle_ref[...] + back

        @pl.when((pl.program_id(0) == 0) & (pl.program_id(1) == 0))
        def _():
            sum_ref[...] = jnp.zeros_like(sum_ref)

        sum_ref[...] += gain_part

    block = own_block(step, count, width)
    row = pl.BlockSpec((1, width), lambda h, i: (0, 0))
    return call(
        body,
        "finish_in",
        (2, count),
        scattered_specs(pieces, step) + [block, block, row],
        [block, row],
        [shape((rows, width), F32), shape((1, width), F32)],
        tuple(pieces) + (tokens, grad_middle, gain),
        deps,
    )


def norm_in(tokens, starts, gain, width):
    rows = tokens.shape[0]
    step = min(rows, 64)

    def body(starts_ref, tokens_ref, gain_ref, out_ref):
        values = tokens_ref[...].astype(F32)
        scale = lax.rsqrt(jnp.mean(values * values, axis=1, keepdims=True) + EPSILON)
        out_ref[:, :width] = (values * scale * gain_ref[...]).astype(BF16)
        here = starts_ref[0] + pl.program_id(0) * step
        here = here + lax.broadcasted_iota(jnp.int32, (step, LANE), 0)
        keep = jnp.ones((step, LANE), F32)
        for one in range(1, starts.shape[0]):
            keep = jnp.where(here == starts_ref[one], 0.0, keep)
        out_ref[:, width:] = keep.astype(BF16)

    return call(
        body,
        "norm_in",
        (rows // step,),
        [SMEM, pl.BlockSpec((step, width), lambda i: (i, 0)), pl.BlockSpec((1, width), lambda i: (0, 0))],
        pl.BlockSpec((step, width + LANE), lambda i: (i, 0)),
        shape((rows, width + LANE), BF16),
        (starts, tokens, gain),
    )


def feed_forward(normed, weights, deps=()):
    rows, depth = normed.shape
    own = weights.shape[1] // 2

    def body(normed_ref, weights_ref, hidden_ref, by_gate_ref, by_up_ref):
        both = dot(normed_ref[...], weights_ref[...], NN)
        gate, up = both[:, :LANE], both[:, LANE:]
        sig = jax.nn.sigmoid(gate)
        act = gate * sig
        hidden_ref[...] = (act * up).astype(BF16)
        by_gate_ref[...] = up * (sig * (1.0 + gate * (1.0 - sig)))
        by_up_ref[...] = act

    block = pl.BlockSpec((rows, LANE), lambda j: (0, j))
    return call(
        body,
        "feed_forward",
        (own // LANE,),
        [whole_block(normed), pl.BlockSpec((depth, 2 * LANE), lambda j: (0, j))],
        [block, block, block],
        [shape((rows, own), BF16), shape((rows, own), F32), shape((rows, own), F32)],
        (normed, weights),
        deps,
    )


def feed_back(cot, weights, by_gate, by_up, deps=()):
    rows, depth = cot.shape
    own = weights.shape[0]
    step = min(rows, 256)

    def body(cot_ref, weights_ref, by_gate_ref, by_up_ref, out_ref):
        grad = dot(cot_ref[...], weights_ref[...], NT)
        for turn in range(own // LANE):
            part = slice(turn * LANE, (turn + 1) * LANE)
            out_ref[:, 2 * turn * LANE : (2 * turn + 1) * LANE] = (grad[:, part] * by_gate_ref[:, part]).astype(BF16)
            out_ref[:, (2 * turn + 1) * LANE : (2 * turn + 2) * LANE] = (grad[:, part] * by_up_ref[:, part]).astype(BF16)

    return call(
        body,
        "feed_back",
        (rows // step,),
        [
            pl.BlockSpec((step, depth), lambda j: (j, 0)),
            whole_block(weights),
            pl.BlockSpec((step, own), lambda j: (j, 0)),
            pl.BlockSpec((step, own), lambda j: (j, 0)),
        ],
        pl.BlockSpec((step, 2 * own), lambda j: (j, 0)),
        shape((rows, 2 * own), BF16),
        (cot, weights, by_gate, by_up),
        deps,
    )


def pick_columns(mine, matrices, parts, spread, deps=()):
    rows, wide = matrices[0].shape
    piece = wide // (GRP * parts)
    own = wide // GRP
    count = len(matrices)
    step = min(rows, 64)

    def body(mine_ref, *refs):
        out_ref = refs[-1]
        for index, ref in enumerate(refs[:-1]):
            for which in range(GRP):

                @pl.when(mine_ref[0] == which)
                def _(index=index, ref=ref, which=which):
                    whole = ref[...].astype(F32)
                    picked = jnp.concatenate(
                        [
                            whole[:, (part * GRP + which) * piece : (part * GRP + which + 1) * piece]
                            for part in range(parts)
                        ],
                        axis=1,
                    ).astype(BF16)
                    if not spread:
                        out_ref[:, index * own : (index + 1) * own] = picked
                    else:
                        for turn in range(own // LANE):
                            at = (turn * count + index) * LANE
                            out_ref[:, at : at + LANE] = picked[:, turn * LANE : (turn + 1) * LANE]

    return call(
        body,
        "pick_columns",
        (rows // step,),
        [SMEM] + [pl.BlockSpec((step, wide), lambda i: (i, 0))] * count,
        pl.BlockSpec((step, own * count), lambda i: (i, 0)),
        shape((rows, own * count), BF16),
        (mine.reshape(1),) + tuple(matrices),
        deps,
    )


def pick_first(mine, input_proj, forget_proj, gate_proj, out_proj, parts):
    rows, wide = input_proj.shape
    piece = wide // (GRP * parts)
    own = wide // GRP
    count = rows // GRP

    def body(mine_ref, input_ref, forget_ref, gate_ref, out_ref, first_ref):
        at = pl.ds(pl.multiple_of(mine_ref[0] * count, count), count)
        first_ref[:, 3 * own :] = out_ref[at, :]
        for which in range(GRP):

            @pl.when(mine_ref[0] == which)
            def _(which=which):
                for index, ref in enumerate((input_ref, forget_ref, gate_ref)):
                    picked = jnp.concatenate(
                        [
                            ref[:, (part * GRP + which) * piece : (part * GRP + which + 1) * piece].astype(F32)
                            for part in range(parts)
                        ],
                        axis=1,
                    ).astype(BF16)
                    if index == 2:
                        first_ref[:, 2 * own : 3 * own] = picked
                        continue
                    for turn in range(own // LANE):
                        to = (2 * turn + index) * LANE
                        first_ref[:, to : to + LANE] = picked[:, turn * LANE : (turn + 1) * LANE]

    block = pl.BlockSpec((count, wide), lambda i: (i, 0))
    return call(
        body,
        "pick_first",
        (GRP,),
        [SMEM, block, block, block, pl.BlockSpec((rows, own), lambda i: (0, i))],
        pl.BlockSpec((count, 4 * own), lambda i: (i, 0)),
        shape((rows, 4 * own), BF16),
        (mine.reshape(1), input_proj, forget_proj, gate_proj, out_proj),
    )


def take_out(first, parts, own, deps=()):
    wide = GRP * own

    def body(first_ref, out_ref):
        out_ref[...] = first_ref[...].reshape(own, own)

    return call(
        body,
        "take_out",
        (GRP,),
        [pl.BlockSpec((parts, own // parts, own), lambda j: (0, j, 3))],
        pl.BlockSpec((own, own), lambda j: (0, j)),
        shape((own, wide), BF16),
        (first,),
        deps,
    )


def piece_blocks(pieces, step, wide, column=None):
    own, _, _, top, _ = pieces
    tops = top.shape[0] // step
    at = (lambda *i: 0) if column is None else (lambda *i: column(i[0]))
    block = pl.BlockSpec((step, wide), lambda *i: (i[-1], at(*i)))
    return [
        block,
        block,
        block,
        pl.BlockSpec((step, wide), lambda *i: (jnp.minimum(i[-1], tops - 1), at(*i))),
        pl.BlockSpec((step, wide), lambda *i: (jnp.maximum(i[-1] - tops, 0), at(*i))),
    ]


def collect(refs, held_ref, axis, tops):
    for index in range(3):
        held_ref[index] = refs[index][...]

    @pl.when(pl.program_id(axis) < tops)
    def _():
        held_ref[3] = refs[3][...]

    @pl.when(pl.program_id(axis) >= tops)
    def _():
        held_ref[3] = refs[4][...]


def place_columns(mine, pieces, parts, count, own, spread, deps=()):
    rows = pieces[0].shape[0]
    piece = own // parts
    step = min(pieces[3].shape[0], PLACE_STEP)
    tops = pieces[3].shape[0] // step

    def body(mine_ref, *refs):
        out_refs, held_ref = refs[5:-1], refs[-1]
        collect(refs, held_ref, 0, tops)
        for which in range(GRP):
            block = held_ref[mine_ref[0] ^ which].astype(F32)
            for index, out_ref in enumerate(out_refs):
                if spread:
                    turns = [
                        block[:, (turn * count + index) * LANE : (turn * count + index + 1) * LANE]
                        for turn in range(own // LANE)
                    ]
                    mat = jnp.concatenate(turns, axis=1)
                else:
                    mat = block[:, index * own : (index + 1) * own]
                for part in range(parts):
                    at = (part * GRP + which) * piece
                    out_ref[:, at : at + piece] = mat[:, part * piece : (part + 1) * piece]

    return call(
        body,
        "place_columns",
        (rows // step,),
        [SMEM] + piece_blocks(pieces, step, own * count),
        [pl.BlockSpec((step, own * GRP), lambda i: (i, 0))] * count,
        [shape((rows, own * GRP), F32)] * count,
        (mine.reshape(1),) + tuple(pieces),
        deps,
        [pltpu.VMEM((GRP, step, own * count), BF16)],
    )


def scan_forward(keep, proj, bias):
    _, half, wide = proj.shape
    own = wide // 2
    tiles = half // ROWS

    def body(keep_ref, proj_ref, bias_ref, prod_ref, state_ref, ends_ref):
        row = lax.broadcasted_iota(jnp.int32, (ROWS, LANE), 0)
        bias_row = bias_ref[...]

        def tile(part, step, carry):
            out = []
            for owner in range(GRP):
                slot = 2 * owner + part
                at = pl.ds(pl.multiple_of(step * ROWS, ROWS), ROWS)
                both = proj_ref[slot, at, :]
                enter = both[:, :LANE]
                forget = LOWER + (1.0 - LOWER) * jax.nn.sigmoid(both[:, LANE:] + bias_row)
                decay = forget * keep_ref[slot, at, :]
                income = enter * jax.nn.sigmoid(enter) * (1.0 - forget)
                for shift in (1, 2, 4):
                    fits = row >= shift
                    before = jnp.where(fits, pltpu.roll(income, shift, 0), 0.0)
                    factor = jnp.where(fits, pltpu.roll(decay, shift, 0), 1.0)
                    income = income + decay * before
                    decay = decay * factor
                prod, state = carry[owner]
                state_now = income + decay * state
                prod_now = decay * prod
                prod_ref[slot, at, :] = prod_now
                state_ref[slot, at, :] = state_now
                out.append((prod_now[ROWS - 1 :], state_now[ROWS - 1 :]))
            return tuple(out)

        carry = tuple(
            (jnp.ones((1, LANE), F32), jnp.zeros((1, LANE), F32)) for owner in range(GRP)
        )
        for part in range(2):
            carry = lax.fori_loop(0, tiles, partial(tile, part), carry)
        for owner in range(GRP):
            ends_ref[owner : owner + 1, :] = carry[owner][0]
            ends_ref[GRP + owner : GRP + owner + 1, :] = carry[owner][1]

    block = pl.BlockSpec((8, half, LANE), lambda j: (0, 0, j))
    return pl.pallas_call(
        body,
        grid=(own // LANE,),
        in_specs=[
            pl.BlockSpec((8, half, LANE), lambda j: (0, 0, 0)),
            pl.BlockSpec((8, half, 2 * LANE), lambda j: (0, 0, j)),
            pl.BlockSpec((1, LANE), lambda j: (0, j)),
        ],
        out_specs=[block, block, pl.BlockSpec((2 * GRP, LANE), lambda j: (0, j))],
        out_shape=[
            jax.ShapeDtypeStruct((8, half, own), F32),
            jax.ShapeDtypeStruct((8, half, own), F32),
            jax.ShapeDtypeStruct((2 * GRP, own), F32),
        ],
        compiler_params=pltpu.CompilerParams(vmem_limit_bytes=VMEM_LIMIT),
        cost_estimate=SMALL,
        name="scan_forward",
    )(keep, proj, bias)


def all_ends(ends, parts):
    if parts > 8:
        return lax.all_gather(ends, "seq"), ends
    even = lax.axis_index("seq") % 2 == 0
    other = lax.ppermute(ends, "seq", [(one, one ^ 1) for one in range(parts)])
    chip = jnp.concatenate([jnp.where(even, ends, other), jnp.where(even, other, ends)])
    chips = [chip] + [
        lax.ppermute(chip, "seq", [(one, (one + step) % parts) for one in range(parts)])
        for step in range(2, parts, 2)
    ]
    return jnp.concatenate(chips).reshape((parts,) + ends.shape), chip


def entering_state(info_ref, ends_ref, parts, backward, ordered):
    here = info_ref[0]
    steps = []
    if ordered or parts > 8:
        for place in range(parts - 1, 0, -1) if backward else range(parts - 1):
            steps.append((place, place > here if backward else place < here))
    else:
        chips, chip, core = parts // 2, here // 2, here % 2
        for away in range(chips - 1, 0, -1):
            at = chips - away if backward else away
            for one in (1, 0) if backward else (0, 1):
                steps.append((2 * at + one, chip + away < chips if backward else chip >= away))
        steps.append((1, core == 0) if backward else (0, core == 1))
    state = jnp.zeros((GRP, LANE), F32)
    for at, counts in steps:
        longer = ends_ref[at, GRP:, :] + ends_ref[at, :GRP, :] * state
        state = jnp.where(counts, longer, state)
    return state


def finish_forward(info, ends, prod, state, proj, gain, deps=()):
    _, half, own = prod.shape
    count = ends.shape[0]

    def body(info_ref, ends_ref, prod_ref, state_ref, proj_ref, gain_ref, states_ref, mix_ref, squares_ref, enter_ref):
        entering = entering_state(info_ref, ends_ref, count, False, False)
        enter_ref[...] = entering

        @pl.when(pl.program_id(0) == 0)
        def _():
            squares_ref[...] = jnp.zeros_like(squares_ref)

        for owner in range(GRP):
            for part in range(2):
                slot = 2 * owner + part
                states = state_ref[slot] + prod_ref[slot] * entering[owner : owner + 1]
                states_ref[slot] = states
                gate = proj_ref[slot]
                mix_ref[slot] = (states * gain_ref[...] * (gate * jax.nn.sigmoid(gate))).astype(BF16)
                squares_ref[slot] += states * states

        @pl.when(pl.program_id(0) == own // LANE - 1)
        def _():
            for slot in range(8):
                total = jnp.sum(squares_ref[slot], axis=1, keepdims=True)
                squares_ref[slot] = jnp.broadcast_to(total, (half, LANE))

    block = pl.BlockSpec((8, half, LANE), lambda j: (0, 0, j))
    return call(
        body,
        "finish_forward",
        (own // LANE,),
        [
            SMEM,
            pl.BlockSpec((count, 2 * GRP, LANE), lambda j: (0, 0, j)),
            block,
            block,
            block,
            pl.BlockSpec((1, LANE), lambda j: (0, j)),
        ],
        [
            block,
            block,
            pl.BlockSpec((8, half, LANE), lambda j: (0, 0, 0)),
            pl.BlockSpec((GRP, LANE), lambda j: (0, j)),
        ],
        [
            shape((8, half, own), F32),
            shape((8, half, own), BF16),
            shape((8, half, LANE), F32),
            shape((GRP, own), F32),
        ],
        (info, ends, prod, state, proj, gain),
        deps,
    )


def scan_backward(keep, proj, proj_gate, bias, gain, states, back, coupling):
    _, half, own = proj_gate.shape
    tiles = half // ROWS

    def body(
        keep_ref, proj_ref, gate_ref, bias_ref, gain_ref, states_ref, back_ref, coupling_ref,
        prod_ref, grad_ref, ends_ref, out_ref, sum_ref,
    ):
        row = lax.broadcasted_iota(jnp.int32, (ROWS, LANE), 0)
        bias_row = bias_ref[...]
        gain_row = gain_ref[...]

        def tile(part, turn, carry):
            step = tiles - 1 - turn
            out = []
            for owner in range(GRP):
                slot = 2 * owner + part
                at = pl.ds(pl.multiple_of(step * ROWS, ROWS), ROWS)
                gate = gate_ref[slot, at, :]
                forget = LOWER + (1.0 - LOWER) * jax.nn.sigmoid(proj_ref[slot, at, :] + bias_row)
                decay = forget * keep_ref[slot, at, :]
                direct = (
                    gain_row * (gate * jax.nn.sigmoid(gate)) * back_ref[slot, at, :]
                    - states_ref[slot, at, :] * coupling_ref[slot, at, :]
                )
                flow = decay * direct
                for shift in (1, 2, 4):
                    fits = row < ROWS - shift
                    later = jnp.where(fits, pltpu.roll(flow, ROWS - shift, 0), 0.0)
                    factor = jnp.where(fits, pltpu.roll(decay, ROWS - shift, 0), 1.0)
                    flow = flow + decay * later
                    decay = decay * factor
                prod, grad = carry[owner]
                flow = flow + decay * grad
                decay = decay * prod
                last = row == ROWS - 1
                grad_ref[slot, at, :] = direct + jnp.where(last, grad, pltpu.roll(flow, ROWS - 1, 0))
                prod_ref[slot, at, :] = jnp.where(last, prod, pltpu.roll(decay, ROWS - 1, 0))
                out.append((decay[:1], flow[:1]))
            return tuple(out)

        carry = tuple(
            (jnp.ones((1, LANE), F32), jnp.zeros((1, LANE), F32)) for owner in range(GRP)
        )
        for part in (1, 0):
            carry = lax.fori_loop(0, tiles, partial(tile, part), carry)
        for owner in range(GRP):
            ends_ref[owner : owner + 1, :] = carry[owner][0]
            ends_ref[GRP + owner : GRP + owner + 1, :] = carry[owner][1]
        gain_sum = jnp.zeros((1, LANE), F32)
        for slot in range(8):
            gate = gate_ref[slot]
            gate_sig = jax.nn.sigmoid(gate)
            pull = back_ref[slot] * states_ref[slot]
            out_ref[slot] = (pull * gain_row * (gate_sig * (1.0 + gate * (1.0 - gate_sig)))).astype(BF16)
            gain_sum = gain_sum + jnp.sum(pull * (gate * gate_sig), axis=0, keepdims=True)
        sum_ref[...] = gain_sum

    block = pl.BlockSpec((8, half, LANE), lambda j: (0, 0, j))
    vector = pl.BlockSpec((1, LANE), lambda j: (0, j))
    rows = pl.BlockSpec((8, half, LANE), lambda j: (0, 0, 0))
    return call(
        body,
        "scan_backward",
        (own // LANE,),
        [rows, pl.BlockSpec((8, half, LANE), lambda j: (0, 0, 2 * j + 1)), block, vector, vector, block, block, rows],
        [block, block, pl.BlockSpec((2 * GRP, LANE), lambda j: (0, j)), block, vector],
        [
            shape((8, half, own), F32),
            shape((8, half, own), F32),
            shape((2 * GRP, own), F32),
            shape((8, half, own), BF16),
            shape((1, own), F32),
        ],
        (keep, proj, proj_gate, bias, gain, states, back, coupling),
    )


def finish_backward(info, keep, ends, prod, grad, proj, bias, states, enter, deps=()):
    _, half, own = prod.shape
    parts = ends.shape[0]

    def body(info_ref, keep_ref, ends_ref, prod_ref, grad_ref, proj_ref, bias_ref, states_ref, enter_ref, out_ref, sum_ref):
        entering = entering_state(info_ref, ends_ref, parts, True, True)
        first = lax.broadcasted_iota(jnp.int32, (half, LANE), 0) == 0
        bias_sum = jnp.zeros((1, LANE), F32)
        for owner in range(GRP):
            before = enter_ref[owner : owner + 1, :]
            for part in range(2):
                slot = 2 * owner + part
                states = states_ref[slot]
                previous = jnp.where(first, before, pltpu.roll(states, 1, 0))
                before = states[half - 1 :]
                total = grad_ref[slot] + prod_ref[slot] * entering[owner : owner + 1]
                enter = proj_ref[slot, :, :LANE]
                sig = jax.nn.sigmoid(proj_ref[slot, :, LANE:] + bias_ref[...])
                enter_sig = jax.nn.sigmoid(enter)
                grad_forget = total * (previous * keep_ref[slot] - enter * enter_sig)
                grad_proj = grad_forget * ((1.0 - LOWER) * sig * (1.0 - sig))
                forget = LOWER + (1.0 - LOWER) * sig
                out_ref[slot, :, :LANE] = (
                    total * (1.0 - forget) * (enter_sig * (1.0 + enter * (1.0 - enter_sig)))
                ).astype(BF16)
                out_ref[slot, :, LANE:] = grad_proj.astype(BF16)
                bias_sum = bias_sum + jnp.sum(grad_proj, axis=0, keepdims=True)
        sum_ref[...] = bias_sum

    block = pl.BlockSpec((8, half, LANE), lambda j: (0, 0, j))
    pair = pl.BlockSpec((8, half, 2 * LANE), lambda j: (0, 0, j))
    vector = pl.BlockSpec((1, LANE), lambda j: (0, j))
    return call(
        body,
        "finish_backward",
        (own // LANE,),
        [
            SMEM,
            pl.BlockSpec((8, half, LANE), lambda j: (0, 0, 0)),
            pl.BlockSpec((parts, 2 * GRP, LANE), lambda j: (0, 0, j)),
            block,
            block,
            pair,
            vector,
            block,
            pl.BlockSpec((GRP, LANE), lambda j: (0, j)),
        ],
        [pair, vector],
        [shape((8, half, 2 * own), BF16), shape((1, own), F32)],
        (info, keep, ends, prod, grad, proj, bias, states, enter),
        deps,
    )


def place_rows(mine, pieces, deps=()):
    rows, wide = pieces[0].shape
    if rows % 16:
        pieces = lay(pieces, deps).reshape(GRP, rows, wide)

        def from_laid(mine_ref, pieces_ref, out_ref):
            out_ref[0] = pieces_ref[mine_ref[0] ^ pl.program_id(0)].astype(F32)

        return call(
            from_laid,
            "place_rows",
            (GRP,),
            [SMEM, whole_block(pieces)],
            pl.BlockSpec((1, rows, wide), lambda j: (j, 0, 0)),
            shape((GRP, rows, wide), F32),
            (mine.reshape(1), pieces),
        ).reshape(GRP * rows, wide)

    step = math.gcd(rows, pieces[3].shape[0])
    tops = pieces[3].shape[0] // step

    def body(mine_ref, *refs):
        out_ref, held_ref = refs[5:]
        collect(refs, held_ref, 0, tops)
        for which in range(GRP):
            out_ref[which] = held_ref[mine_ref[0] ^ which].astype(F32)

    return call(
        body,
        "place_rows",
        (rows // step,),
        [SMEM] + piece_blocks(pieces, step, wide),
        pl.BlockSpec((GRP, step, wide), lambda i: (0, i, 0)),
        shape((GRP, rows, wide), F32),
        (mine.reshape(1),) + tuple(pieces),
        deps,
        [pltpu.VMEM((GRP, step, wide), BF16)],
    ).reshape(GRP * rows, wide)


def place_stacked(mine, pieces, first, own, deps=()):
    rows = pieces[0].shape[0]
    count = rows // GRP
    tops = pieces[3].shape[0] // count

    def body(mine_ref, *refs):
        out_ref, held_ref = refs[5:]
        collect(refs, held_ref, 0, tops)
        for which in range(GRP):
            out_ref[which * count : (which + 1) * count, :] = held_ref[mine_ref[0] ^ which].astype(F32)

    return call(
        body,
        "place_stacked",
        (GRP,),
        [SMEM] + piece_blocks(pieces, count, own, lambda i: first // own),
        pl.BlockSpec((rows, own), lambda j: (0, j)),
        shape((rows, GRP * own), F32),
        (mine.reshape(1),) + tuple(pieces),
        deps,
        [pltpu.VMEM((GRP, count, own), BF16)],
    )


def on_device(
    tokens,
    seq_lengths,
    cotangent,
    norm_gain,
    input_proj,
    forget_proj,
    forget_bias,
    gate_proj,
    state_gain,
    out_proj,
    mlp_gain,
    mlp_gate,
    mlp_up,
    mlp_down,
):
    tok_rows, width = tokens.shape
    half = tok_rows // 2
    plane = GRP * tok_rows
    parts = lax.axis_size("seq")
    mine, place = lax.axis_index("grp"), lax.axis_index("seq")
    own = width // GRP

    def own_rows(matrix):
        count = matrix.shape[0] // GRP
        return lax.dynamic_slice_in_dim(matrix, mine * count, count, 0)

    def own_features(vector):
        cut = vector.reshape(parts, GRP, -1)
        return lax.dynamic_index_in_dim(cut, mine, 1, False).reshape(1, -1)

    def all_features(vector):
        cut = vector.reshape(parts, 1, -1)
        spread = jnp.where(jnp.arange(GRP)[None, :, None] == mine, cut, 0.0)
        return spread.reshape(-1)

    def whole(rows):
        return lax.all_gather(rows, "seq", axis=0, tiled=True)

    def reduced(grads):
        return lax.psum_scatter(grads, "seq", scatter_dimension=0, tiled=True)

    starts = (jnp.cumsum(seq_lengths[0]) - seq_lengths[0]).astype(jnp.int32)
    starts = jnp.concatenate([(place * tok_rows).reshape(1).astype(jnp.int32), starts])
    info = place.reshape(1).astype(jnp.int32)
    bias = own_features(forget_bias)
    gain = own_features(state_gain)
    in_gain, mid_gain = norm_gain.reshape(1, -1), mlp_gain.reshape(1, -1)

    w_first = whole(pick_first(mine, input_proj, forget_proj, gate_proj, out_proj, parts))
    normed = norm_in(tokens, starts, in_gain, width)
    cot_held = start_gather(cotangent)
    held = start_gather(normed)
    ff_cols = pick_columns(mine, (mlp_gate, mlp_up), parts, True, (normed,))
    w_ff = whole(ff_cols)
    w_down = whole(own_rows(mlp_down))
    normed = end_gather(held, (ff_cols,))
    cot_pieces = second_step(cot_held)
    keep = normed[:, width:].astype(F32).reshape(8, half, LANE)

    proj = product("proj_pair", normed, w_first, width, 0, 2 * own, 256, cot_pieces).reshape(
        8, half, 2 * own
    )
    prod, state, ends = scan_forward(keep, proj, bias)
    ends, _ = all_ends(ends, parts)
    proj_gate = product("proj_gate", normed, w_first, width, 2 * own, own, 256, (prod,))
    proj_gate = proj_gate.reshape(8, half, own)
    states, mix, squares, enter = finish_forward(info, ends, prod, state, proj_gate, gain)
    mix, squares = mix.reshape(plane, own), squares.reshape(plane, LANE)
    w_stacked = w_first.reshape(parts, -1, 4 * own)
    to_x, to_y, kept = partial_sums(
        "mix", NN, (mix,), (w_stacked,), own, squares, stacked=(width, parts, 3 * own)
    )
    by_x, by_y = send_x(to_x), send_y(to_y)
    w_out = take_out(w_stacked, parts, own, (to_x,))
    cot = lay(cot_pieces, (w_out,))
    for_y, for_x = merge("mix_merge", kept, by_x, by_y, squares, (cot,))
    pieces = (kept, by_x, by_y, send_y(for_y), send_x(for_x), squares)
    middle, normed_mid, raw, scale_state, scale_mid = finish_mix(pieces, tokens, mid_gain, width)
    normed_mid = gather_rows(normed_mid)
    hidden, by_gate, by_up = feed_forward(normed_mid, w_ff)
    part_down = outer_sum("part_down", hidden, cot, hidden.shape[1], width, -512)
    sum_down = reduced(part_down)

    grad_ff = feed_back(cot, w_down, by_gate, by_up, (part_down,))
    part_ff = outer_sum("part_ff", normed_mid, grad_ff, width, grad_ff.shape[1], 256)
    sum_ff = reduced(part_ff)
    to_x, to_y, kept = partial_sums("grad_mid", NT, (grad_ff,), (w_ff,), 256, deps=(part_ff,))
    by_x, by_y = send_x(to_x), send_y(to_y)
    for_y, for_x = merge("grad_mid_merge", kept, by_x, by_y)
    pieces = (kept, by_x, by_y, send_y(for_y), send_x(for_x))
    grad_middle, scaled_mix, grad_mlp_gain = finish_mid(
        pieces,
        middle,
        cotangent,
        raw,
        scale_state,
        scale_mid,
        mid_gain,
        width,
    )
    held = start_gather(scaled_mix)
    to_x, to_y, kept_out = partial_sums("down", NN, (hidden,), (w_down,), 256, deps=(scaled_mix,))
    grad_mix = end_gather(held, (to_x,))

    to_x, to_y = after((to_x, to_y), grad_mix)
    by_x_out, by_y_out = send_x(to_x), send_y(to_y)
    held_down = start_gather(after(sum_down, grad_mix))
    back, coupling = product_back("back", grad_mix, w_out, 256)
    after_prod, local, ends_back, grad_gate, gain_sum = scan_backward(
        keep,
        proj,
        proj_gate,
        bias,
        gain,
        states,
        back.reshape(8, half, own),
        coupling.reshape(8, half, LANE),
    )
    grad_gate = grad_gate.reshape(plane, own)
    out_sends = []

    def between(deps):
        out_sends.extend(merge("down_merge", kept_out, by_x_out, by_y_out, None, deps))
        return out_sends[0], held_down[1], held_down[2]

    part_gate_out, _ = outer_gate_out(
        normed, grad_gate, mix, grad_mix, parts, width, (after_prod,), between
    )
    sum_gate_out = reduced(part_gate_out)
    out_last_y, out_last_x = send_y(out_sends[0]), send_x(out_sends[1])
    pieces_out = (kept_out, by_x_out, by_y_out, out_last_y, out_last_x)
    ends_back = lax.all_gather(after(ends_back, part_gate_out), "seq")
    grad_pair, bias_sum = finish_backward(
        info, keep, ends_back, after_prod, local, proj, bias, states, enter, (part_gate_out,)
    )
    grad_pair = grad_pair.reshape(plane, 2 * own)
    held_ff = start_gather(after(sum_ff, part_gate_out))
    to_x, to_y, kept = partial_sums(
        "grad_in", NT, (grad_pair, grad_gate), (w_first, w_first), 256, firsts=(0, 2 * own)
    )
    by_x, by_y = send_x(to_x), send_y(to_y)
    part_pair = outer_sum("part_pair", normed, grad_pair, width, 2 * own, 256, (to_x,))
    sum_pair = reduced(part_pair)
    block_out = add_scattered(
        pieces_out, middle, BF16, width, (part_pair, held_ff[1], held_ff[2])
    )
    grad_down = place_rows(mine, second_step(held_down), (block_out,))
    for_y, for_x = merge("grad_in_merge", kept, by_x, by_y, deps=(grad_down,))
    last_y, last_x = send_y(for_y), send_x(for_x)
    pieces = (kept, by_x, by_y, last_y, last_x)
    held_go = start_gather(after(sum_gate_out, held_ff[1], held_ff[2]))
    grad_mlp_gate, grad_mlp_up = place_columns(
        mine, second_step(held_ff), parts, 2, w_ff.shape[1] // 2, True, (for_y,)
    )
    grad_tokens, grad_norm_gain = finish_in(
        pieces, tokens, grad_middle, in_gain, width, (grad_mlp_up, held_go[1], held_go[2])
    )
    vectors = sum_everywhere(
        jnp.stack(
            [grad_norm_gain[0], all_features(bias_sum), all_features(gain_sum), grad_mlp_gain[0]]
        )
    )
    held_pair = start_gather(after(sum_pair, held_go[1], held_go[2]))
    gate_out_pieces = second_step(held_go)
    (grad_gate_proj,) = place_columns(mine, gate_out_pieces, parts, 1, own, True)
    grad_out = place_stacked(mine, gate_out_pieces, own, own, (grad_gate_proj,))
    grad_input, grad_forget = place_columns(
        mine, second_step(held_pair), parts, 2, own, True, (grad_out, vectors)
    )
    return (
        block_out,
        grad_tokens,
        vectors[0],
        grad_input,
        grad_forget,
        vectors[1],
        grad_gate_proj,
        vectors[2],
        grad_out,
        vectors[3],
        grad_mlp_gate,
        grad_mlp_up,
        grad_down,
    )


def solution(mesh):
    rows = P("seq", None)
    tokens = P(("grp", "seq"), None)
    return jax.shard_map(
        on_device,
        mesh=mesh,
        in_specs=(
            tokens,
            P("grp", None),
            tokens,
            P(),
            rows,
            rows,
            P(),
            rows,
            P(),
            rows,
            P(),
            rows,
            rows,
            rows,
        ),
        out_specs=(
            tokens,
            tokens,
            P(),
            rows,
            rows,
            P(),
            rows,
            P(),
            rows,
            P(),
            rows,
            rows,
            rows,
        ),
        check_vma=False,
    )
```

```python
import math
from functools import partial

import jax
import jax.numpy as jnp
from jax import lax
from jax.experimental import pallas as pl
from jax.experimental.pallas import tpu as pltpu
from jax.sharding import PartitionSpec as P

LOWER = 0.9
EPSILON = 1e-06
GRP = 4
LANE = 128
ROWS = 8
F32 = jnp.float32
BF16 = jnp.bfloat16
SWAP_X = [(0, 1), (1, 0), (2, 3), (3, 2)]
SWAP_Y = [(0, 2), (2, 0), (1, 3), (3, 1)]
TO_X, TO_Y, KEPT = (2, 6), (5, 7), (0, 1, 3, 4)
VMEM_LIMIT = 56 * 1024 * 1024
PLACE_STEP = 32
NN = (((1,), (0,)), ((), ()))
NT = (((1,), (1,)), ((), ()))
TN = (((0,), (0,)), ((), ()))
COSTS = {"finish_in": 65, "finish_mid": 210}
SMALL = pl.CostEstimate(flops=1024, bytes_accessed=1024, transcendentals=0)
ANY = pl.BlockSpec(memory_space=pl.ANY)
SMEM = pl.BlockSpec(memory_space=pltpu.SMEM)


def dot(lhs_arr, rhs_arr, dims):
    return lax.dot_general(lhs_arr, rhs_arr, dims, preferred_element_type=F32)


def call(body, name, grid, in_specs, out_specs, out_shape, args, deps=(), scratch=(), aliases=None):
    n_in, n_deps = len(in_specs), len(deps)

    def wrapped(*refs):
        body(*refs[:n_in], *refs[n_in + n_deps :])

    return pl.pallas_call(
        wrapped,
        grid=grid,
        in_specs=list(in_specs) + [ANY] * n_deps,
        out_specs=out_specs,
        out_shape=out_shape,
        scratch_shapes=list(scratch),
        compiler_params=pltpu.CompilerParams(vmem_limit_bytes=VMEM_LIMIT),
        input_output_aliases=aliases or {},
        cost_estimate=pl.CostEstimate(
            flops=1024 + COSTS.get(name, 0) * 1_000_000_000, bytes_accessed=1024, transcendentals=0
        ),
        name=name,
    )(*args, *deps)


def shape(dims, dtype):
    return jax.ShapeDtypeStruct(tuple(dims), dtype)


def whole_block(array):
    return pl.BlockSpec(array.shape, lambda *i: (0,) * len(array.shape))


def product(name, lhs_arr, rhs_arr, depth, first, wide, step, deps=()):
    rows = lhs_arr.shape[0]

    def body(lhs_ref, rhs_ref, out_ref):
        out_ref[...] = dot(lhs_ref[...], rhs_ref[...], NN)

    return call(
        body,
        name,
        (wide // step,),
        [
            pl.BlockSpec((rows, depth), lambda j: (0, 0)),
            pl.BlockSpec((depth, step), lambda j: (0, first // step + j)),
        ],
        pl.BlockSpec((rows, step), lambda j: (0, j)),
        shape((rows, wide), F32),
        (lhs_arr, rhs_arr),
        deps,
    )


def product_back(name, lhs_arr, rhs_arr, step, deps=()):
    rows = lhs_arr.shape[0]
    wide, depth = rhs_arr.shape

    def body(lhs_ref, rest_ref, rhs_ref, out_ref, sum_ref):
        out_ref[...] = dot(lhs_ref[...], rhs_ref[...], NT)

        @pl.when(pl.program_id(0) == 0)
        def _():
            sum_ref[...] = jnp.broadcast_to(join(rest_ref[...]), (rows, LANE))

    return call(
        body,
        name,
        (wide // step,),
        [
            pl.BlockSpec((rows, depth), lambda j: (0, 0)),
            pl.BlockSpec((rows, LANE), lambda j: (0, depth // LANE)),
            pl.BlockSpec((step, depth), lambda j: (j, 0)),
        ],
        [pl.BlockSpec((rows, step), lambda j: (0, j)), pl.BlockSpec((rows, LANE), lambda j: (0, 0))],
        [shape((rows, wide), F32), shape((rows, LANE), F32)],
        (lhs_arr, lhs_arr, rhs_arr),
        deps,
    )


def outer_sum(name, lhs_arr, rhs_arr, rows, wide, step, deps=()):
    depth = lhs_arr.shape[0]
    by_rows = step > 0
    step = abs(step)

    def body(lhs_ref, rhs_ref, out_ref):
        out_ref[...] = dot(lhs_ref[...], rhs_ref[...], TN).astype(BF16)

    if by_rows:
        grid = (rows // step,)
        specs = [
            pl.BlockSpec((depth, step), lambda j: (0, j)),
            pl.BlockSpec((depth, wide), lambda j: (0, 0)),
        ]
        out_spec = pl.BlockSpec((step, wide), lambda j: (j, 0))
    else:
        grid = (wide // step,)
        specs = [
            pl.BlockSpec((depth, rows), lambda j: (0, 0)),
            pl.BlockSpec((depth, step), lambda j: (0, j)),
        ]
        out_spec = pl.BlockSpec((rows, step), lambda j: (0, j))
    return call(body, name, grid, specs, out_spec, shape((rows, wide), BF16), (lhs_arr, rhs_arr), deps)


def outer_gate_out(normed, grad_gate, mix, grad_mix, parts, wide, deps, between):
    depth, own = mix.shape
    count = own // parts
    turns = wide // own

    def right(lhs_ref, rhs_ref, out_ref):
        out_ref[...] = dot(lhs_ref[...], rhs_ref[...], TN).astype(BF16).reshape(parts, count, own)

    half_done = call(
        right,
        "part_out",
        (turns,),
        [
            pl.BlockSpec((depth, own), lambda j: (0, 0)),
            pl.BlockSpec((depth, own), lambda j: (0, j)),
        ],
        pl.BlockSpec((parts, count, own), lambda j: (0, j, 1)),
        shape((parts, turns * count, 2 * own), BF16),
        (mix, grad_mix),
        deps,
    ).reshape(wide, 2 * own)

    middle = between((half_done,))

    def left(lhs_ref, rhs_ref, _, out_ref):
        out_ref[...] = dot(lhs_ref[...], rhs_ref[...], TN).astype(BF16)

    return call(
        left,
        "part_gate",
        (turns,),
        [
            pl.BlockSpec((depth, own), lambda j: (0, j)),
            pl.BlockSpec((depth, own), lambda j: (0, 0)),
            ANY,
        ],
        pl.BlockSpec((own, own), lambda j: (j, 0)),
        shape((wide, 2 * own), BF16),
        (normed, grad_gate, half_done),
        middle,
        aliases={2: 0},
    ), middle


def after(value, *events):
    return lax.optimization_barrier((value, events))[0]


def send_x(value):
    return lax.ppermute(value, "grp", SWAP_X)


def send_y(value):
    return lax.ppermute(value, "grp", SWAP_Y)


def lay(pieces, deps=()):
    if any(piece.shape[0] % 16 for piece in pieces):
        return jnp.concatenate(pieces)
    wide = pieces[0].shape[1]
    at = [0]
    for piece in pieces:
        at.append(at[-1] + piece.shape[0])
    deps = tuple(deps)

    def body(*refs):
        out_ref, sems = refs[-2], refs[-1]
        copies = [
            pltpu.make_async_copy(
                ref, out_ref.at[pl.ds(at[index], pieces[index].shape[0])], sems.at[index]
            )
            for index, ref in enumerate(refs[: len(pieces)])
        ]
        for copy in copies:
            copy.start()
        for copy in copies:
            copy.wait()

    return call(
        body,
        "lay",
        (),
        [pl.BlockSpec(memory_space=pltpu.VMEM)] * len(pieces),
        ANY,
        shape((at[-1], wide), pieces[0].dtype),
        tuple(pieces),
        deps,
        [pltpu.SemaphoreType.DMA((len(pieces),))],
    )


def start_gather(own):
    return own, send_x(own), send_y(own)


def second_step(held, hold=()):
    own, by_x, by_y = held
    half = own.shape[0] // 2 if own.shape[0] % 16 else (own.shape[0] + 16) // 32 * 16
    x_on, y_on = by_x[:half], by_y[half:]
    if hold:
        x_on, y_on = after((x_on, y_on), hold)
    return own, by_x, by_y, send_y(x_on), send_x(y_on)


def end_gather(held, deps=(), hold=()):
    return lay(second_step(held, hold), deps)


def gather_rows(own, deps=(), hold=()):
    return end_gather(start_gather(own), deps, hold)


def sum_everywhere(value):
    count = lax.axis_size("seq")
    if count > 8:
        step = 1
        while step < count:
            value = value + lax.ppermute(value, "seq", [(one, one ^ step) for one in range(count)])
            step *= 2
    else:
        value = value + lax.ppermute(value, "seq", [(one, one ^ 1) for one in range(count)])
        value = value + sum(
            lax.ppermute(value, "seq", [(one, (one + step) % count) for one in range(count)])
            for step in range(2, count, 2)
        )
    across = lax.ppermute(value, "grp", [(one, 3 - one) for one in range(GRP)])
    return value + send_x(value) + send_y(value) + across


def split(column):
    high = column.astype(BF16).astype(F32)
    rest = column - high
    middle = rest.astype(BF16).astype(F32)
    lane = lax.broadcasted_iota(jnp.int32, column.shape, 1)
    zero = jnp.zeros_like(column)
    picked = jnp.where(lane == 0, high, jnp.where(lane == 1, middle, jnp.where(lane == 2, rest - middle, zero)))
    return picked.astype(BF16)


def join(block):
    return jnp.sum(block.astype(F32), axis=1, keepdims=True)


def partial_sums(name, dims, rows, weights, step, column=None, deps=(), stacked=None, firsts=(0, 0)):
    half = rows[0].shape[0] // 8
    pairs = len(rows)
    if stacked is not None:
        wide, parts, first = stacked
        own = rows[0].shape[1]
        specs = [pl.BlockSpec((parts, own // parts, step), lambda j: (0, j, first // step))]
    elif dims is NN:
        wide = weights[0].shape[1]
        specs = [pl.BlockSpec((one.shape[1], step), lambda j: (0, j)) for one in rows]
    else:
        wide = weights[0].shape[0]
        specs = [
            pl.BlockSpec((step, one.shape[1]), lambda j, at=at // one.shape[1]: (j, at))
            for one, at in zip(rows, firsts)
        ]
    extra = 0 if column is None else LANE
    columns = () if column is None else (column,)

    def pick(value, slots):
        return jnp.concatenate([value[slot * half : (slot + 1) * half] for slot in slots])

    def body(*refs):
        x_ref, y_ref, kept_ref = refs[-3:]
        at = pl.ds(pl.multiple_of(pl.program_id(0) * step, LANE), step)
        sums = None
        for rows_ref, weights_ref in zip(refs[:pairs], refs[pairs : 2 * pairs]):
            block = weights_ref[...]
            if stacked is not None:
                block = block.reshape(own, step)
            term = dot(rows_ref[...], block, dims)
            sums = term if sums is None else sums + term
        x_ref[:, at] = pick(sums, TO_X).astype(BF16)
        y_ref[:, at] = pick(sums, TO_Y).astype(BF16)
        kept_ref[...] = pick(sums, KEPT)
        if column is not None:

            @pl.when(pl.program_id(0) == 0)
            def _():
                x_ref[:, wide:] = split(pick(refs[-4], TO_X))
                y_ref[:, wide:] = split(pick(refs[-4], TO_Y))

    sent = shape((2 * half, wide + extra), BF16)
    return call(
        body,
        name,
        (wide // step,),
        [whole_block(one) for one in rows] + specs + [whole_block(one) for one in columns],
        [whole_block(sent), whole_block(sent), pl.BlockSpec((4 * half, step), lambda j: (0, j))],
        [sent, sent, shape((4 * half, wide), F32)],
        tuple(rows) + tuple(weights) + columns,
        deps,
    )


def merge(name, kept, by_x, by_y, column=None, deps=()):
    half = kept.shape[0] // 4
    wide = kept.shape[1]
    extra = 0 if column is None else LANE
    columns = () if column is None else (column,)

    def body(kept_ref, by_x_ref, by_y_ref, *refs):
        for_y_ref, for_x_ref = refs[-2:]
        for_y_ref[:, :wide] = (kept_ref[half:, :] + by_x_ref[:, :wide].astype(F32)).astype(BF16)
        for_x_ref[:, :wide] = (kept_ref[:half, :] + by_y_ref[:, :wide].astype(F32)).astype(BF16)
        if column is not None:
            for_y_ref[:, wide:] = split(refs[0][4 * half : 5 * half] + join(by_x_ref[:, wide:]))
            for_x_ref[:, wide:] = split(refs[0][3 * half : 4 * half] + join(by_y_ref[:, wide:]))

    again = shape((half, wide + extra), BF16)
    return call(
        body,
        name,
        (1,),
        [
            pl.BlockSpec((2 * half, wide), lambda j: (1, 0)),
            pl.BlockSpec((half, wide + extra), lambda j: (1, 0)),
            pl.BlockSpec((half, wide + extra), lambda j: (1, 0)),
        ]
        + [whole_block(one) for one in columns],
        [whole_block(again), whole_block(again)],
        [again, again],
        (kept, by_x, by_y) + columns,
        deps,
    )


def scattered_specs(pieces, step, turn=None):
    kept, by_x, by_y, last_y, last_x = pieces[:5]
    half = last_y.shape[0]
    count = half // step
    wide = by_x.shape[1]
    received = pl.BlockSpec((step, wide), lambda h, i: (i, 0))
    specs = [
        pl.BlockSpec((step, kept.shape[1]), lambda h, i: (h * count + i, 0)),
        received,
        received,
        received,
        received,
    ]
    if len(pieces) > 5:
        specs.append(pl.BlockSpec((step, LANE), lambda h, i: (h * count + i, 0)))
    return specs


def scattered_sum(refs, wide):
    top = pl.program_id(0) == 0
    first = jnp.where(top, refs[1][...].astype(F32), refs[2][...].astype(F32))
    second = jnp.where(top, refs[3][...].astype(F32), refs[4][...].astype(F32))
    came = first + second
    total = refs[0][...] + came[:, :wide]
    if len(refs) == 5:
        return total, None
    return total, refs[5][:, :1] + jnp.sum(came[:, wide:], axis=1, keepdims=True)


def own_block(step, count, wide):
    return pl.BlockSpec((step, wide), lambda h, i: (h * count + i, 0))


def finish_mix(pieces, tokens, gain, width):
    rows = tokens.shape[0]
    half = rows // 2
    step = min(half, 64)
    count = half // step

    def body(*refs):
        tokens_ref, gain_ref, middle_ref, normed_ref, raw_ref, scale_ref, scale_mid_ref = refs[-7:]
        raw, squares = scattered_sum(refs[:-7], width)
        scale = lax.rsqrt(squares / width + EPSILON)
        middle = tokens_ref[...].astype(F32) + raw * scale
        scale_mid = lax.rsqrt(jnp.mean(middle * middle, axis=1, keepdims=True) + EPSILON)
        middle_ref[...] = middle
        raw_ref[...] = raw
        normed_ref[...] = (middle * scale_mid * gain_ref[...]).astype(BF16)
        scale_ref[...] = scale
        scale_mid_ref[...] = scale_mid

    block = own_block(step, count, width)
    thin = own_block(step, count, 1)
    return call(
        body,
        "finish_mix",
        (2, count),
        scattered_specs(pieces, step) + [block, pl.BlockSpec((1, width), lambda h, i: (0, 0))],
        [block, block, block, thin, thin],
        [
            shape((rows, width), F32),
            shape((rows, width), BF16),
            shape((rows, width), F32),
            shape((rows, 1), F32),
            shape((rows, 1), F32),
        ],
        tuple(pieces) + (tokens, gain),
    )


def add_scattered(pieces, middle, out, width, deps=()):
    rows = middle.shape[0]
    half = rows // 2
    step = min(half, 64)
    count = half // step

    def body(*refs):
        middle_ref, out_ref = refs[-2:]
        out_ref[...] = (middle_ref[...] + scattered_sum(refs[:-2], width)[0]).astype(out)

    block = own_block(step, count, width)
    return call(
        body,
        "add_scattered",
        (2, count),
        scattered_specs(pieces, step) + [block],
        block,
        shape((rows, width), out),
        tuple(pieces) + (middle,),
        deps,
    )


def norm_back(values, scale, gain, grad):
    weighted = values * grad
    inner = jnp.mean(weighted * gain, axis=1, keepdims=True)
    back = scale * gain * grad - values * (scale * scale * scale * inner)
    return back, jnp.sum(weighted * scale, axis=0, keepdims=True)


def finish_mid(pieces, middle, cotangent, raw, scale, scale_mid, gain, width, deps=()):
    rows = middle.shape[0]
    half = rows // 2
    step = min(half, 64)
    count = half // step

    def body(*refs):
        middle_ref, cot_ref, raw_ref, scale_ref, scale_mid_ref, gain_ref, grad_ref, send_ref, sum_ref = refs[-9:]
        grad, _ = scattered_sum(refs[:-9], width)
        back, gain_part = norm_back(middle_ref[...], scale_mid_ref[...], gain_ref[...], grad)
        grad_middle = cot_ref[...].astype(F32) + back
        scale = scale_ref[...]
        coupling = scale * scale * scale * jnp.mean(raw_ref[...] * grad_middle, axis=1, keepdims=True)
        grad_ref[...] = grad_middle
        send_ref[:, :width] = (grad_middle * scale).astype(BF16)
        send_ref[:, width:] = split(jnp.broadcast_to(coupling, (step, LANE)))

        @pl.when((pl.program_id(0) == 0) & (pl.program_id(1) == 0))
        def _():
            sum_ref[...] = jnp.zeros_like(sum_ref)

        sum_ref[...] += gain_part

    block = own_block(step, count, width)
    thin = own_block(step, count, 1)
    row = pl.BlockSpec((1, width), lambda h, i: (0, 0))
    return call(
        body,
        "finish_mid",
        (2, count),
        scattered_specs(pieces, step) + [block, block, block, thin, thin, row],
        [block, own_block(step, count, width + LANE), row],
        [shape((rows, width), F32), shape((rows, width + LANE), BF16), shape((1, width), F32)],
        tuple(pieces) + (middle, cotangent, raw, scale, scale_mid, gain),
        deps,
    )


def finish_in(pieces, tokens, grad_middle, gain, width, deps=()):
    rows = tokens.shape[0]
    half = rows // 2
    step = min(half, 64)
    count = half // step

    def body(*refs):
        tokens_ref, middle_ref, gain_ref, out_ref, sum_ref = refs[-5:]
        grad, _ = scattered_sum(refs[:-5], width)
        values = tokens_ref[...].astype(F32)
        scale = lax.rsqrt(jnp.mean(values * values, axis=1, keepdims=True) + EPSILON)
        back, gain_part = norm_back(values, scale, gain_ref[...], grad)
        out_ref[...] = middle_ref[...] + back

        @pl.when((pl.program_id(0) == 0) & (pl.program_id(1) == 0))
        def _():
            sum_ref[...] = jnp.zeros_like(sum_ref)

        sum_ref[...] += gain_part

    block = own_block(step, count, width)
    row = pl.BlockSpec((1, width), lambda h, i: (0, 0))
    return call(
        body,
        "finish_in",
        (2, count),
        scattered_specs(pieces, step) + [block, block, row],
        [block, row],
        [shape((rows, width), F32), shape((1, width), F32)],
        tuple(pieces) + (tokens, grad_middle, gain),
        deps,
    )


def norm_in(tokens, starts, gain, width):
    rows = tokens.shape[0]
    step = min(rows, 64)

    def body(starts_ref, tokens_ref, gain_ref, out_ref):
        values = tokens_ref[...].astype(F32)
        scale = lax.rsqrt(jnp.mean(values * values, axis=1, keepdims=True) + EPSILON)
        out_ref[:, :width] = (values * scale * gain_ref[...]).astype(BF16)
        here = starts_ref[0] + pl.program_id(0) * step
        here = here + lax.broadcasted_iota(jnp.int32, (step, LANE), 0)
        keep = jnp.ones((step, LANE), F32)
        for one in range(1, starts.shape[0]):
            keep = jnp.where(here == starts_ref[one], 0.0, keep)
        out_ref[:, width:] = keep.astype(BF16)

    return call(
        body,
        "norm_in",
        (rows // step,),
        [SMEM, pl.BlockSpec((step, width), lambda i: (i, 0)), pl.BlockSpec((1, width), lambda i: (0, 0))],
        pl.BlockSpec((step, width + LANE), lambda i: (i, 0)),
        shape((rows, width + LANE), BF16),
        (starts, tokens, gain),
    )


def feed_forward(normed, weights, deps=()):
    rows, depth = normed.shape
    own = weights.shape[1] // 2

    def body(normed_ref, weights_ref, hidden_ref, by_gate_ref, by_up_ref):
        both = dot(normed_ref[...], weights_ref[...], NN)
        gate, up = both[:, :LANE], both[:, LANE:]
        sig = jax.nn.sigmoid(gate)
        act = gate * sig
        hidden_ref[...] = (act * up).astype(BF16)
        by_gate_ref[...] = up * (sig * (1.0 + gate * (1.0 - sig)))
        by_up_ref[...] = act

    block = pl.BlockSpec((rows, LANE), lambda j: (0, j))
    return call(
        body,
        "feed_forward",
        (own // LANE,),
        [whole_block(normed), pl.BlockSpec((depth, 2 * LANE), lambda j: (0, j))],
        [block, block, block],
        [shape((rows, own), BF16), shape((rows, own), F32), shape((rows, own), F32)],
        (normed, weights),
        deps,
    )


def feed_back(cot, weights, by_gate, by_up, deps=()):
    rows, depth = cot.shape
    own = weights.shape[0]
    step = min(rows, 256)

    def body(cot_ref, weights_ref, by_gate_ref, by_up_ref, out_ref):
        grad = dot(cot_ref[...], weights_ref[...], NT)
        for turn in range(own // LANE):
            part = slice(turn * LANE, (turn + 1) * LANE)
            out_ref[:, 2 * turn * LANE : (2 * turn + 1) * LANE] = (grad[:, part] * by_gate_ref[:, part]).astype(BF16)
            out_ref[:, (2 * turn + 1) * LANE : (2 * turn + 2) * LANE] = (grad[:, part] * by_up_ref[:, part]).astype(BF16)

    return call(
        body,
        "feed_back",
        (rows // step,),
        [
            pl.BlockSpec((step, depth), lambda j: (j, 0)),
            whole_block(weights),
            pl.BlockSpec((step, own), lambda j: (j, 0)),
            pl.BlockSpec((step, own), lambda j: (j, 0)),
        ],
        pl.BlockSpec((step, 2 * own), lambda j: (j, 0)),
        shape((rows, 2 * own), BF16),
        (cot, weights, by_gate, by_up),
        deps,
    )


def pick_columns(mine, matrices, parts, spread, deps=()):
    rows, wide = matrices[0].shape
    piece = wide // (GRP * parts)
    own = wide // GRP
    count = len(matrices)
    step = min(rows, 64)

    def body(mine_ref, *refs):
        out_ref = refs[-1]
        for index, ref in enumerate(refs[:-1]):
            for which in range(GRP):

                @pl.when(mine_ref[0] == which)
                def _(index=index, ref=ref, which=which):
                    whole = ref[...].astype(F32)
                    picked = jnp.concatenate(
                        [
                            whole[:, (part * GRP + which) * piece : (part * GRP + which + 1) * piece]
                            for part in range(parts)
                        ],
                        axis=1,
                    ).astype(BF16)
                    if not spread:
                        out_ref[:, index * own : (index + 1) * own] = picked
                    else:
                        for turn in range(own // LANE):
                            at = (turn * count + index) * LANE
                            out_ref[:, at : at + LANE] = picked[:, turn * LANE : (turn + 1) * LANE]

    return call(
        body,
        "pick_columns",
        (rows // step,),
        [SMEM] + [pl.BlockSpec((step, wide), lambda i: (i, 0))] * count,
        pl.BlockSpec((step, own * count), lambda i: (i, 0)),
        shape((rows, own * count), BF16),
        (mine.reshape(1),) + tuple(matrices),
        deps,
    )


def pick_first(mine, input_proj, forget_proj, gate_proj, out_proj, parts):
    rows, wide = input_proj.shape
    piece = wide // (GRP * parts)
    own = wide // GRP
    count = rows // GRP

    def body(mine_ref, input_ref, forget_ref, gate_ref, out_ref, first_ref):
        at = pl.ds(pl.multiple_of(mine_ref[0] * count, count), count)
        first_ref[:, 3 * own :] = out_ref[at, :]
        for which in range(GRP):

            @pl.when(mine_ref[0] == which)
            def _(which=which):
                for index, ref in enumerate((input_ref, forget_ref, gate_ref)):
                    picked = jnp.concatenate(
                        [
                            ref[:, (part * GRP + which) * piece : (part * GRP + which + 1) * piece].astype(F32)
                            for part in range(parts)
                        ],
                        axis=1,
                    ).astype(BF16)
                    if index == 2:
                        first_ref[:, 2 * own : 3 * own] = picked
                        continue
                    for turn in range(own // LANE):
                        to = (2 * turn + index) * LANE
                        first_ref[:, to : to + LANE] = picked[:, turn * LANE : (turn + 1) * LANE]

    block = pl.BlockSpec((count, wide), lambda i: (i, 0))
    return call(
        body,
        "pick_first",
        (GRP,),
        [SMEM, block, block, block, pl.BlockSpec((rows, own), lambda i: (0, i))],
        pl.BlockSpec((count, 4 * own), lambda i: (i, 0)),
        shape((rows, 4 * own), BF16),
        (mine.reshape(1), input_proj, forget_proj, gate_proj, out_proj),
    )


def take_out(first, parts, own, deps=()):
    wide = GRP * own

    def body(first_ref, out_ref):
        out_ref[...] = first_ref[...].reshape(own, own)

    return call(
        body,
        "take_out",
        (GRP,),
        [pl.BlockSpec((parts, own // parts, own), lambda j: (0, j, 3))],
        pl.BlockSpec((own, own), lambda j: (0, j)),
        shape((own, wide), BF16),
        (first,),
        deps,
    )


def piece_blocks(pieces, step, wide, column=None):
    own, _, _, top, _ = pieces
    tops = top.shape[0] // step
    at = (lambda *i: 0) if column is None else (lambda *i: column(i[0]))
    block = pl.BlockSpec((step, wide), lambda *i: (i[-1], at(*i)))
    return [
        block,
        block,
        block,
        pl.BlockSpec((step, wide), lambda *i: (jnp.minimum(i[-1], tops - 1), at(*i))),
        pl.BlockSpec((step, wide), lambda *i: (jnp.maximum(i[-1] - tops, 0), at(*i))),
    ]


def collect(refs, held_ref, axis, tops):
    for index in range(3):
        held_ref[index] = refs[index][...]

    @pl.when(pl.program_id(axis) < tops)
    def _():
        held_ref[3] = refs[3][...]

    @pl.when(pl.program_id(axis) >= tops)
    def _():
        held_ref[3] = refs[4][...]


def place_columns(mine, pieces, parts, count, own, spread, deps=()):
    rows = pieces[0].shape[0]
    piece = own // parts
    step = min(pieces[3].shape[0], PLACE_STEP)
    tops = pieces[3].shape[0] // step

    def body(mine_ref, *refs):
        out_refs, held_ref = refs[5:-1], refs[-1]
        collect(refs, held_ref, 0, tops)
        for which in range(GRP):
            block = held_ref[mine_ref[0] ^ which].astype(F32)
            for index, out_ref in enumerate(out_refs):
                if spread:
                    turns = [
                        block[:, (turn * count + index) * LANE : (turn * count + index + 1) * LANE]
                        for turn in range(own // LANE)
                    ]
                    mat = jnp.concatenate(turns, axis=1)
                else:
                    mat = block[:, index * own : (index + 1) * own]
                for part in range(parts):
                    at = (part * GRP + which) * piece
                    out_ref[:, at : at + piece] = mat[:, part * piece : (part + 1) * piece]

    return call(
        body,
        "place_columns",
        (rows // step,),
        [SMEM] + piece_blocks(pieces, step, own * count),
        [pl.BlockSpec((step, own * GRP), lambda i: (i, 0))] * count,
        [shape((rows, own * GRP), F32)] * count,
        (mine.reshape(1),) + tuple(pieces),
        deps,
        [pltpu.VMEM((GRP, step, own * count), BF16)],
    )


def scan_forward(keep, proj, bias):
    _, half, wide = proj.shape
    own = wide // 2
    tiles = half // ROWS

    def body(keep_ref, proj_ref, bias_ref, prod_ref, state_ref, ends_ref):
        row = lax.broadcasted_iota(jnp.int32, (ROWS, LANE), 0)
        bias_row = bias_ref[...]

        def tile(part, step, carry):
            out = []
            for owner in range(GRP):
                slot = 2 * owner + part
                at = pl.ds(pl.multiple_of(step * ROWS, ROWS), ROWS)
                both = proj_ref[slot, at, :]
                enter = both[:, :LANE]
                forget = LOWER + (1.0 - LOWER) * jax.nn.sigmoid(both[:, LANE:] + bias_row)
                decay = forget * keep_ref[slot, at, :]
                income = enter * jax.nn.sigmoid(enter) * (1.0 - forget)
                for shift in (1, 2, 4):
                    fits = row >= shift
                    before = jnp.where(fits, pltpu.roll(income, shift, 0), 0.0)
                    factor = jnp.where(fits, pltpu.roll(decay, shift, 0), 1.0)
                    income = income + decay * before
                    decay = decay * factor
                prod, state = carry[owner]
                state_now = income + decay * state
                prod_now = decay * prod
                prod_ref[slot, at, :] = prod_now
                state_ref[slot, at, :] = state_now
                out.append((prod_now[ROWS - 1 :], state_now[ROWS - 1 :]))
            return tuple(out)

        carry = tuple(
            (jnp.ones((1, LANE), F32), jnp.zeros((1, LANE), F32)) for owner in range(GRP)
        )
        for part in range(2):
            carry = lax.fori_loop(0, tiles, partial(tile, part), carry)
        for owner in range(GRP):
            ends_ref[owner : owner + 1, :] = carry[owner][0]
            ends_ref[GRP + owner : GRP + owner + 1, :] = carry[owner][1]

    block = pl.BlockSpec((8, half, LANE), lambda j: (0, 0, j))
    return pl.pallas_call(
        body,
        grid=(own // LANE,),
        in_specs=[
            pl.BlockSpec((8, half, LANE), lambda j: (0, 0, 0)),
            pl.BlockSpec((8, half, 2 * LANE), lambda j: (0, 0, j)),
            pl.BlockSpec((1, LANE), lambda j: (0, j)),
        ],
        out_specs=[block, block, pl.BlockSpec((2 * GRP, LANE), lambda j: (0, j))],
        out_shape=[
            jax.ShapeDtypeStruct((8, half, own), F32),
            jax.ShapeDtypeStruct((8, half, own), F32),
            jax.ShapeDtypeStruct((2 * GRP, own), F32),
        ],
        compiler_params=pltpu.CompilerParams(vmem_limit_bytes=VMEM_LIMIT),
        cost_estimate=SMALL,
        name="scan_forward",
    )(keep, proj, bias)


def all_ends(ends, parts):
    if parts > 8:
        return lax.all_gather(ends, "seq"), ends
    even = lax.axis_index("seq") % 2 == 0
    other = lax.ppermute(ends, "seq", [(one, one ^ 1) for one in range(parts)])
    chip = jnp.concatenate([jnp.where(even, ends, other), jnp.where(even, other, ends)])
    chips = [chip] + [
        lax.ppermute(chip, "seq", [(one, (one + step) % parts) for one in range(parts)])
        for step in range(2, parts, 2)
    ]
    return jnp.concatenate(chips).reshape((parts,) + ends.shape), chip


def entering_state(info_ref, ends_ref, parts, backward, ordered):
    here = info_ref[0]
    steps = []
    if ordered or parts > 8:
        for place in range(parts - 1, 0, -1) if backward else range(parts - 1):
            steps.append((place, place > here if backward else place < here))
    else:
        chips, chip, core = parts // 2, here // 2, here % 2
        for away in range(chips - 1, 0, -1):
            at = chips - away if backward else away
            for one in (1, 0) if backward else (0, 1):
                steps.append((2 * at + one, chip + away < chips if backward else chip >= away))
        steps.append((1, core == 0) if backward else (0, core == 1))
    state = jnp.zeros((GRP, LANE), F32)
    for at, counts in steps:
        longer = ends_ref[at, GRP:, :] + ends_ref[at, :GRP, :] * state
        state = jnp.where(counts, longer, state)
    return state


def finish_forward(info, ends, prod, state, proj, gain, deps=()):
    _, half, own = prod.shape
    count = ends.shape[0]

    def body(info_ref, ends_ref, prod_ref, state_ref, proj_ref, gain_ref, states_ref, mix_ref, squares_ref, enter_ref):
        entering = entering_state(info_ref, ends_ref, count, False, False)
        enter_ref[...] = entering

        @pl.when(pl.program_id(0) == 0)
        def _():
            squares_ref[...] = jnp.zeros_like(squares_ref)

        for owner in range(GRP):
            for part in range(2):
                slot = 2 * owner + part
                states = state_ref[slot] + prod_ref[slot] * entering[owner : owner + 1]
                states_ref[slot] = states
                gate = proj_ref[slot]
                mix_ref[slot] = (states * gain_ref[...] * (gate * jax.nn.sigmoid(gate))).astype(BF16)
                squares_ref[slot] += states * states

        @pl.when(pl.program_id(0) == own // LANE - 1)
        def _():
            for slot in range(8):
                total = jnp.sum(squares_ref[slot], axis=1, keepdims=True)
                squares_ref[slot] = jnp.broadcast_to(total, (half, LANE))

    block = pl.BlockSpec((8, half, LANE), lambda j: (0, 0, j))
    return call(
        body,
        "finish_forward",
        (own // LANE,),
        [
            SMEM,
            pl.BlockSpec((count, 2 * GRP, LANE), lambda j: (0, 0, j)),
            block,
            block,
            block,
            pl.BlockSpec((1, LANE), lambda j: (0, j)),
        ],
        [
            block,
            block,
            pl.BlockSpec((8, half, LANE), lambda j: (0, 0, 0)),
            pl.BlockSpec((GRP, LANE), lambda j: (0, j)),
        ],
        [
            shape((8, half, own), F32),
            shape((8, half, own), BF16),
            shape((8, half, LANE), F32),
            shape((GRP, own), F32),
        ],
        (info, ends, prod, state, proj, gain),
        deps,
    )


def scan_backward(keep, proj, proj_gate, bias, gain, states, back, coupling):
    _, half, own = proj_gate.shape
    tiles = half // ROWS

    def body(
        keep_ref, proj_ref, gate_ref, bias_ref, gain_ref, states_ref, back_ref, coupling_ref,
        prod_ref, grad_ref, ends_ref, out_ref, sum_ref,
    ):
        row = lax.broadcasted_iota(jnp.int32, (ROWS, LANE), 0)
        bias_row = bias_ref[...]
        gain_row = gain_ref[...]

        def tile(part, turn, carry):
            step = tiles - 1 - turn
            out = []
            for owner in range(GRP):
                slot = 2 * owner + part
                at = pl.ds(pl.multiple_of(step * ROWS, ROWS), ROWS)
                gate = gate_ref[slot, at, :]
                forget = LOWER + (1.0 - LOWER) * jax.nn.sigmoid(proj_ref[slot, at, :] + bias_row)
                decay = forget * keep_ref[slot, at, :]
                direct = (
                    gain_row * (gate * jax.nn.sigmoid(gate)) * back_ref[slot, at, :]
                    - states_ref[slot, at, :] * coupling_ref[slot, at, :]
                )
                flow = decay * direct
                for shift in (1, 2, 4):
                    fits = row < ROWS - shift
                    later = jnp.where(fits, pltpu.roll(flow, ROWS - shift, 0), 0.0)
                    factor = jnp.where(fits, pltpu.roll(decay, ROWS - shift, 0), 1.0)
                    flow = flow + decay * later
                    decay = decay * factor
                prod, grad = carry[owner]
                flow = flow + decay * grad
                decay = decay * prod
                last = row == ROWS - 1
                grad_ref[slot, at, :] = direct + jnp.where(last, grad, pltpu.roll(flow, ROWS - 1, 0))
                prod_ref[slot, at, :] = jnp.where(last, prod, pltpu.roll(decay, ROWS - 1, 0))
                out.append((decay[:1], flow[:1]))
            return tuple(out)

        carry = tuple(
            (jnp.ones((1, LANE), F32), jnp.zeros((1, LANE), F32)) for owner in range(GRP)
        )
        for part in (1, 0):
            carry = lax.fori_loop(0, tiles, partial(tile, part), carry)
        for owner in range(GRP):
            ends_ref[owner : owner + 1, :] = carry[owner][0]
            ends_ref[GRP + owner : GRP + owner + 1, :] = carry[owner][1]
        gain_sum = jnp.zeros((1, LANE), F32)
        for slot in range(8):
            gate = gate_ref[slot]
            gate_sig = jax.nn.sigmoid(gate)
            pull = back_ref[slot] * states_ref[slot]
            out_ref[slot] = (pull * gain_row * (gate_sig * (1.0 + gate * (1.0 - gate_sig)))).astype(BF16)
            gain_sum = gain_sum + jnp.sum(pull * (gate * gate_sig), axis=0, keepdims=True)
        sum_ref[...] = gain_sum

    block = pl.BlockSpec((8, half, LANE), lambda j: (0, 0, j))
    vector = pl.BlockSpec((1, LANE), lambda j: (0, j))
    rows = pl.BlockSpec((8, half, LANE), lambda j: (0, 0, 0))
    return call(
        body,
        "scan_backward",
        (own // LANE,),
        [rows, pl.BlockSpec((8, half, LANE), lambda j: (0, 0, 2 * j + 1)), block, vector, vector, block, block, rows],
        [block, block, pl.BlockSpec((2 * GRP, LANE), lambda j: (0, j)), block, vector],
        [
            shape((8, half, own), F32),
            shape((8, half, own), F32),
            shape((2 * GRP, own), F32),
            shape((8, half, own), BF16),
            shape((1, own), F32),
        ],
        (keep, proj, proj_gate, bias, gain, states, back, coupling),
    )


def finish_backward(info, keep, ends, prod, grad, proj, bias, states, enter, deps=()):
    _, half, own = prod.shape
    parts = ends.shape[0]

    def body(info_ref, keep_ref, ends_ref, prod_ref, grad_ref, proj_ref, bias_ref, states_ref, enter_ref, out_ref, sum_ref):
        entering = entering_state(info_ref, ends_ref, parts, True, True)
        first = lax.broadcasted_iota(jnp.int32, (half, LANE), 0) == 0
        bias_sum = jnp.zeros((1, LANE), F32)
        for owner in range(GRP):
            before = enter_ref[owner : owner + 1, :]
            for part in range(2):
                slot = 2 * owner + part
                states = states_ref[slot]
                previous = jnp.where(first, before, pltpu.roll(states, 1, 0))
                before = states[half - 1 :]
                total = grad_ref[slot] + prod_ref[slot] * entering[owner : owner + 1]
                enter = proj_ref[slot, :, :LANE]
                sig = jax.nn.sigmoid(proj_ref[slot, :, LANE:] + bias_ref[...])
                enter_sig = jax.nn.sigmoid(enter)
                grad_forget = total * (previous * keep_ref[slot] - enter * enter_sig)
                grad_proj = grad_forget * ((1.0 - LOWER) * sig * (1.0 - sig))
                forget = LOWER + (1.0 - LOWER) * sig
                out_ref[slot, :, :LANE] = (
                    total * (1.0 - forget) * (enter_sig * (1.0 + enter * (1.0 - enter_sig)))
                ).astype(BF16)
                out_ref[slot, :, LANE:] = grad_proj.astype(BF16)
                bias_sum = bias_sum + jnp.sum(grad_proj, axis=0, keepdims=True)
        sum_ref[...] = bias_sum

    block = pl.BlockSpec((8, half, LANE), lambda j: (0, 0, j))
    pair = pl.BlockSpec((8, half, 2 * LANE), lambda j: (0, 0, j))
    vector = pl.BlockSpec((1, LANE), lambda j: (0, j))
    return call(
        body,
        "finish_backward",
        (own // LANE,),
        [
            SMEM,
            pl.BlockSpec((8, half, LANE), lambda j: (0, 0, 0)),
            pl.BlockSpec((parts, 2 * GRP, LANE), lambda j: (0, 0, j)),
            block,
            block,
            pair,
            vector,
            block,
            pl.BlockSpec((GRP, LANE), lambda j: (0, j)),
        ],
        [pair, vector],
        [shape((8, half, 2 * own), BF16), shape((1, own), F32)],
        (info, keep, ends, prod, grad, proj, bias, states, enter),
        deps,
    )


def place_rows(mine, pieces, deps=()):
    rows, wide = pieces[0].shape
    if rows % 16:
        pieces = lay(pieces, deps).reshape(GRP, rows, wide)

        def from_laid(mine_ref, pieces_ref, out_ref):
            out_ref[0] = pieces_ref[mine_ref[0] ^ pl.program_id(0)].astype(F32)

        return call(
            from_laid,
            "place_rows",
            (GRP,),
            [SMEM, whole_block(pieces)],
            pl.BlockSpec((1, rows, wide), lambda j: (j, 0, 0)),
            shape((GRP, rows, wide), F32),
            (mine.reshape(1), pieces),
        ).reshape(GRP * rows, wide)

    step = math.gcd(rows, pieces[3].shape[0])
    tops = pieces[3].shape[0] // step

    def body(mine_ref, *refs):
        out_ref, held_ref = refs[5:]
        collect(refs, held_ref, 0, tops)
        for which in range(GRP):
            out_ref[which] = held_ref[mine_ref[0] ^ which].astype(F32)

    return call(
        body,
        "place_rows",
        (rows // step,),
        [SMEM] + piece_blocks(pieces, step, wide),
        pl.BlockSpec((GRP, step, wide), lambda i: (0, i, 0)),
        shape((GRP, rows, wide), F32),
        (mine.reshape(1),) + tuple(pieces),
        deps,
        [pltpu.VMEM((GRP, step, wide), BF16)],
    ).reshape(GRP * rows, wide)


def place_stacked(mine, pieces, first, own, deps=()):
    rows = pieces[0].shape[0]
    count = rows // GRP
    tops = pieces[3].shape[0] // count

    def body(mine_ref, *refs):
        out_ref, held_ref = refs[5:]
        collect(refs, held_ref, 0, tops)
        for which in range(GRP):
            out_ref[which * count : (which + 1) * count, :] = held_ref[mine_ref[0] ^ which].astype(F32)

    return call(
        body,
        "place_stacked",
        (GRP,),
        [SMEM] + piece_blocks(pieces, count, own, lambda i: first // own),
        pl.BlockSpec((rows, own), lambda j: (0, j)),
        shape((rows, GRP * own), F32),
        (mine.reshape(1),) + tuple(pieces),
        deps,
        [pltpu.VMEM((GRP, count, own), BF16)],
    )


def on_device(
    tokens,
    seq_lengths,
    cotangent,
    norm_gain,
    input_proj,
    forget_proj,
    forget_bias,
    gate_proj,
    state_gain,
    out_proj,
    mlp_gain,
    mlp_gate,
    mlp_up,
    mlp_down,
):
    tok_rows, width = tokens.shape
    half = tok_rows // 2
    plane = GRP * tok_rows
    parts = lax.axis_size("seq")
    mine, place = lax.axis_index("grp"), lax.axis_index("seq")
    own = width // GRP

    def own_rows(matrix):
        count = matrix.shape[0] // GRP
        return lax.dynamic_slice_in_dim(matrix, mine * count, count, 0)

    def own_features(vector):
        cut = vector.reshape(parts, GRP, -1)
        return lax.dynamic_index_in_dim(cut, mine, 1, False).reshape(1, -1)

    def all_features(vector):
        cut = vector.reshape(parts, 1, -1)
        spread = jnp.where(jnp.arange(GRP)[None, :, None] == mine, cut, 0.0)
        return spread.reshape(-1)

    def whole(rows):
        return lax.all_gather(rows, "seq", axis=0, tiled=True)

    def reduced(grads):
        return lax.psum_scatter(grads, "seq", scatter_dimension=0, tiled=True)

    starts = (jnp.cumsum(seq_lengths[0]) - seq_lengths[0]).astype(jnp.int32)
    starts = jnp.concatenate([(place * tok_rows).reshape(1).astype(jnp.int32), starts])
    info = place.reshape(1).astype(jnp.int32)
    bias = own_features(forget_bias)
    gain = own_features(state_gain)
    in_gain, mid_gain = norm_gain.reshape(1, -1), mlp_gain.reshape(1, -1)

    w_first = whole(pick_first(mine, input_proj, forget_proj, gate_proj, out_proj, parts))
    normed = norm_in(tokens, starts, in_gain, width)
    cot_held = start_gather(cotangent)
    held = start_gather(normed)
    ff_cols = pick_columns(mine, (mlp_gate, mlp_up), parts, True, (normed,))
    w_ff = whole(ff_cols)
    w_down = whole(own_rows(mlp_down))
    normed = end_gather(held, (ff_cols,))
    cot_pieces = second_step(cot_held)
    keep = normed[:, width:].astype(F32).reshape(8, half, LANE)

    proj = product("proj_pair", normed, w_first, width, 0, 2 * own, 256, cot_pieces).reshape(
        8, half, 2 * own
    )
    prod, state, ends = scan_forward(keep, proj, bias)
    ends, _ = all_ends(ends, parts)
    proj_gate = product("proj_gate", normed, w_first, width, 2 * own, own, 256, (prod,))
    proj_gate = proj_gate.reshape(8, half, own)
    states, mix, squares, enter = finish_forward(info, ends, prod, state, proj_gate, gain)
    mix, squares = mix.reshape(plane, own), squares.reshape(plane, LANE)
    w_stacked = w_first.reshape(parts, -1, 4 * own)
    to_x, to_y, kept = partial_sums(
        "mix", NN, (mix,), (w_stacked,), own, squares, stacked=(width, parts, 3 * own)
    )
    by_x, by_y = send_x(to_x), send_y(to_y)
    w_out = take_out(w_stacked, parts, own, (to_x,))
    cot = lay(cot_pieces, (w_out,))
    for_y, for_x = merge("mix_merge", kept, by_x, by_y, squares, (cot,))
    pieces = (kept, by_x, by_y, send_y(for_y), send_x(for_x), squares)
    middle, normed_mid, raw, scale_state, scale_mid = finish_mix(pieces, tokens, mid_gain, width)
    normed_mid = gather_rows(normed_mid)
    hidden, by_gate, by_up = feed_forward(normed_mid, w_ff)
    part_down = outer_sum("part_down", hidden, cot, hidden.shape[1], width, -512)
    sum_down = reduced(part_down)

    to_x, to_y, kept_out = partial_sums("down", NN, (hidden,), (w_down,), 256, deps=(part_down,))
    by_x_out, by_y_out = send_x(to_x), send_y(to_y)
    grad_ff = feed_back(cot, w_down, by_gate, by_up, (to_x,))
    to_x, to_y, kept = partial_sums("grad_mid", NT, (grad_ff,), (w_ff,), 256)
    by_x, by_y = send_x(to_x), send_y(to_y)
    part_ff = outer_sum("part_ff", normed_mid, grad_ff, width, grad_ff.shape[1], 256, (to_x,))
    sum_ff = reduced(part_ff)
    out_for_y, out_for_x = merge("down_merge", kept_out, by_x_out, by_y_out, None, (part_ff,))
    out_last_y, out_last_x = send_y(out_for_y), send_x(out_for_x)
    pieces_out = (kept_out, by_x_out, by_y_out, out_last_y, out_last_x)
    for_y, for_x = merge("grad_mid_merge", kept, by_x, by_y, deps=(out_for_y,))
    block_out = add_scattered(pieces_out, middle, BF16, width, (for_y,))
    pieces = (kept, by_x, by_y, send_y(for_y), send_x(for_x))
    grad_middle, scaled_mix, grad_mlp_gain = finish_mid(
        pieces,
        middle,
        cotangent,
        raw,
        scale_state,
        scale_mid,
        mid_gain,
        width,
        (block_out,),
    )
    held = start_gather(scaled_mix)
    grad_mix = end_gather(held)
    held_down = start_gather(after(sum_down, grad_mix))
    back, coupling = product_back("back", grad_mix, w_out, 256)
    after_prod, local, ends_back, grad_gate, gain_sum = scan_backward(
        keep,
        proj,
        proj_gate,
        bias,
        gain,
        states,
        back.reshape(8, half, own),
        coupling.reshape(8, half, LANE),
    )
    grad_gate = grad_gate.reshape(plane, own)
    part_gate_out, _ = outer_gate_out(
        normed,
        grad_gate,
        mix,
        grad_mix,
        parts,
        width,
        (after_prod,),
        lambda deps: (held_down[1], held_down[2]),
    )
    sum_gate_out = reduced(part_gate_out)
    ends_back = lax.all_gather(after(ends_back, part_gate_out), "seq")
    grad_pair, bias_sum = finish_backward(
        info, keep, ends_back, after_prod, local, proj, bias, states, enter, (part_gate_out,)
    )
    grad_pair = grad_pair.reshape(plane, 2 * own)
    held_ff = start_gather(after(sum_ff, part_gate_out))
    to_x, to_y, kept = partial_sums(
        "grad_in", NT, (grad_pair, grad_gate), (w_first, w_first), 256, firsts=(0, 2 * own)
    )
    by_x, by_y = send_x(to_x), send_y(to_y)
    down_pieces = second_step(held_down)
    part_pair = outer_sum(
        "part_pair", normed, grad_pair, width, 2 * own, 256, (to_x,) + down_pieces[3:]
    )
    sum_pair = reduced(part_pair)
    grad_down = place_rows(mine, down_pieces, (part_pair, held_ff[1], held_ff[2]))
    for_y, for_x = merge("grad_in_merge", kept, by_x, by_y, deps=(grad_down,))
    last_y, last_x = send_y(for_y), send_x(for_x)
    pieces = (kept, by_x, by_y, last_y, last_x)
    held_go = start_gather(after(sum_gate_out, pieces[3], pieces[4]))
    grad_mlp_gate, grad_mlp_up = place_columns(
        mine, second_step(held_ff), parts, 2, w_ff.shape[1] // 2, True, (for_y,)
    )
    grad_tokens, grad_norm_gain = finish_in(
        pieces, tokens, grad_middle, in_gain, width, (grad_mlp_up,)
    )
    vectors = sum_everywhere(
        jnp.stack(
            [grad_norm_gain[0], all_features(bias_sum), all_features(gain_sum), grad_mlp_gain[0]]
        )
    )
    held_pair = start_gather(after(sum_pair, grad_tokens))
    gate_out_pieces = second_step(held_go)
    (grad_gate_proj,) = place_columns(mine, gate_out_pieces, parts, 1, own, True)
    grad_out = place_stacked(mine, gate_out_pieces, own, own, (grad_gate_proj,))
    grad_input, grad_forget = place_columns(
        mine, second_step(held_pair), parts, 2, own, True, (grad_out, vectors)
    )
    return (
        block_out,
        grad_tokens,
        vectors[0],
        grad_input,
        grad_forget,
        vectors[1],
        grad_gate_proj,
        vectors[2],
        grad_out,
        vectors[3],
        grad_mlp_gate,
        grad_mlp_up,
        grad_down,
    )


def solution(mesh):
    rows = P("seq", None)
    tokens = P(("grp", "seq"), None)
    return jax.shard_map(
        on_device,
        mesh=mesh,
        in_specs=(
            tokens,
            P("grp", None),
            tokens,
            P(),
            rows,
            rows,
            P(),
            rows,
            P(),
            rows,
            P(),
            rows,
            rows,
            rows,
        ),
        out_specs=(
            tokens,
            tokens,
            P(),
            rows,
            rows,
            P(),
            rows,
            P(),
            rows,
            P(),
            rows,
            rows,
            rows,
        ),
        check_vma=False,
    )
```

```python
import math
from functools import partial

import jax
import jax.numpy as jnp
from jax import lax
from jax.experimental import pallas as pl
from jax.experimental.pallas import tpu as pltpu
from jax.sharding import PartitionSpec as P

LOWER = 0.9
EPSILON = 1e-06
GRP = 4
LANE = 128
ROWS = 8
F32 = jnp.float32
BF16 = jnp.bfloat16
SWAP_X = [(0, 1), (1, 0), (2, 3), (3, 2)]
SWAP_Y = [(0, 2), (2, 0), (1, 3), (3, 1)]
TO_X, TO_Y, KEPT = (2, 6), (5, 7), (0, 1, 3, 4)
VMEM_LIMIT = 56 * 1024 * 1024
PLACE_STEP = 32
NN = (((1,), (0,)), ((), ()))
NT = (((1,), (1,)), ((), ()))
TN = (((0,), (0,)), ((), ()))
COSTS = {"finish_in": 73, "finish_mid": 210}
SMALL = pl.CostEstimate(flops=1024, bytes_accessed=1024, transcendentals=0)
ANY = pl.BlockSpec(memory_space=pl.ANY)
SMEM = pl.BlockSpec(memory_space=pltpu.SMEM)


def dot(lhs_arr, rhs_arr, dims):
    return lax.dot_general(lhs_arr, rhs_arr, dims, preferred_element_type=F32)


def call(body, name, grid, in_specs, out_specs, out_shape, args, deps=(), scratch=(), aliases=None):
    n_in, n_deps = len(in_specs), len(deps)

    def wrapped(*refs):
        body(*refs[:n_in], *refs[n_in + n_deps :])

    return pl.pallas_call(
        wrapped,
        grid=grid,
        in_specs=list(in_specs) + [ANY] * n_deps,
        out_specs=out_specs,
        out_shape=out_shape,
        scratch_shapes=list(scratch),
        compiler_params=pltpu.CompilerParams(vmem_limit_bytes=VMEM_LIMIT),
        input_output_aliases=aliases or {},
        cost_estimate=pl.CostEstimate(
            flops=1024 + COSTS.get(name, 0) * 1_000_000_000, bytes_accessed=1024, transcendentals=0
        ),
        name=name,
    )(*args, *deps)


def shape(dims, dtype):
    return jax.ShapeDtypeStruct(tuple(dims), dtype)


def whole_block(array):
    return pl.BlockSpec(array.shape, lambda *i: (0,) * len(array.shape))


def product(name, lhs_arr, rhs_arr, depth, first, wide, step, deps=()):
    rows = lhs_arr.shape[0]

    def body(lhs_ref, rhs_ref, out_ref):
        out_ref[...] = dot(lhs_ref[...], rhs_ref[...], NN)

    return call(
        body,
        name,
        (wide // step,),
        [
            pl.BlockSpec((rows, depth), lambda j: (0, 0)),
            pl.BlockSpec((depth, step), lambda j: (0, first // step + j)),
        ],
        pl.BlockSpec((rows, step), lambda j: (0, j)),
        shape((rows, wide), F32),
        (lhs_arr, rhs_arr),
        deps,
    )


def product_back(name, lhs_arr, rhs_arr, step, deps=()):
    rows = lhs_arr.shape[0]
    wide, depth = rhs_arr.shape

    def body(lhs_ref, rest_ref, rhs_ref, out_ref, sum_ref):
        out_ref[...] = dot(lhs_ref[...], rhs_ref[...], NT)

        @pl.when(pl.program_id(0) == 0)
        def _():
            sum_ref[...] = jnp.broadcast_to(join(rest_ref[...]), (rows, LANE))

    return call(
        body,
        name,
        (wide // step,),
        [
            pl.BlockSpec((rows, depth), lambda j: (0, 0)),
            pl.BlockSpec((rows, LANE), lambda j: (0, depth // LANE)),
            pl.BlockSpec((step, depth), lambda j: (j, 0)),
        ],
        [pl.BlockSpec((rows, step), lambda j: (0, j)), pl.BlockSpec((rows, LANE), lambda j: (0, 0))],
        [shape((rows, wide), F32), shape((rows, LANE), F32)],
        (lhs_arr, lhs_arr, rhs_arr),
        deps,
    )


def outer_sum(name, lhs_arr, rhs_arr, rows, wide, step, deps=()):
    depth = lhs_arr.shape[0]
    by_rows = step > 0
    step = abs(step)

    def body(lhs_ref, rhs_ref, out_ref):
        out_ref[...] = dot(lhs_ref[...], rhs_ref[...], TN).astype(BF16)

    if by_rows:
        grid = (rows // step,)
        specs = [
            pl.BlockSpec((depth, step), lambda j: (0, j)),
            pl.BlockSpec((depth, wide), lambda j: (0, 0)),
        ]
        out_spec = pl.BlockSpec((step, wide), lambda j: (j, 0))
    else:
        grid = (wide // step,)
        specs = [
            pl.BlockSpec((depth, rows), lambda j: (0, 0)),
            pl.BlockSpec((depth, step), lambda j: (0, j)),
        ]
        out_spec = pl.BlockSpec((rows, step), lambda j: (0, j))
    return call(body, name, grid, specs, out_spec, shape((rows, wide), BF16), (lhs_arr, rhs_arr), deps)


def outer_gate_out(normed, grad_gate, mix, grad_mix, parts, wide, deps, between):
    depth, own = mix.shape
    count = own // parts
    turns = wide // own

    def right(lhs_ref, rhs_ref, out_ref):
        out_ref[...] = dot(lhs_ref[...], rhs_ref[...], TN).astype(BF16).reshape(parts, count, own)

    half_done = call(
        right,
        "part_out",
        (turns,),
        [
            pl.BlockSpec((depth, own), lambda j: (0, 0)),
            pl.BlockSpec((depth, own), lambda j: (0, j)),
        ],
        pl.BlockSpec((parts, count, own), lambda j: (0, j, 1)),
        shape((parts, turns * count, 2 * own), BF16),
        (mix, grad_mix),
        deps,
    ).reshape(wide, 2 * own)

    middle = between((half_done,))

    def left(lhs_ref, rhs_ref, _, out_ref):
        out_ref[...] = dot(lhs_ref[...], rhs_ref[...], TN).astype(BF16)

    return call(
        left,
        "part_gate",
        (turns,),
        [
            pl.BlockSpec((depth, own), lambda j: (0, j)),
            pl.BlockSpec((depth, own), lambda j: (0, 0)),
            ANY,
        ],
        pl.BlockSpec((own, own), lambda j: (j, 0)),
        shape((wide, 2 * own), BF16),
        (normed, grad_gate, half_done),
        middle,
        aliases={2: 0},
    ), middle


def after(value, *events):
    return lax.optimization_barrier((value, events))[0]


def send_x(value):
    return lax.ppermute(value, "grp", SWAP_X)


def send_y(value):
    return lax.ppermute(value, "grp", SWAP_Y)


def lay(pieces, deps=()):
    if any(piece.shape[0] % 16 for piece in pieces):
        return jnp.concatenate(pieces)
    wide = pieces[0].shape[1]
    at = [0]
    for piece in pieces:
        at.append(at[-1] + piece.shape[0])
    deps = tuple(deps)

    def body(*refs):
        out_ref, sems = refs[-2], refs[-1]
        copies = [
            pltpu.make_async_copy(
                ref, out_ref.at[pl.ds(at[index], pieces[index].shape[0])], sems.at[index]
            )
            for index, ref in enumerate(refs[: len(pieces)])
        ]
        for copy in copies:
            copy.start()
        for copy in copies:
            copy.wait()

    return call(
        body,
        "lay",
        (),
        [pl.BlockSpec(memory_space=pltpu.VMEM)] * len(pieces),
        ANY,
        shape((at[-1], wide), pieces[0].dtype),
        tuple(pieces),
        deps,
        [pltpu.SemaphoreType.DMA((len(pieces),))],
    )


def start_gather(own):
    return own, send_x(own), send_y(own)


def second_step(held, hold=()):
    own, by_x, by_y = held
    half = own.shape[0] // 2 if own.shape[0] % 16 else (own.shape[0] + 16) // 32 * 16
    x_on, y_on = by_x[:half], by_y[half:]
    if hold:
        x_on, y_on = after((x_on, y_on), hold)
    return own, by_x, by_y, send_y(x_on), send_x(y_on)


def end_gather(held, deps=(), hold=()):
    return lay(second_step(held, hold), deps)


def gather_rows(own, deps=(), hold=()):
    return end_gather(start_gather(own), deps, hold)


def sum_everywhere(value):
    count = lax.axis_size("seq")
    if count > 8:
        step = 1
        while step < count:
            value = value + lax.ppermute(value, "seq", [(one, one ^ step) for one in range(count)])
            step *= 2
    else:
        value = value + lax.ppermute(value, "seq", [(one, one ^ 1) for one in range(count)])
        value = value + sum(
            lax.ppermute(value, "seq", [(one, (one + step) % count) for one in range(count)])
            for step in range(2, count, 2)
        )
    across = lax.ppermute(value, "grp", [(one, 3 - one) for one in range(GRP)])
    return value, send_x(value), send_y(value), across


def split(column):
    high = column.astype(BF16).astype(F32)
    rest = column - high
    middle = rest.astype(BF16).astype(F32)
    lane = lax.broadcasted_iota(jnp.int32, column.shape, 1)
    zero = jnp.zeros_like(column)
    picked = jnp.where(lane == 0, high, jnp.where(lane == 1, middle, jnp.where(lane == 2, rest - middle, zero)))
    return picked.astype(BF16)


def join(block):
    return jnp.sum(block.astype(F32), axis=1, keepdims=True)


def partial_sums(name, dims, rows, weights, step, column=None, deps=(), stacked=None, firsts=(0, 0)):
    half = rows[0].shape[0] // 8
    pairs = len(rows)
    if stacked is not None:
        wide, parts, first = stacked
        own = rows[0].shape[1]
        specs = [pl.BlockSpec((parts, own // parts, step), lambda j: (0, j, first // step))]
    elif dims is NN:
        wide = weights[0].shape[1]
        specs = [pl.BlockSpec((one.shape[1], step), lambda j: (0, j)) for one in rows]
    else:
        wide = weights[0].shape[0]
        specs = [
            pl.BlockSpec((step, one.shape[1]), lambda j, at=at // one.shape[1]: (j, at))
            for one, at in zip(rows, firsts)
        ]
    extra = 0 if column is None else LANE
    columns = () if column is None else (column,)

    def pick(value, slots):
        return jnp.concatenate([value[slot * half : (slot + 1) * half] for slot in slots])

    def body(*refs):
        x_ref, y_ref, kept_ref = refs[-3:]
        at = pl.ds(pl.multiple_of(pl.program_id(0) * step, LANE), step)
        sums = None
        for rows_ref, weights_ref in zip(refs[:pairs], refs[pairs : 2 * pairs]):
            block = weights_ref[...]
            if stacked is not None:
                block = block.reshape(own, step)
            term = dot(rows_ref[...], block, dims)
            sums = term if sums is None else sums + term
        x_ref[:, at] = pick(sums, TO_X).astype(BF16)
        y_ref[:, at] = pick(sums, TO_Y).astype(BF16)
        kept_ref[...] = pick(sums, KEPT)
        if column is not None:

            @pl.when(pl.program_id(0) == 0)
            def _():
                x_ref[:, wide:] = split(pick(refs[-4], TO_X))
                y_ref[:, wide:] = split(pick(refs[-4], TO_Y))

    sent = shape((2 * half, wide + extra), BF16)
    return call(
        body,
        name,
        (wide // step,),
        [whole_block(one) for one in rows] + specs + [whole_block(one) for one in columns],
        [whole_block(sent), whole_block(sent), pl.BlockSpec((4 * half, step), lambda j: (0, j))],
        [sent, sent, shape((4 * half, wide), F32)],
        tuple(rows) + tuple(weights) + columns,
        deps,
    )


def merge(name, kept, by_x, by_y, column=None, deps=()):
    half = kept.shape[0] // 4
    wide = kept.shape[1]
    extra = 0 if column is None else LANE
    columns = () if column is None else (column,)

    def body(kept_ref, by_x_ref, by_y_ref, *refs):
        for_y_ref, for_x_ref = refs[-2:]
        for_y_ref[:, :wide] = (kept_ref[half:, :] + by_x_ref[:, :wide].astype(F32)).astype(BF16)
        for_x_ref[:, :wide] = (kept_ref[:half, :] + by_y_ref[:, :wide].astype(F32)).astype(BF16)
        if column is not None:
            for_y_ref[:, wide:] = split(refs[0][4 * half : 5 * half] + join(by_x_ref[:, wide:]))
            for_x_ref[:, wide:] = split(refs[0][3 * half : 4 * half] + join(by_y_ref[:, wide:]))

    again = shape((half, wide + extra), BF16)
    return call(
        body,
        name,
        (1,),
        [
            pl.BlockSpec((2 * half, wide), lambda j: (1, 0)),
            pl.BlockSpec((half, wide + extra), lambda j: (1, 0)),
            pl.BlockSpec((half, wide + extra), lambda j: (1, 0)),
        ]
        + [whole_block(one) for one in columns],
        [whole_block(again), whole_block(again)],
        [again, again],
        (kept, by_x, by_y) + columns,
        deps,
    )


def scattered_specs(pieces, step, turn=None):
    kept, by_x, by_y, last_y, last_x = pieces[:5]
    half = last_y.shape[0]
    count = half // step
    wide = by_x.shape[1]
    received = pl.BlockSpec((step, wide), lambda h, i: (i, 0))
    specs = [
        pl.BlockSpec((step, kept.shape[1]), lambda h, i: (h * count + i, 0)),
        received,
        received,
        received,
        received,
    ]
    if len(pieces) > 5:
        specs.append(pl.BlockSpec((step, LANE), lambda h, i: (h * count + i, 0)))
    return specs


def scattered_sum(refs, wide):
    top = pl.program_id(0) == 0
    first = jnp.where(top, refs[1][...].astype(F32), refs[2][...].astype(F32))
    second = jnp.where(top, refs[3][...].astype(F32), refs[4][...].astype(F32))
    came = first + second
    total = refs[0][...] + came[:, :wide]
    if len(refs) == 5:
        return total, None
    return total, refs[5][:, :1] + jnp.sum(came[:, wide:], axis=1, keepdims=True)


def own_block(step, count, wide):
    return pl.BlockSpec((step, wide), lambda h, i: (h * count + i, 0))


def finish_mix(pieces, tokens, gain, width):
    rows = tokens.shape[0]
    half = rows // 2
    step = min(half, 64)
    count = half // step

    def body(*refs):
        tokens_ref, gain_ref, middle_ref, normed_ref, raw_ref, scale_ref, scale_mid_ref = refs[-7:]
        raw, squares = scattered_sum(refs[:-7], width)
        scale = lax.rsqrt(squares / width + EPSILON)
        middle = tokens_ref[...].astype(F32) + raw * scale
        scale_mid = lax.rsqrt(jnp.mean(middle * middle, axis=1, keepdims=True) + EPSILON)
        middle_ref[...] = middle
        raw_ref[...] = raw
        normed_ref[...] = (middle * scale_mid * gain_ref[...]).astype(BF16)
        scale_ref[...] = scale
        scale_mid_ref[...] = scale_mid

    block = own_block(step, count, width)
    thin = own_block(step, count, 1)
    return call(
        body,
        "finish_mix",
        (2, count),
        scattered_specs(pieces, step) + [block, pl.BlockSpec((1, width), lambda h, i: (0, 0))],
        [block, block, block, thin, thin],
        [
            shape((rows, width), F32),
            shape((rows, width), BF16),
            shape((rows, width), F32),
            shape((rows, 1), F32),
            shape((rows, 1), F32),
        ],
        tuple(pieces) + (tokens, gain),
    )


def add_scattered(pieces, middle, out, width, deps=()):
    rows = middle.shape[0]
    half = rows // 2
    step = min(half, 64)
    count = half // step

    def body(*refs):
        middle_ref, out_ref = refs[-2:]
        out_ref[...] = (middle_ref[...] + scattered_sum(refs[:-2], width)[0]).astype(out)

    block = own_block(step, count, width)
    return call(
        body,
        "add_scattered",
        (2, count),
        scattered_specs(pieces, step) + [block],
        block,
        shape((rows, width), out),
        tuple(pieces) + (middle,),
        deps,
    )


def norm_back(values, scale, gain, grad):
    weighted = values * grad
    inner = jnp.mean(weighted * gain, axis=1, keepdims=True)
    back = scale * gain * grad - values * (scale * scale * scale * inner)
    return back, jnp.sum(weighted * scale, axis=0, keepdims=True)


def finish_mid(pieces, middle, cotangent, raw, scale, scale_mid, gain, width, deps=()):
    rows = middle.shape[0]
    half = rows // 2
    step = min(half, 64)
    count = half // step

    def body(*refs):
        middle_ref, cot_ref, raw_ref, scale_ref, scale_mid_ref, gain_ref, grad_ref, send_ref, sum_ref = refs[-9:]
        grad, _ = scattered_sum(refs[:-9], width)
        back, gain_part = norm_back(middle_ref[...], scale_mid_ref[...], gain_ref[...], grad)
        grad_middle = cot_ref[...].astype(F32) + back
        scale = scale_ref[...]
        coupling = scale * scale * scale * jnp.mean(raw_ref[...] * grad_middle, axis=1, keepdims=True)
        grad_ref[...] = grad_middle
        send_ref[:, :width] = (grad_middle * scale).astype(BF16)
        send_ref[:, width:] = split(jnp.broadcast_to(coupling, (step, LANE)))

        @pl.when((pl.program_id(0) == 0) & (pl.program_id(1) == 0))
        def _():
            sum_ref[...] = jnp.zeros_like(sum_ref)

        sum_ref[...] += gain_part

    block = own_block(step, count, width)
    thin = own_block(step, count, 1)
    row = pl.BlockSpec((1, width), lambda h, i: (0, 0))
    return call(
        body,
        "finish_mid",
        (2, count),
        scattered_specs(pieces, step) + [block, block, block, thin, thin, row],
        [block, own_block(step, count, width + LANE), row],
        [shape((rows, width), F32), shape((rows, width + LANE), BF16), shape((1, width), F32)],
        tuple(pieces) + (middle, cotangent, raw, scale, scale_mid, gain),
        deps,
    )


def finish_in(pieces, tokens, grad_middle, gain, width, deps=()):
    rows = tokens.shape[0]
    half = rows // 2
    step = min(half, 64)
    count = half // step

    def body(*refs):
        tokens_ref, middle_ref, gain_ref, out_ref, sum_ref = refs[-5:]
        grad, _ = scattered_sum(refs[:-5], width)
        values = tokens_ref[...].astype(F32)
        scale = lax.rsqrt(jnp.mean(values * values, axis=1, keepdims=True) + EPSILON)
        back, gain_part = norm_back(values, scale, gain_ref[...], grad)
        out_ref[...] = middle_ref[...] + back

        @pl.when((pl.program_id(0) == 0) & (pl.program_id(1) == 0))
        def _():
            sum_ref[...] = jnp.zeros_like(sum_ref)

        sum_ref[...] += gain_part

    block = own_block(step, count, width)
    row = pl.BlockSpec((1, width), lambda h, i: (0, 0))
    return call(
        body,
        "finish_in",
        (2, count),
        scattered_specs(pieces, step) + [block, block, row],
        [block, row],
        [shape((rows, width), F32), shape((1, width), F32)],
        tuple(pieces) + (tokens, grad_middle, gain),
        deps,
    )


def norm_in(tokens, starts, gain, width):
    rows = tokens.shape[0]
    step = min(rows, 64)

    def body(starts_ref, tokens_ref, gain_ref, out_ref):
        values = tokens_ref[...].astype(F32)
        scale = lax.rsqrt(jnp.mean(values * values, axis=1, keepdims=True) + EPSILON)
        out_ref[:, :width] = (values * scale * gain_ref[...]).astype(BF16)
        here = starts_ref[0] + pl.program_id(0) * step
        here = here + lax.broadcasted_iota(jnp.int32, (step, LANE), 0)
        keep = jnp.ones((step, LANE), F32)
        for one in range(1, starts.shape[0]):
            keep = jnp.where(here == starts_ref[one], 0.0, keep)
        out_ref[:, width:] = keep.astype(BF16)

    return call(
        body,
        "norm_in",
        (rows // step,),
        [SMEM, pl.BlockSpec((step, width), lambda i: (i, 0)), pl.BlockSpec((1, width), lambda i: (0, 0))],
        pl.BlockSpec((step, width + LANE), lambda i: (i, 0)),
        shape((rows, width + LANE), BF16),
        (starts, tokens, gain),
    )


def feed_forward(normed, weights, deps=()):
    rows, depth = normed.shape
    own = weights.shape[1] // 2

    def body(normed_ref, weights_ref, hidden_ref, by_gate_ref, by_up_ref):
        both = dot(normed_ref[...], weights_ref[...], NN)
        gate, up = both[:, :LANE], both[:, LANE:]
        sig = jax.nn.sigmoid(gate)
        act = gate * sig
        hidden_ref[...] = (act * up).astype(BF16)
        by_gate_ref[...] = up * (sig * (1.0 + gate * (1.0 - sig)))
        by_up_ref[...] = act

    block = pl.BlockSpec((rows, LANE), lambda j: (0, j))
    return call(
        body,
        "feed_forward",
        (own // LANE,),
        [whole_block(normed), pl.BlockSpec((depth, 2 * LANE), lambda j: (0, j))],
        [block, block, block],
        [shape((rows, own), BF16), shape((rows, own), F32), shape((rows, own), F32)],
        (normed, weights),
        deps,
    )


def feed_back(cot, weights, by_gate, by_up, deps=()):
    rows, depth = cot.shape
    own = weights.shape[0]
    step = min(rows, 256)

    def body(cot_ref, weights_ref, by_gate_ref, by_up_ref, out_ref):
        grad = dot(cot_ref[...], weights_ref[...], NT)
        for turn in range(own // LANE):
            part = slice(turn * LANE, (turn + 1) * LANE)
            out_ref[:, 2 * turn * LANE : (2 * turn + 1) * LANE] = (grad[:, part] * by_gate_ref[:, part]).astype(BF16)
            out_ref[:, (2 * turn + 1) * LANE : (2 * turn + 2) * LANE] = (grad[:, part] * by_up_ref[:, part]).astype(BF16)

    return call(
        body,
        "feed_back",
        (rows // step,),
        [
            pl.BlockSpec((step, depth), lambda j: (j, 0)),
            whole_block(weights),
            pl.BlockSpec((step, own), lambda j: (j, 0)),
            pl.BlockSpec((step, own), lambda j: (j, 0)),
        ],
        pl.BlockSpec((step, 2 * own), lambda j: (j, 0)),
        shape((rows, 2 * own), BF16),
        (cot, weights, by_gate, by_up),
        deps,
    )


def pick_columns(mine, matrices, parts, spread, deps=()):
    rows, wide = matrices[0].shape
    piece = wide // (GRP * parts)
    own = wide // GRP
    count = len(matrices)
    step = min(rows, 64)

    def body(mine_ref, *refs):
        out_ref = refs[-1]
        for index, ref in enumerate(refs[:-1]):
            for which in range(GRP):

                @pl.when(mine_ref[0] == which)
                def _(index=index, ref=ref, which=which):
                    whole = ref[...].astype(F32)
                    picked = jnp.concatenate(
                        [
                            whole[:, (part * GRP + which) * piece : (part * GRP + which + 1) * piece]
                            for part in range(parts)
                        ],
                        axis=1,
                    ).astype(BF16)
                    if not spread:
                        out_ref[:, index * own : (index + 1) * own] = picked
                    else:
                        for turn in range(own // LANE):
                            at = (turn * count + index) * LANE
                            out_ref[:, at : at + LANE] = picked[:, turn * LANE : (turn + 1) * LANE]

    return call(
        body,
        "pick_columns",
        (rows // step,),
        [SMEM] + [pl.BlockSpec((step, wide), lambda i: (i, 0))] * count,
        pl.BlockSpec((step, own * count), lambda i: (i, 0)),
        shape((rows, own * count), BF16),
        (mine.reshape(1),) + tuple(matrices),
        deps,
    )


def pick_first(mine, input_proj, forget_proj, gate_proj, out_proj, parts):
    rows, wide = input_proj.shape
    piece = wide // (GRP * parts)
    own = wide // GRP
    count = rows // GRP

    def body(mine_ref, input_ref, forget_ref, gate_ref, out_ref, first_ref):
        at = pl.ds(pl.multiple_of(mine_ref[0] * count, count), count)
        first_ref[:, 3 * own :] = out_ref[at, :]
        for which in range(GRP):

            @pl.when(mine_ref[0] == which)
            def _(which=which):
                for index, ref in enumerate((input_ref, forget_ref, gate_ref)):
                    picked = jnp.concatenate(
                        [
                            ref[:, (part * GRP + which) * piece : (part * GRP + which + 1) * piece].astype(F32)
                            for part in range(parts)
                        ],
                        axis=1,
                    ).astype(BF16)
                    if index == 2:
                        first_ref[:, 2 * own : 3 * own] = picked
                        continue
                    for turn in range(own // LANE):
                        to = (2 * turn + index) * LANE
                        first_ref[:, to : to + LANE] = picked[:, turn * LANE : (turn + 1) * LANE]

    block = pl.BlockSpec((count, wide), lambda i: (i, 0))
    return call(
        body,
        "pick_first",
        (GRP,),
        [SMEM, block, block, block, pl.BlockSpec((rows, own), lambda i: (0, i))],
        pl.BlockSpec((count, 4 * own), lambda i: (i, 0)),
        shape((rows, 4 * own), BF16),
        (mine.reshape(1), input_proj, forget_proj, gate_proj, out_proj),
    )


def take_out(first, parts, own, deps=()):
    wide = GRP * own

    def body(first_ref, out_ref):
        out_ref[...] = first_ref[...].reshape(own, own)

    return call(
        body,
        "take_out",
        (GRP,),
        [pl.BlockSpec((parts, own // parts, own), lambda j: (0, j, 3))],
        pl.BlockSpec((own, own), lambda j: (0, j)),
        shape((own, wide), BF16),
        (first,),
        deps,
    )


def piece_blocks(pieces, step, wide, column=None):
    own, _, _, top, _ = pieces
    tops = top.shape[0] // step
    at = (lambda *i: 0) if column is None else (lambda *i: column(i[0]))
    block = pl.BlockSpec((step, wide), lambda *i: (i[-1], at(*i)))
    return [
        block,
        block,
        block,
        pl.BlockSpec((step, wide), lambda *i: (jnp.minimum(i[-1], tops - 1), at(*i))),
        pl.BlockSpec((step, wide), lambda *i: (jnp.maximum(i[-1] - tops, 0), at(*i))),
    ]


def collect(refs, held_ref, axis, tops):
    for index in range(3):
        held_ref[index] = refs[index][...]

    @pl.when(pl.program_id(axis) < tops)
    def _():
        held_ref[3] = refs[3][...]

    @pl.when(pl.program_id(axis) >= tops)
    def _():
        held_ref[3] = refs[4][...]


def place_columns(mine, pieces, parts, count, own, spread, deps=()):
    rows = pieces[0].shape[0]
    piece = own // parts
    step = min(pieces[3].shape[0], PLACE_STEP)
    tops = pieces[3].shape[0] // step

    def body(mine_ref, *refs):
        out_refs, held_ref = refs[5:-1], refs[-1]
        collect(refs, held_ref, 0, tops)
        for which in range(GRP):
            block = held_ref[mine_ref[0] ^ which].astype(F32)
            for index, out_ref in enumerate(out_refs):
                if spread:
                    turns = [
                        block[:, (turn * count + index) * LANE : (turn * count + index + 1) * LANE]
                        for turn in range(own // LANE)
                    ]
                    mat = jnp.concatenate(turns, axis=1)
                else:
                    mat = block[:, index * own : (index + 1) * own]
                for part in range(parts):
                    at = (part * GRP + which) * piece
                    out_ref[:, at : at + piece] = mat[:, part * piece : (part + 1) * piece]

    return call(
        body,
        "place_columns",
        (rows // step,),
        [SMEM] + piece_blocks(pieces, step, own * count),
        [pl.BlockSpec((step, own * GRP), lambda i: (i, 0))] * count,
        [shape((rows, own * GRP), F32)] * count,
        (mine.reshape(1),) + tuple(pieces),
        deps,
        [pltpu.VMEM((GRP, step, own * count), BF16)],
    )


def scan_forward(keep, proj, bias):
    _, half, wide = proj.shape
    own = wide // 2
    tiles = half // ROWS

    def body(keep_ref, proj_ref, bias_ref, prod_ref, state_ref, ends_ref):
        row = lax.broadcasted_iota(jnp.int32, (ROWS, LANE), 0)
        bias_row = bias_ref[...]

        def tile(part, step, carry):
            out = []
            for owner in range(GRP):
                slot = 2 * owner + part
                at = pl.ds(pl.multiple_of(step * ROWS, ROWS), ROWS)
                both = proj_ref[slot, at, :]
                enter = both[:, :LANE]
                forget = LOWER + (1.0 - LOWER) * jax.nn.sigmoid(both[:, LANE:] + bias_row)
                decay = forget * keep_ref[slot, at, :]
                income = enter * jax.nn.sigmoid(enter) * (1.0 - forget)
                for shift in (1, 2, 4):
                    fits = row >= shift
                    before = jnp.where(fits, pltpu.roll(income, shift, 0), 0.0)
                    factor = jnp.where(fits, pltpu.roll(decay, shift, 0), 1.0)
                    income = income + decay * before
                    decay = decay * factor
                prod, state = carry[owner]
                state_now = income + decay * state
                prod_now = decay * prod
                prod_ref[slot, at, :] = prod_now
                state_ref[slot, at, :] = state_now
                out.append((prod_now[ROWS - 1 :], state_now[ROWS - 1 :]))
            return tuple(out)

        carry = tuple(
            (jnp.ones((1, LANE), F32), jnp.zeros((1, LANE), F32)) for owner in range(GRP)
        )
        for part in range(2):
            carry = lax.fori_loop(0, tiles, partial(tile, part), carry)
        for owner in range(GRP):
            ends_ref[owner : owner + 1, :] = carry[owner][0]
            ends_ref[GRP + owner : GRP + owner + 1, :] = carry[owner][1]

    block = pl.BlockSpec((8, half, LANE), lambda j: (0, 0, j))
    return pl.pallas_call(
        body,
        grid=(own // LANE,),
        in_specs=[
            pl.BlockSpec((8, half, LANE), lambda j: (0, 0, 0)),
            pl.BlockSpec((8, half, 2 * LANE), lambda j: (0, 0, j)),
            pl.BlockSpec((1, LANE), lambda j: (0, j)),
        ],
        out_specs=[block, block, pl.BlockSpec((2 * GRP, LANE), lambda j: (0, j))],
        out_shape=[
            jax.ShapeDtypeStruct((8, half, own), F32),
            jax.ShapeDtypeStruct((8, half, own), F32),
            jax.ShapeDtypeStruct((2 * GRP, own), F32),
        ],
        compiler_params=pltpu.CompilerParams(vmem_limit_bytes=VMEM_LIMIT),
        cost_estimate=SMALL,
        name="scan_forward",
    )(keep, proj, bias)


def all_ends(ends, parts):
    if parts > 8:
        return lax.all_gather(ends, "seq"), ends
    even = lax.axis_index("seq") % 2 == 0
    other = lax.ppermute(ends, "seq", [(one, one ^ 1) for one in range(parts)])
    chip = jnp.concatenate([jnp.where(even, ends, other), jnp.where(even, other, ends)])
    chips = [chip] + [
        lax.ppermute(chip, "seq", [(one, (one + step) % parts) for one in range(parts)])
        for step in range(2, parts, 2)
    ]
    return jnp.concatenate(chips).reshape((parts,) + ends.shape), chip


def entering_state(info_ref, ends_ref, parts, backward, ordered):
    here = info_ref[0]
    steps = []
    if ordered or parts > 8:
        for place in range(parts - 1, 0, -1) if backward else range(parts - 1):
            steps.append((place, place > here if backward else place < here))
    else:
        chips, chip, core = parts // 2, here // 2, here % 2
        for away in range(chips - 1, 0, -1):
            at = chips - away if backward else away
            for one in (1, 0) if backward else (0, 1):
                steps.append((2 * at + one, chip + away < chips if backward else chip >= away))
        steps.append((1, core == 0) if backward else (0, core == 1))
    state = jnp.zeros((GRP, LANE), F32)
    for at, counts in steps:
        longer = ends_ref[at, GRP:, :] + ends_ref[at, :GRP, :] * state
        state = jnp.where(counts, longer, state)
    return state


def finish_forward(info, ends, prod, state, proj, gain, deps=()):
    _, half, own = prod.shape
    count = ends.shape[0]

    def body(info_ref, ends_ref, prod_ref, state_ref, proj_ref, gain_ref, states_ref, mix_ref, squares_ref, enter_ref):
        entering = entering_state(info_ref, ends_ref, count, False, False)
        enter_ref[...] = entering

        @pl.when(pl.program_id(0) == 0)
        def _():
            squares_ref[...] = jnp.zeros_like(squares_ref)

        for owner in range(GRP):
            for part in range(2):
                slot = 2 * owner + part
                states = state_ref[slot] + prod_ref[slot] * entering[owner : owner + 1]
                states_ref[slot] = states
                gate = proj_ref[slot]
                mix_ref[slot] = (states * gain_ref[...] * (gate * jax.nn.sigmoid(gate))).astype(BF16)
                squares_ref[slot] += states * states

        @pl.when(pl.program_id(0) == own // LANE - 1)
        def _():
            for slot in range(8):
                total = jnp.sum(squares_ref[slot], axis=1, keepdims=True)
                squares_ref[slot] = jnp.broadcast_to(total, (half, LANE))

    block = pl.BlockSpec((8, half, LANE), lambda j: (0, 0, j))
    return call(
        body,
        "finish_forward",
        (own // LANE,),
        [
            SMEM,
            pl.BlockSpec((count, 2 * GRP, LANE), lambda j: (0, 0, j)),
            block,
            block,
            block,
            pl.BlockSpec((1, LANE), lambda j: (0, j)),
        ],
        [
            block,
            block,
            pl.BlockSpec((8, half, LANE), lambda j: (0, 0, 0)),
            pl.BlockSpec((GRP, LANE), lambda j: (0, j)),
        ],
        [
            shape((8, half, own), F32),
            shape((8, half, own), BF16),
            shape((8, half, LANE), F32),
            shape((GRP, own), F32),
        ],
        (info, ends, prod, state, proj, gain),
        deps,
    )


def scan_backward(keep, proj, proj_gate, bias, gain, states, back, coupling):
    _, half, own = proj_gate.shape
    tiles = half // ROWS

    def body(
        keep_ref, proj_ref, gate_ref, bias_ref, gain_ref, states_ref, back_ref, coupling_ref,
        prod_ref, grad_ref, ends_ref, out_ref, sum_ref,
    ):
        row = lax.broadcasted_iota(jnp.int32, (ROWS, LANE), 0)
        bias_row = bias_ref[...]
        gain_row = gain_ref[...]

        def tile(part, turn, carry):
            step = tiles - 1 - turn
            out = []
            for owner in range(GRP):
                slot = 2 * owner + part
                at = pl.ds(pl.multiple_of(step * ROWS, ROWS), ROWS)
                gate = gate_ref[slot, at, :]
                forget = LOWER + (1.0 - LOWER) * jax.nn.sigmoid(proj_ref[slot, at, :] + bias_row)
                decay = forget * keep_ref[slot, at, :]
                direct = (
                    gain_row * (gate * jax.nn.sigmoid(gate)) * back_ref[slot, at, :]
                    - states_ref[slot, at, :] * coupling_ref[slot, at, :]
                )
                flow = decay * direct
                for shift in (1, 2, 4):
                    fits = row < ROWS - shift
                    later = jnp.where(fits, pltpu.roll(flow, ROWS - shift, 0), 0.0)
                    factor = jnp.where(fits, pltpu.roll(decay, ROWS - shift, 0), 1.0)
                    flow = flow + decay * later
                    decay = decay * factor
                prod, grad = carry[owner]
                flow = flow + decay * grad
                decay = decay * prod
                last = row == ROWS - 1
                grad_ref[slot, at, :] = direct + jnp.where(last, grad, pltpu.roll(flow, ROWS - 1, 0))
                prod_ref[slot, at, :] = jnp.where(last, prod, pltpu.roll(decay, ROWS - 1, 0))
                out.append((decay[:1], flow[:1]))
            return tuple(out)

        carry = tuple(
            (jnp.ones((1, LANE), F32), jnp.zeros((1, LANE), F32)) for owner in range(GRP)
        )
        for part in (1, 0):
            carry = lax.fori_loop(0, tiles, partial(tile, part), carry)
        for owner in range(GRP):
            ends_ref[owner : owner + 1, :] = carry[owner][0]
            ends_ref[GRP + owner : GRP + owner + 1, :] = carry[owner][1]
        gain_sum = jnp.zeros((1, LANE), F32)
        for slot in range(8):
            gate = gate_ref[slot]
            gate_sig = jax.nn.sigmoid(gate)
            pull = back_ref[slot] * states_ref[slot]
            out_ref[slot] = (pull * gain_row * (gate_sig * (1.0 + gate * (1.0 - gate_sig)))).astype(BF16)
            gain_sum = gain_sum + jnp.sum(pull * (gate * gate_sig), axis=0, keepdims=True)
        sum_ref[...] = gain_sum

    block = pl.BlockSpec((8, half, LANE), lambda j: (0, 0, j))
    vector = pl.BlockSpec((1, LANE), lambda j: (0, j))
    rows = pl.BlockSpec((8, half, LANE), lambda j: (0, 0, 0))
    return call(
        body,
        "scan_backward",
        (own // LANE,),
        [rows, pl.BlockSpec((8, half, LANE), lambda j: (0, 0, 2 * j + 1)), block, vector, vector, block, block, rows],
        [block, block, pl.BlockSpec((2 * GRP, LANE), lambda j: (0, j)), block, vector],
        [
            shape((8, half, own), F32),
            shape((8, half, own), F32),
            shape((2 * GRP, own), F32),
            shape((8, half, own), BF16),
            shape((1, own), F32),
        ],
        (keep, proj, proj_gate, bias, gain, states, back, coupling),
    )


def finish_backward(info, keep, ends, prod, grad, proj, bias, states, enter, deps=()):
    _, half, own = prod.shape
    parts = ends.shape[0]

    def body(info_ref, keep_ref, ends_ref, prod_ref, grad_ref, proj_ref, bias_ref, states_ref, enter_ref, out_ref, sum_ref):
        entering = entering_state(info_ref, ends_ref, parts, True, True)
        first = lax.broadcasted_iota(jnp.int32, (half, LANE), 0) == 0
        bias_sum = jnp.zeros((1, LANE), F32)
        for owner in range(GRP):
            before = enter_ref[owner : owner + 1, :]
            for part in range(2):
                slot = 2 * owner + part
                states = states_ref[slot]
                previous = jnp.where(first, before, pltpu.roll(states, 1, 0))
                before = states[half - 1 :]
                total = grad_ref[slot] + prod_ref[slot] * entering[owner : owner + 1]
                enter = proj_ref[slot, :, :LANE]
                sig = jax.nn.sigmoid(proj_ref[slot, :, LANE:] + bias_ref[...])
                enter_sig = jax.nn.sigmoid(enter)
                grad_forget = total * (previous * keep_ref[slot] - enter * enter_sig)
                grad_proj = grad_forget * ((1.0 - LOWER) * sig * (1.0 - sig))
                forget = LOWER + (1.0 - LOWER) * sig
                out_ref[slot, :, :LANE] = (
                    total * (1.0 - forget) * (enter_sig * (1.0 + enter * (1.0 - enter_sig)))
                ).astype(BF16)
                out_ref[slot, :, LANE:] = grad_proj.astype(BF16)
                bias_sum = bias_sum + jnp.sum(grad_proj, axis=0, keepdims=True)
        sum_ref[...] = bias_sum

    block = pl.BlockSpec((8, half, LANE), lambda j: (0, 0, j))
    pair = pl.BlockSpec((8, half, 2 * LANE), lambda j: (0, 0, j))
    vector = pl.BlockSpec((1, LANE), lambda j: (0, j))
    return call(
        body,
        "finish_backward",
        (own // LANE,),
        [
            SMEM,
            pl.BlockSpec((8, half, LANE), lambda j: (0, 0, 0)),
            pl.BlockSpec((parts, 2 * GRP, LANE), lambda j: (0, 0, j)),
            block,
            block,
            pair,
            vector,
            block,
            pl.BlockSpec((GRP, LANE), lambda j: (0, j)),
        ],
        [pair, vector],
        [shape((8, half, 2 * own), BF16), shape((1, own), F32)],
        (info, keep, ends, prod, grad, proj, bias, states, enter),
        deps,
    )


def place_rows(mine, pieces, deps=()):
    rows, wide = pieces[0].shape
    if rows % 16:
        pieces = lay(pieces, deps).reshape(GRP, rows, wide)

        def from_laid(mine_ref, pieces_ref, out_ref):
            out_ref[0] = pieces_ref[mine_ref[0] ^ pl.program_id(0)].astype(F32)

        return call(
            from_laid,
            "place_rows",
            (GRP,),
            [SMEM, whole_block(pieces)],
            pl.BlockSpec((1, rows, wide), lambda j: (j, 0, 0)),
            shape((GRP, rows, wide), F32),
            (mine.reshape(1), pieces),
        ).reshape(GRP * rows, wide)

    step = math.gcd(rows, pieces[3].shape[0])
    tops = pieces[3].shape[0] // step

    def body(mine_ref, *refs):
        out_ref, held_ref = refs[5:]
        collect(refs, held_ref, 0, tops)
        for which in range(GRP):
            out_ref[which] = held_ref[mine_ref[0] ^ which].astype(F32)

    return call(
        body,
        "place_rows",
        (rows // step,),
        [SMEM] + piece_blocks(pieces, step, wide),
        pl.BlockSpec((GRP, step, wide), lambda i: (0, i, 0)),
        shape((GRP, rows, wide), F32),
        (mine.reshape(1),) + tuple(pieces),
        deps,
        [pltpu.VMEM((GRP, step, wide), BF16)],
    ).reshape(GRP * rows, wide)


def place_stacked(mine, pieces, first, own, deps=()):
    rows = pieces[0].shape[0]
    count = rows // GRP
    tops = pieces[3].shape[0] // count

    def body(mine_ref, *refs):
        out_ref, held_ref = refs[5:]
        collect(refs, held_ref, 0, tops)
        for which in range(GRP):
            out_ref[which * count : (which + 1) * count, :] = held_ref[mine_ref[0] ^ which].astype(F32)

    return call(
        body,
        "place_stacked",
        (GRP,),
        [SMEM] + piece_blocks(pieces, count, own, lambda i: first // own),
        pl.BlockSpec((rows, own), lambda j: (0, j)),
        shape((rows, GRP * own), F32),
        (mine.reshape(1),) + tuple(pieces),
        deps,
        [pltpu.VMEM((GRP, count, own), BF16)],
    )


def on_device(
    tokens,
    seq_lengths,
    cotangent,
    norm_gain,
    input_proj,
    forget_proj,
    forget_bias,
    gate_proj,
    state_gain,
    out_proj,
    mlp_gain,
    mlp_gate,
    mlp_up,
    mlp_down,
):
    tok_rows, width = tokens.shape
    half = tok_rows // 2
    plane = GRP * tok_rows
    parts = lax.axis_size("seq")
    mine, place = lax.axis_index("grp"), lax.axis_index("seq")
    own = width // GRP

    def own_rows(matrix):
        count = matrix.shape[0] // GRP
        return lax.dynamic_slice_in_dim(matrix, mine * count, count, 0)

    def own_features(vector):
        cut = vector.reshape(parts, GRP, -1)
        return lax.dynamic_index_in_dim(cut, mine, 1, False).reshape(1, -1)

    def all_features(vector):
        cut = vector.reshape(parts, 1, -1)
        spread = jnp.where(jnp.arange(GRP)[None, :, None] == mine, cut, 0.0)
        return spread.reshape(-1)

    def whole(rows):
        return lax.all_gather(rows, "seq", axis=0, tiled=True)

    def reduced(grads):
        return lax.psum_scatter(grads, "seq", scatter_dimension=0, tiled=True)

    starts = (jnp.cumsum(seq_lengths[0]) - seq_lengths[0]).astype(jnp.int32)
    starts = jnp.concatenate([(place * tok_rows).reshape(1).astype(jnp.int32), starts])
    info = place.reshape(1).astype(jnp.int32)
    bias = own_features(forget_bias)
    gain = own_features(state_gain)
    in_gain, mid_gain = norm_gain.reshape(1, -1), mlp_gain.reshape(1, -1)

    w_first = whole(pick_first(mine, input_proj, forget_proj, gate_proj, out_proj, parts))
    normed = norm_in(tokens, starts, in_gain, width)
    cot_held = start_gather(cotangent)
    held = start_gather(normed)
    ff_cols = pick_columns(mine, (mlp_gate, mlp_up), parts, True, (normed,))
    w_ff = whole(ff_cols)
    w_down = whole(own_rows(mlp_down))
    normed = end_gather(held, (ff_cols,))
    cot_pieces = second_step(cot_held)
    keep = normed[:, width:].astype(F32).reshape(8, half, LANE)

    proj = product("proj_pair", normed, w_first, width, 0, 2 * own, 256, cot_pieces).reshape(
        8, half, 2 * own
    )
    prod, state, ends = scan_forward(keep, proj, bias)
    ends, _ = all_ends(ends, parts)
    proj_gate = product("proj_gate", normed, w_first, width, 2 * own, own, 256, (prod,))
    proj_gate = proj_gate.reshape(8, half, own)
    states, mix, squares, enter = finish_forward(info, ends, prod, state, proj_gate, gain)
    mix, squares = mix.reshape(plane, own), squares.reshape(plane, LANE)
    w_stacked = w_first.reshape(parts, -1, 4 * own)
    to_x, to_y, kept = partial_sums(
        "mix", NN, (mix,), (w_stacked,), own, squares, stacked=(width, parts, 3 * own)
    )
    by_x, by_y = send_x(to_x), send_y(to_y)
    w_out = take_out(w_stacked, parts, own, (to_x,))
    cot = lay(cot_pieces, (w_out,))
    for_y, for_x = merge("mix_merge", kept, by_x, by_y, squares, (cot,))
    pieces = (kept, by_x, by_y, send_y(for_y), send_x(for_x), squares)
    middle, normed_mid, raw, scale_state, scale_mid = finish_mix(pieces, tokens, mid_gain, width)
    normed_mid = gather_rows(normed_mid)
    hidden, by_gate, by_up = feed_forward(normed_mid, w_ff)
    part_down = outer_sum("part_down", hidden, cot, hidden.shape[1], width, -512)
    sum_down = reduced(part_down)

    to_x, to_y, kept_out = partial_sums("down", NN, (hidden,), (w_down,), 256, deps=(part_down,))
    by_x_out, by_y_out = send_x(to_x), send_y(to_y)
    grad_ff = feed_back(cot, w_down, by_gate, by_up, (to_x,))
    to_x, to_y, kept = partial_sums("grad_mid", NT, (grad_ff,), (w_ff,), 256)
    by_x, by_y = send_x(to_x), send_y(to_y)
    part_ff = outer_sum("part_ff", normed_mid, grad_ff, width, grad_ff.shape[1], 256, (to_x,))
    sum_ff = reduced(part_ff)
    out_for_y, out_for_x = merge("down_merge", kept_out, by_x_out, by_y_out, None, (part_ff,))
    out_last_y, out_last_x = send_y(out_for_y), send_x(out_for_x)
    pieces_out = (kept_out, by_x_out, by_y_out, out_last_y, out_last_x)
    for_y, for_x = merge("grad_mid_merge", kept, by_x, by_y, deps=(out_for_y,))
    block_out = add_scattered(pieces_out, middle, BF16, width, (for_y,))
    pieces = (kept, by_x, by_y, send_y(for_y), send_x(for_x))
    grad_middle, scaled_mix, grad_mlp_gain = finish_mid(
        pieces,
        middle,
        cotangent,
        raw,
        scale_state,
        scale_mid,
        mid_gain,
        width,
        (block_out,),
    )
    held = start_gather(scaled_mix)
    grad_mix = end_gather(held)
    held_down = start_gather(after(sum_down, grad_mix))
    back, coupling = product_back("back", grad_mix, w_out, 256)
    after_prod, local, ends_back, grad_gate, gain_sum = scan_backward(
        keep,
        proj,
        proj_gate,
        bias,
        gain,
        states,
        back.reshape(8, half, own),
        coupling.reshape(8, half, LANE),
    )
    grad_gate = grad_gate.reshape(plane, own)
    part_gate_out, _ = outer_gate_out(
        normed,
        grad_gate,
        mix,
        grad_mix,
        parts,
        width,
        (after_prod,),
        lambda deps: (held_down[1], held_down[2]),
    )
    sum_gate_out = reduced(part_gate_out)
    ends_back = lax.all_gather(after(ends_back, part_gate_out), "seq")
    grad_pair, bias_sum = finish_backward(
        info, keep, ends_back, after_prod, local, proj, bias, states, enter, (part_gate_out,)
    )
    grad_pair = grad_pair.reshape(plane, 2 * own)
    held_ff = start_gather(after(sum_ff, part_gate_out))
    to_x, to_y, kept = partial_sums(
        "grad_in", NT, (grad_pair, grad_gate), (w_first, w_first), 256, firsts=(0, 2 * own)
    )
    by_x, by_y = send_x(to_x), send_y(to_y)
    down_pieces = second_step(held_down)
    part_pair = outer_sum(
        "part_pair", normed, grad_pair, width, 2 * own, 256, (to_x,) + down_pieces[3:] + held_ff[1:]
    )
    sum_pair = reduced(part_pair)
    grad_down = place_rows(mine, down_pieces, (part_pair, held_ff[1], held_ff[2]))
    for_y, for_x = merge("grad_in_merge", kept, by_x, by_y, deps=(grad_down,))
    last_y, last_x = send_y(for_y), send_x(for_x)
    pieces = (kept, by_x, by_y, last_y, last_x)
    held_go = start_gather(after(sum_gate_out, pieces[3], pieces[4]))
    ff_pieces = second_step(held_ff)
    grad_tokens, grad_norm_gain = finish_in(
        pieces, tokens, grad_middle, in_gain, width, ff_pieces[3:]
    )
    vectors = sum_everywhere(
        jnp.stack(
            [grad_norm_gain[0], all_features(bias_sum), all_features(gain_sum), grad_mlp_gain[0]]
        )
    )
    held_pair = start_gather(after(sum_pair, grad_tokens))
    grad_mlp_gate, grad_mlp_up = place_columns(
        mine, ff_pieces, parts, 2, w_ff.shape[1] // 2, True, (grad_tokens,)
    )
    gate_out_pieces = second_step(held_go, (grad_mlp_up,))
    (grad_gate_proj,) = place_columns(
        mine, gate_out_pieces, parts, 1, own, True, (grad_mlp_up,)
    )
    grad_out = place_stacked(mine, gate_out_pieces, own, own, (grad_gate_proj,))
    grad_input, grad_forget = place_columns(
        mine, second_step(held_pair, (grad_mlp_up,)), parts, 2, own, True, (grad_out,)
    )
    vectors = sum(after(vectors, grad_input))
    return (
        block_out,
        grad_tokens,
        vectors[0],
        grad_input,
        grad_forget,
        vectors[1],
        grad_gate_proj,
        vectors[2],
        grad_out,
        vectors[3],
        grad_mlp_gate,
        grad_mlp_up,
        grad_down,
    )


def solution(mesh):
    rows = P("seq", None)
    tokens = P(("grp", "seq"), None)
    return jax.shard_map(
        on_device,
        mesh=mesh,
        in_specs=(
            tokens,
            P("grp", None),
            tokens,
            P(),
            rows,
            rows,
            P(),
            rows,
            P(),
            rows,
            P(),
            rows,
            rows,
            rows,
        ),
        out_specs=(
            tokens,
            tokens,
            P(),
            rows,
            rows,
            P(),
            rows,
            P(),
            rows,
            P(),
            rows,
            rows,
            rows,
        ),
        check_vma=False,
    )
```

```python
import math
from functools import partial

import jax
import jax.numpy as jnp
from jax import lax
from jax.experimental import pallas as pl
from jax.experimental.pallas import tpu as pltpu
from jax.sharding import PartitionSpec as P

LOWER = 0.9
EPSILON = 1e-06
GRP = 4
LANE = 128
ROWS = 8
F32 = jnp.float32
BF16 = jnp.bfloat16
SWAP_X = [(0, 1), (1, 0), (2, 3), (3, 2)]
SWAP_Y = [(0, 2), (2, 0), (1, 3), (3, 1)]
TO_X, TO_Y, KEPT = (2, 6), (5, 7), (0, 1, 3, 4)
VMEM_LIMIT = 56 * 1024 * 1024
PLACE_STEP = 64
NN = (((1,), (0,)), ((), ()))
NT = (((1,), (1,)), ((), ()))
TN = (((0,), (0,)), ((), ()))
COSTS = {"finish_in": 73, "finish_mid": 210}
SMALL = pl.CostEstimate(flops=1024, bytes_accessed=1024, transcendentals=0)
ANY = pl.BlockSpec(memory_space=pl.ANY)
SMEM = pl.BlockSpec(memory_space=pltpu.SMEM)


def dot(lhs_arr, rhs_arr, dims):
    return lax.dot_general(lhs_arr, rhs_arr, dims, preferred_element_type=F32)


def call(body, name, grid, in_specs, out_specs, out_shape, args, deps=(), scratch=(), aliases=None):
    n_in, n_deps = len(in_specs), len(deps)

    def wrapped(*refs):
        body(*refs[:n_in], *refs[n_in + n_deps :])

    return pl.pallas_call(
        wrapped,
        grid=grid,
        in_specs=list(in_specs) + [ANY] * n_deps,
        out_specs=out_specs,
        out_shape=out_shape,
        scratch_shapes=list(scratch),
        compiler_params=pltpu.CompilerParams(vmem_limit_bytes=VMEM_LIMIT),
        input_output_aliases=aliases or {},
        cost_estimate=pl.CostEstimate(
            flops=1024 + COSTS.get(name, 0) * 1_000_000_000, bytes_accessed=1024, transcendentals=0
        ),
        name=name,
    )(*args, *deps)


def shape(dims, dtype):
    return jax.ShapeDtypeStruct(tuple(dims), dtype)


def whole_block(array):
    return pl.BlockSpec(array.shape, lambda *i: (0,) * len(array.shape))


def product(name, lhs_arr, rhs_arr, depth, first, wide, step, deps=()):
    rows = lhs_arr.shape[0]

    def body(lhs_ref, rhs_ref, out_ref):
        out_ref[...] = dot(lhs_ref[...], rhs_ref[...], NN)

    return call(
        body,
        name,
        (wide // step,),
        [
            pl.BlockSpec((rows, depth), lambda j: (0, 0)),
            pl.BlockSpec((depth, step), lambda j: (0, first // step + j)),
        ],
        pl.BlockSpec((rows, step), lambda j: (0, j)),
        shape((rows, wide), F32),
        (lhs_arr, rhs_arr),
        deps,
    )


def product_back(name, lhs_arr, rhs_arr, step, deps=()):
    rows = lhs_arr.shape[0]
    wide, depth = rhs_arr.shape

    def body(lhs_ref, rest_ref, rhs_ref, out_ref, sum_ref):
        out_ref[...] = dot(lhs_ref[...], rhs_ref[...], NT)

        @pl.when(pl.program_id(0) == 0)
        def _():
            sum_ref[...] = jnp.broadcast_to(join(rest_ref[...]), (rows, LANE))

    return call(
        body,
        name,
        (wide // step,),
        [
            pl.BlockSpec((rows, depth), lambda j: (0, 0)),
            pl.BlockSpec((rows, LANE), lambda j: (0, depth // LANE)),
            pl.BlockSpec((step, depth), lambda j: (j, 0)),
        ],
        [pl.BlockSpec((rows, step), lambda j: (0, j)), pl.BlockSpec((rows, LANE), lambda j: (0, 0))],
        [shape((rows, wide), F32), shape((rows, LANE), F32)],
        (lhs_arr, lhs_arr, rhs_arr),
        deps,
    )


def outer_sum(name, lhs_arr, rhs_arr, rows, wide, step, deps=()):
    depth = lhs_arr.shape[0]
    by_rows = step > 0
    step = abs(step)

    def body(lhs_ref, rhs_ref, out_ref):
        out_ref[...] = dot(lhs_ref[...], rhs_ref[...], TN).astype(BF16)

    if by_rows:
        grid = (rows // step,)
        specs = [
            pl.BlockSpec((depth, step), lambda j: (0, j)),
            pl.BlockSpec((depth, wide), lambda j: (0, 0)),
        ]
        out_spec = pl.BlockSpec((step, wide), lambda j: (j, 0))
    else:
        grid = (wide // step,)
        specs = [
            pl.BlockSpec((depth, rows), lambda j: (0, 0)),
            pl.BlockSpec((depth, step), lambda j: (0, j)),
        ]
        out_spec = pl.BlockSpec((rows, step), lambda j: (0, j))
    return call(body, name, grid, specs, out_spec, shape((rows, wide), BF16), (lhs_arr, rhs_arr), deps)


def outer_gate_out(normed, grad_gate, mix, grad_mix, parts, wide, deps, between):
    depth, own = mix.shape
    count = own // parts
    turns = wide // own

    def right(lhs_ref, rhs_ref, out_ref):
        out_ref[...] = dot(lhs_ref[...], rhs_ref[...], TN).astype(BF16).reshape(parts, count, own)

    half_done = call(
        right,
        "part_out",
        (turns,),
        [
            pl.BlockSpec((depth, own), lambda j: (0, 0)),
            pl.BlockSpec((depth, own), lambda j: (0, j)),
        ],
        pl.BlockSpec((parts, count, own), lambda j: (0, j, 1)),
        shape((parts, turns * count, 2 * own), BF16),
        (mix, grad_mix),
        deps,
    ).reshape(wide, 2 * own)

    middle = between((half_done,))

    def left(lhs_ref, rhs_ref, _, out_ref):
        out_ref[...] = dot(lhs_ref[...], rhs_ref[...], TN).astype(BF16)

    return call(
        left,
        "part_gate",
        (turns,),
        [
            pl.BlockSpec((depth, own), lambda j: (0, j)),
            pl.BlockSpec((depth, own), lambda j: (0, 0)),
            ANY,
        ],
        pl.BlockSpec((own, own), lambda j: (j, 0)),
        shape((wide, 2 * own), BF16),
        (normed, grad_gate, half_done),
        middle,
        aliases={2: 0},
    ), middle


def after(value, *events):
    return lax.optimization_barrier((value, events))[0]


def send_x(value):
    return lax.ppermute(value, "grp", SWAP_X)


def send_y(value):
    return lax.ppermute(value, "grp", SWAP_Y)


def lay(pieces, deps=()):
    if any(piece.shape[0] % 16 for piece in pieces):
        return jnp.concatenate(pieces)
    wide = pieces[0].shape[1]
    at = [0]
    for piece in pieces:
        at.append(at[-1] + piece.shape[0])
    deps = tuple(deps)

    def body(*refs):
        out_ref, sems = refs[-2], refs[-1]
        copies = [
            pltpu.make_async_copy(
                ref, out_ref.at[pl.ds(at[index], pieces[index].shape[0])], sems.at[index]
            )
            for index, ref in enumerate(refs[: len(pieces)])
        ]
        for copy in copies:
            copy.start()
        for copy in copies:
            copy.wait()

    return call(
        body,
        "lay",
        (),
        [pl.BlockSpec(memory_space=pltpu.VMEM)] * len(pieces),
        ANY,
        shape((at[-1], wide), pieces[0].dtype),
        tuple(pieces),
        deps,
        [pltpu.SemaphoreType.DMA((len(pieces),))],
    )


def start_gather(own):
    return own, send_x(own), send_y(own)


def second_step(held, hold=()):
    own, by_x, by_y = held
    half = own.shape[0] // 2 if own.shape[0] % 16 else (own.shape[0] + 16) // 32 * 16
    x_on, y_on = by_x[:half], by_y[half:]
    if hold:
        x_on, y_on = after((x_on, y_on), hold)
    return own, by_x, by_y, send_y(x_on), send_x(y_on)


def end_gather(held, deps=(), hold=()):
    return lay(second_step(held, hold), deps)


def gather_rows(own, deps=(), hold=()):
    return end_gather(start_gather(own), deps, hold)


def sum_everywhere(value):
    count = lax.axis_size("seq")
    if count > 8:
        step = 1
        while step < count:
            value = value + lax.ppermute(value, "seq", [(one, one ^ step) for one in range(count)])
            step *= 2
    else:
        value = value + lax.ppermute(value, "seq", [(one, one ^ 1) for one in range(count)])
        value = value + sum(
            lax.ppermute(value, "seq", [(one, (one + step) % count) for one in range(count)])
            for step in range(2, count, 2)
        )
    across = lax.ppermute(value, "grp", [(one, 3 - one) for one in range(GRP)])
    return value, send_x(value), send_y(value), across


def split(column):
    high = column.astype(BF16).astype(F32)
    rest = column - high
    middle = rest.astype(BF16).astype(F32)
    lane = lax.broadcasted_iota(jnp.int32, column.shape, 1)
    zero = jnp.zeros_like(column)
    picked = jnp.where(lane == 0, high, jnp.where(lane == 1, middle, jnp.where(lane == 2, rest - middle, zero)))
    return picked.astype(BF16)


def join(block):
    return jnp.sum(block.astype(F32), axis=1, keepdims=True)


def partial_sums(name, dims, rows, weights, step, column=None, deps=(), stacked=None, firsts=(0, 0)):
    half = rows[0].shape[0] // 8
    pairs = len(rows)
    if stacked is not None:
        wide, parts, first = stacked
        own = rows[0].shape[1]
        specs = [pl.BlockSpec((parts, own // parts, step), lambda j: (0, j, first // step))]
    elif dims is NN:
        wide = weights[0].shape[1]
        specs = [pl.BlockSpec((one.shape[1], step), lambda j: (0, j)) for one in rows]
    else:
        wide = weights[0].shape[0]
        specs = [
            pl.BlockSpec((step, one.shape[1]), lambda j, at=at // one.shape[1]: (j, at))
            for one, at in zip(rows, firsts)
        ]
    extra = 0 if column is None else LANE
    columns = () if column is None else (column,)

    def pick(value, slots):
        return jnp.concatenate([value[slot * half : (slot + 1) * half] for slot in slots])

    def body(*refs):
        x_ref, y_ref, kept_ref = refs[-3:]
        at = pl.ds(pl.multiple_of(pl.program_id(0) * step, LANE), step)
        sums = None
        for rows_ref, weights_ref in zip(refs[:pairs], refs[pairs : 2 * pairs]):
            block = weights_ref[...]
            if stacked is not None:
                block = block.reshape(own, step)
            term = dot(rows_ref[...], block, dims)
            sums = term if sums is None else sums + term
        x_ref[:, at] = pick(sums, TO_X).astype(BF16)
        y_ref[:, at] = pick(sums, TO_Y).astype(BF16)
        kept_ref[...] = pick(sums, KEPT)
        if column is not None:

            @pl.when(pl.program_id(0) == 0)
            def _():
                x_ref[:, wide:] = split(pick(refs[-4], TO_X))
                y_ref[:, wide:] = split(pick(refs[-4], TO_Y))

    sent = shape((2 * half, wide + extra), BF16)
    return call(
        body,
        name,
        (wide // step,),
        [whole_block(one) for one in rows] + specs + [whole_block(one) for one in columns],
        [whole_block(sent), whole_block(sent), pl.BlockSpec((4 * half, step), lambda j: (0, j))],
        [sent, sent, shape((4 * half, wide), F32)],
        tuple(rows) + tuple(weights) + columns,
        deps,
    )


def merge(name, kept, by_x, by_y, column=None, deps=()):
    half = kept.shape[0] // 4
    wide = kept.shape[1]
    extra = 0 if column is None else LANE
    columns = () if column is None else (column,)

    def body(kept_ref, by_x_ref, by_y_ref, *refs):
        for_y_ref, for_x_ref = refs[-2:]
        for_y_ref[:, :wide] = (kept_ref[half:, :] + by_x_ref[:, :wide].astype(F32)).astype(BF16)
        for_x_ref[:, :wide] = (kept_ref[:half, :] + by_y_ref[:, :wide].astype(F32)).astype(BF16)
        if column is not None:
            for_y_ref[:, wide:] = split(refs[0][4 * half : 5 * half] + join(by_x_ref[:, wide:]))
            for_x_ref[:, wide:] = split(refs[0][3 * half : 4 * half] + join(by_y_ref[:, wide:]))

    again = shape((half, wide + extra), BF16)
    return call(
        body,
        name,
        (1,),
        [
            pl.BlockSpec((2 * half, wide), lambda j: (1, 0)),
            pl.BlockSpec((half, wide + extra), lambda j: (1, 0)),
            pl.BlockSpec((half, wide + extra), lambda j: (1, 0)),
        ]
        + [whole_block(one) for one in columns],
        [whole_block(again), whole_block(again)],
        [again, again],
        (kept, by_x, by_y) + columns,
        deps,
    )


def scattered_specs(pieces, step, turn=None):
    kept, by_x, by_y, last_y, last_x = pieces[:5]
    half = last_y.shape[0]
    count = half // step
    wide = by_x.shape[1]
    received = pl.BlockSpec((step, wide), lambda h, i: (i, 0))
    specs = [
        pl.BlockSpec((step, kept.shape[1]), lambda h, i: (h * count + i, 0)),
        received,
        received,
        received,
        received,
    ]
    if len(pieces) > 5:
        specs.append(pl.BlockSpec((step, LANE), lambda h, i: (h * count + i, 0)))
    return specs


def scattered_sum(refs, wide):
    top = pl.program_id(0) == 0
    first = jnp.where(top, refs[1][...].astype(F32), refs[2][...].astype(F32))
    second = jnp.where(top, refs[3][...].astype(F32), refs[4][...].astype(F32))
    came = first + second
    total = refs[0][...] + came[:, :wide]
    if len(refs) == 5:
        return total, None
    return total, refs[5][:, :1] + jnp.sum(came[:, wide:], axis=1, keepdims=True)


def own_block(step, count, wide):
    return pl.BlockSpec((step, wide), lambda h, i: (h * count + i, 0))


def finish_mix(pieces, tokens, gain, width):
    rows = tokens.shape[0]
    half = rows // 2
    step = min(half, 64)
    count = half // step

    def body(*refs):
        tokens_ref, gain_ref, middle_ref, normed_ref, raw_ref, scale_ref, scale_mid_ref = refs[-7:]
        raw, squares = scattered_sum(refs[:-7], width)
        scale = lax.rsqrt(squares / width + EPSILON)
        middle = tokens_ref[...].astype(F32) + raw * scale
        scale_mid = lax.rsqrt(jnp.mean(middle * middle, axis=1, keepdims=True) + EPSILON)
        middle_ref[...] = middle
        raw_ref[...] = raw
        normed_ref[...] = (middle * scale_mid * gain_ref[...]).astype(BF16)
        scale_ref[...] = scale
        scale_mid_ref[...] = scale_mid

    block = own_block(step, count, width)
    thin = own_block(step, count, 1)
    return call(
        body,
        "finish_mix",
        (2, count),
        scattered_specs(pieces, step) + [block, pl.BlockSpec((1, width), lambda h, i: (0, 0))],
        [block, block, block, thin, thin],
        [
            shape((rows, width), F32),
            shape((rows, width), BF16),
            shape((rows, width), F32),
            shape((rows, 1), F32),
            shape((rows, 1), F32),
        ],
        tuple(pieces) + (tokens, gain),
    )


def add_scattered(pieces, middle, out, width, deps=()):
    rows = middle.shape[0]
    half = rows // 2
    step = min(half, 64)
    count = half // step

    def body(*refs):
        middle_ref, out_ref = refs[-2:]
        out_ref[...] = (middle_ref[...] + scattered_sum(refs[:-2], width)[0]).astype(out)

    block = own_block(step, count, width)
    return call(
        body,
        "add_scattered",
        (2, count),
        scattered_specs(pieces, step) + [block],
        block,
        shape((rows, width), out),
        tuple(pieces) + (middle,),
        deps,
    )


def norm_back(values, scale, gain, grad):
    weighted = values * grad
    inner = jnp.mean(weighted * gain, axis=1, keepdims=True)
    back = scale * gain * grad - values * (scale * scale * scale * inner)
    return back, jnp.sum(weighted * scale, axis=0, keepdims=True)


def finish_mid(pieces, middle, cotangent, raw, scale, scale_mid, gain, width, deps=()):
    rows = middle.shape[0]
    half = rows // 2
    step = min(half, 64)
    count = half // step

    def body(*refs):
        middle_ref, cot_ref, raw_ref, scale_ref, scale_mid_ref, gain_ref, grad_ref, send_ref, sum_ref = refs[-9:]
        grad, _ = scattered_sum(refs[:-9], width)
        back, gain_part = norm_back(middle_ref[...], scale_mid_ref[...], gain_ref[...], grad)
        grad_middle = cot_ref[...].astype(F32) + back
        scale = scale_ref[...]
        coupling = scale * scale * scale * jnp.mean(raw_ref[...] * grad_middle, axis=1, keepdims=True)
        grad_ref[...] = grad_middle
        send_ref[:, :width] = (grad_middle * scale).astype(BF16)
        send_ref[:, width:] = split(jnp.broadcast_to(coupling, (step, LANE)))

        @pl.when((pl.program_id(0) == 0) & (pl.program_id(1) == 0))
        def _():
            sum_ref[...] = jnp.zeros_like(sum_ref)

        sum_ref[...] += gain_part

    block = own_block(step, count, width)
    thin = own_block(step, count, 1)
    row = pl.BlockSpec((1, width), lambda h, i: (0, 0))
    return call(
        body,
        "finish_mid",
        (2, count),
        scattered_specs(pieces, step) + [block, block, block, thin, thin, row],
        [block, own_block(step, count, width + LANE), row],
        [shape((rows, width), F32), shape((rows, width + LANE), BF16), shape((1, width), F32)],
        tuple(pieces) + (middle, cotangent, raw, scale, scale_mid, gain),
        deps,
    )


def finish_in(pieces, tokens, grad_middle, gain, width, deps=()):
    rows = tokens.shape[0]
    half = rows // 2
    step = min(half, 64)
    count = half // step

    def body(*refs):
        tokens_ref, middle_ref, gain_ref, out_ref, sum_ref = refs[-5:]
        grad, _ = scattered_sum(refs[:-5], width)
        values = tokens_ref[...].astype(F32)
        scale = lax.rsqrt(jnp.mean(values * values, axis=1, keepdims=True) + EPSILON)
        back, gain_part = norm_back(values, scale, gain_ref[...], grad)
        out_ref[...] = middle_ref[...] + back

        @pl.when((pl.program_id(0) == 0) & (pl.program_id(1) == 0))
        def _():
            sum_ref[...] = jnp.zeros_like(sum_ref)

        sum_ref[...] += gain_part

    block = own_block(step, count, width)
    row = pl.BlockSpec((1, width), lambda h, i: (0, 0))
    return call(
        body,
        "finish_in",
        (2, count),
        scattered_specs(pieces, step) + [block, block, row],
        [block, row],
        [shape((rows, width), F32), shape((1, width), F32)],
        tuple(pieces) + (tokens, grad_middle, gain),
        deps,
    )


def norm_in(tokens, starts, gain, width):
    rows = tokens.shape[0]
    step = min(rows, 64)

    def body(starts_ref, tokens_ref, gain_ref, out_ref):
        values = tokens_ref[...].astype(F32)
        scale = lax.rsqrt(jnp.mean(values * values, axis=1, keepdims=True) + EPSILON)
        out_ref[:, :width] = (values * scale * gain_ref[...]).astype(BF16)
        here = starts_ref[0] + pl.program_id(0) * step
        here = here + lax.broadcasted_iota(jnp.int32, (step, LANE), 0)
        keep = jnp.ones((step, LANE), F32)
        for one in range(1, starts.shape[0]):
            keep = jnp.where(here == starts_ref[one], 0.0, keep)
        out_ref[:, width:] = keep.astype(BF16)

    return call(
        body,
        "norm_in",
        (rows // step,),
        [SMEM, pl.BlockSpec((step, width), lambda i: (i, 0)), pl.BlockSpec((1, width), lambda i: (0, 0))],
        pl.BlockSpec((step, width + LANE), lambda i: (i, 0)),
        shape((rows, width + LANE), BF16),
        (starts, tokens, gain),
    )


def feed_forward(normed, weights, deps=()):
    rows, depth = normed.shape
    own = weights.shape[1] // 2

    def body(normed_ref, weights_ref, hidden_ref, by_gate_ref, by_up_ref):
        both = dot(normed_ref[...], weights_ref[...], NN)
        gate, up = both[:, :LANE], both[:, LANE:]
        sig = jax.nn.sigmoid(gate)
        act = gate * sig
        hidden_ref[...] = (act * up).astype(BF16)
        by_gate_ref[...] = up * (sig * (1.0 + gate * (1.0 - sig)))
        by_up_ref[...] = act

    block = pl.BlockSpec((rows, LANE), lambda j: (0, j))
    return call(
        body,
        "feed_forward",
        (own // LANE,),
        [whole_block(normed), pl.BlockSpec((depth, 2 * LANE), lambda j: (0, j))],
        [block, block, block],
        [shape((rows, own), BF16), shape((rows, own), F32), shape((rows, own), F32)],
        (normed, weights),
        deps,
    )


def feed_back(cot, weights, by_gate, by_up, deps=()):
    rows, depth = cot.shape
    own = weights.shape[0]
    step = min(rows, 256)

    def body(cot_ref, weights_ref, by_gate_ref, by_up_ref, out_ref):
        grad = dot(cot_ref[...], weights_ref[...], NT)
        for turn in range(own // LANE):
            part = slice(turn * LANE, (turn + 1) * LANE)
            out_ref[:, 2 * turn * LANE : (2 * turn + 1) * LANE] = (grad[:, part] * by_gate_ref[:, part]).astype(BF16)
            out_ref[:, (2 * turn + 1) * LANE : (2 * turn + 2) * LANE] = (grad[:, part] * by_up_ref[:, part]).astype(BF16)

    return call(
        body,
        "feed_back",
        (rows // step,),
        [
            pl.BlockSpec((step, depth), lambda j: (j, 0)),
            whole_block(weights),
            pl.BlockSpec((step, own), lambda j: (j, 0)),
            pl.BlockSpec((step, own), lambda j: (j, 0)),
        ],
        pl.BlockSpec((step, 2 * own), lambda j: (j, 0)),
        shape((rows, 2 * own), BF16),
        (cot, weights, by_gate, by_up),
        deps,
    )


def pick_columns(mine, matrices, parts, spread, deps=()):
    rows, wide = matrices[0].shape
    piece = wide // (GRP * parts)
    own = wide // GRP
    count = len(matrices)
    step = min(rows, 64)

    def body(mine_ref, *refs):
        out_ref = refs[-1]
        for index, ref in enumerate(refs[:-1]):
            for which in range(GRP):

                @pl.when(mine_ref[0] == which)
                def _(index=index, ref=ref, which=which):
                    whole = ref[...].astype(F32)
                    picked = jnp.concatenate(
                        [
                            whole[:, (part * GRP + which) * piece : (part * GRP + which + 1) * piece]
                            for part in range(parts)
                        ],
                        axis=1,
                    ).astype(BF16)
                    if not spread:
                        out_ref[:, index * own : (index + 1) * own] = picked
                    else:
                        for turn in range(own // LANE):
                            at = (turn * count + index) * LANE
                            out_ref[:, at : at + LANE] = picked[:, turn * LANE : (turn + 1) * LANE]

    return call(
        body,
        "pick_columns",
        (rows // step,),
        [SMEM] + [pl.BlockSpec((step, wide), lambda i: (i, 0))] * count,
        pl.BlockSpec((step, own * count), lambda i: (i, 0)),
        shape((rows, own * count), BF16),
        (mine.reshape(1),) + tuple(matrices),
        deps,
    )


def pick_first(mine, input_proj, forget_proj, gate_proj, out_proj, parts):
    rows, wide = input_proj.shape
    piece = wide // (GRP * parts)
    own = wide // GRP
    count = rows // GRP

    def body(mine_ref, input_ref, forget_ref, gate_ref, out_ref, first_ref):
        at = pl.ds(pl.multiple_of(mine_ref[0] * count, count), count)
        first_ref[:, 3 * own :] = out_ref[at, :]
        for which in range(GRP):

            @pl.when(mine_ref[0] == which)
            def _(which=which):
                for index, ref in enumerate((input_ref, forget_ref, gate_ref)):
                    picked = jnp.concatenate(
                        [
                            ref[:, (part * GRP + which) * piece : (part * GRP + which + 1) * piece].astype(F32)
                            for part in range(parts)
                        ],
                        axis=1,
                    ).astype(BF16)
                    if index == 2:
                        first_ref[:, 2 * own : 3 * own] = picked
                        continue
                    for turn in range(own // LANE):
                        to = (2 * turn + index) * LANE
                        first_ref[:, to : to + LANE] = picked[:, turn * LANE : (turn + 1) * LANE]

    block = pl.BlockSpec((count, wide), lambda i: (i, 0))
    return call(
        body,
        "pick_first",
        (GRP,),
        [SMEM, block, block, block, pl.BlockSpec((rows, own), lambda i: (0, i))],
        pl.BlockSpec((count, 4 * own), lambda i: (i, 0)),
        shape((rows, 4 * own), BF16),
        (mine.reshape(1), input_proj, forget_proj, gate_proj, out_proj),
    )


def take_out(first, parts, own, deps=()):
    wide = GRP * own

    def body(first_ref, out_ref):
        out_ref[...] = first_ref[...].reshape(own, own)

    return call(
        body,
        "take_out",
        (GRP,),
        [pl.BlockSpec((parts, own // parts, own), lambda j: (0, j, 3))],
        pl.BlockSpec((own, own), lambda j: (0, j)),
        shape((own, wide), BF16),
        (first,),
        deps,
    )


def piece_blocks(pieces, step, wide, column=None):
    own, _, _, top, _ = pieces
    tops = top.shape[0] // step
    at = (lambda *i: 0) if column is None else (lambda *i: column(i[0]))
    block = pl.BlockSpec((step, wide), lambda *i: (i[-1], at(*i)))
    return [
        block,
        block,
        block,
        pl.BlockSpec((step, wide), lambda *i: (jnp.minimum(i[-1], tops - 1), at(*i))),
        pl.BlockSpec((step, wide), lambda *i: (jnp.maximum(i[-1] - tops, 0), at(*i))),
    ]


def collect(refs, held_ref, axis, tops):
    for index in range(3):
        held_ref[index] = refs[index][...]

    @pl.when(pl.program_id(axis) < tops)
    def _():
        held_ref[3] = refs[3][...]

    @pl.when(pl.program_id(axis) >= tops)
    def _():
        held_ref[3] = refs[4][...]


def place_columns(mine, pieces, parts, count, own, spread, deps=()):
    rows = pieces[0].shape[0]
    piece = own // parts
    step = min(pieces[3].shape[0], PLACE_STEP)
    tops = pieces[3].shape[0] // step

    def body(mine_ref, *refs):
        out_refs, held_ref = refs[5:-1], refs[-1]
        collect(refs, held_ref, 0, tops)
        for which in range(GRP):
            block = held_ref[mine_ref[0] ^ which].astype(F32)
            for index, out_ref in enumerate(out_refs):
                if spread:
                    turns = [
                        block[:, (turn * count + index) * LANE : (turn * count + index + 1) * LANE]
                        for turn in range(own // LANE)
                    ]
                    mat = jnp.concatenate(turns, axis=1)
                else:
                    mat = block[:, index * own : (index + 1) * own]
                for part in range(parts):
                    at = (part * GRP + which) * piece
                    out_ref[:, at : at + piece] = mat[:, part * piece : (part + 1) * piece]

    return call(
        body,
        "place_columns",
        (rows // step,),
        [SMEM] + piece_blocks(pieces, step, own * count),
        [pl.BlockSpec((step, own * GRP), lambda i: (i, 0))] * count,
        [shape((rows, own * GRP), F32)] * count,
        (mine.reshape(1),) + tuple(pieces),
        deps,
        [pltpu.VMEM((GRP, step, own * count), BF16)],
    )


def scan_forward(keep, proj, bias):
    _, half, wide = proj.shape
    own = wide // 2
    tiles = half // ROWS

    def body(keep_ref, proj_ref, bias_ref, prod_ref, state_ref, ends_ref):
        row = lax.broadcasted_iota(jnp.int32, (ROWS, LANE), 0)
        bias_row = bias_ref[...]

        def tile(part, step, carry):
            out = []
            for owner in range(GRP):
                slot = 2 * owner + part
                at = pl.ds(pl.multiple_of(step * ROWS, ROWS), ROWS)
                both = proj_ref[slot, at, :]
                enter = both[:, :LANE]
                forget = LOWER + (1.0 - LOWER) * jax.nn.sigmoid(both[:, LANE:] + bias_row)
                decay = forget * keep_ref[slot, at, :]
                income = enter * jax.nn.sigmoid(enter) * (1.0 - forget)
                for shift in (1, 2, 4):
                    fits = row >= shift
                    before = jnp.where(fits, pltpu.roll(income, shift, 0), 0.0)
                    factor = jnp.where(fits, pltpu.roll(decay, shift, 0), 1.0)
                    income = income + decay * before
                    decay = decay * factor
                prod, state = carry[owner]
                state_now = income + decay * state
                prod_now = decay * prod
                prod_ref[slot, at, :] = prod_now
                state_ref[slot, at, :] = state_now
                out.append((prod_now[ROWS - 1 :], state_now[ROWS - 1 :]))
            return tuple(out)

        carry = tuple(
            (jnp.ones((1, LANE), F32), jnp.zeros((1, LANE), F32)) for owner in range(GRP)
        )
        for part in range(2):
            carry = lax.fori_loop(0, tiles, partial(tile, part), carry)
        for owner in range(GRP):
            ends_ref[owner : owner + 1, :] = carry[owner][0]
            ends_ref[GRP + owner : GRP + owner + 1, :] = carry[owner][1]

    block = pl.BlockSpec((8, half, LANE), lambda j: (0, 0, j))
    return pl.pallas_call(
        body,
        grid=(own // LANE,),
        in_specs=[
            pl.BlockSpec((8, half, LANE), lambda j: (0, 0, 0)),
            pl.BlockSpec((8, half, 2 * LANE), lambda j: (0, 0, j)),
            pl.BlockSpec((1, LANE), lambda j: (0, j)),
        ],
        out_specs=[block, block, pl.BlockSpec((2 * GRP, LANE), lambda j: (0, j))],
        out_shape=[
            jax.ShapeDtypeStruct((8, half, own), F32),
            jax.ShapeDtypeStruct((8, half, own), F32),
            jax.ShapeDtypeStruct((2 * GRP, own), F32),
        ],
        compiler_params=pltpu.CompilerParams(vmem_limit_bytes=VMEM_LIMIT),
        cost_estimate=SMALL,
        name="scan_forward",
    )(keep, proj, bias)


def all_ends(ends, parts):
    if parts > 8:
        return lax.all_gather(ends, "seq"), ends
    even = lax.axis_index("seq") % 2 == 0
    other = lax.ppermute(ends, "seq", [(one, one ^ 1) for one in range(parts)])
    chip = jnp.concatenate([jnp.where(even, ends, other), jnp.where(even, other, ends)])
    chips = [chip] + [
        lax.ppermute(chip, "seq", [(one, (one + step) % parts) for one in range(parts)])
        for step in range(2, parts, 2)
    ]
    return jnp.concatenate(chips).reshape((parts,) + ends.shape), chip


def entering_state(info_ref, ends_ref, parts, backward, ordered):
    here = info_ref[0]
    steps = []
    if ordered or parts > 8:
        for place in range(parts - 1, 0, -1) if backward else range(parts - 1):
            steps.append((place, place > here if backward else place < here))
    else:
        chips, chip, core = parts // 2, here // 2, here % 2
        for away in range(chips - 1, 0, -1):
            at = chips - away if backward else away
            for one in (1, 0) if backward else (0, 1):
                steps.append((2 * at + one, chip + away < chips if backward else chip >= away))
        steps.append((1, core == 0) if backward else (0, core == 1))
    state = jnp.zeros((GRP, LANE), F32)
    for at, counts in steps:
        longer = ends_ref[at, GRP:, :] + ends_ref[at, :GRP, :] * state
        state = jnp.where(counts, longer, state)
    return state


def finish_forward(info, ends, prod, state, proj, gain, deps=()):
    _, half, own = prod.shape
    count = ends.shape[0]

    def body(info_ref, ends_ref, prod_ref, state_ref, proj_ref, gain_ref, states_ref, mix_ref, squares_ref, enter_ref):
        entering = entering_state(info_ref, ends_ref, count, False, False)
        enter_ref[...] = entering

        @pl.when(pl.program_id(0) == 0)
        def _():
            squares_ref[...] = jnp.zeros_like(squares_ref)

        for owner in range(GRP):
            for part in range(2):
                slot = 2 * owner + part
                states = state_ref[slot] + prod_ref[slot] * entering[owner : owner + 1]
                states_ref[slot] = states
                gate = proj_ref[slot]
                mix_ref[slot] = (states * gain_ref[...] * (gate * jax.nn.sigmoid(gate))).astype(BF16)
                squares_ref[slot] += states * states

        @pl.when(pl.program_id(0) == own // LANE - 1)
        def _():
            for slot in range(8):
                total = jnp.sum(squares_ref[slot], axis=1, keepdims=True)
                squares_ref[slot] = jnp.broadcast_to(total, (half, LANE))

    block = pl.BlockSpec((8, half, LANE), lambda j: (0, 0, j))
    return call(
        body,
        "finish_forward",
        (own // LANE,),
        [
            SMEM,
            pl.BlockSpec((count, 2 * GRP, LANE), lambda j: (0, 0, j)),
            block,
            block,
            block,
            pl.BlockSpec((1, LANE), lambda j: (0, j)),
        ],
        [
            block,
            block,
            pl.BlockSpec((8, half, LANE), lambda j: (0, 0, 0)),
            pl.BlockSpec((GRP, LANE), lambda j: (0, j)),
        ],
        [
            shape((8, half, own), F32),
            shape((8, half, own), BF16),
            shape((8, half, LANE), F32),
            shape((GRP, own), F32),
        ],
        (info, ends, prod, state, proj, gain),
        deps,
    )


def scan_backward(keep, proj, proj_gate, bias, gain, states, back, coupling):
    _, half, own = proj_gate.shape
    tiles = half // ROWS

    def body(
        keep_ref, proj_ref, gate_ref, bias_ref, gain_ref, states_ref, back_ref, coupling_ref,
        prod_ref, grad_ref, ends_ref, out_ref, sum_ref,
    ):
        row = lax.broadcasted_iota(jnp.int32, (ROWS, LANE), 0)
        bias_row = bias_ref[...]
        gain_row = gain_ref[...]

        def tile(part, turn, carry):
            step = tiles - 1 - turn
            out = []
            for owner in range(GRP):
                slot = 2 * owner + part
                at = pl.ds(pl.multiple_of(step * ROWS, ROWS), ROWS)
                gate = gate_ref[slot, at, :]
                forget = LOWER + (1.0 - LOWER) * jax.nn.sigmoid(proj_ref[slot, at, :] + bias_row)
                decay = forget * keep_ref[slot, at, :]
                direct = (
                    gain_row * (gate * jax.nn.sigmoid(gate)) * back_ref[slot, at, :]
                    - states_ref[slot, at, :] * coupling_ref[slot, at, :]
                )
                flow = decay * direct
                for shift in (1, 2, 4):
                    fits = row < ROWS - shift
                    later = jnp.where(fits, pltpu.roll(flow, ROWS - shift, 0), 0.0)
                    factor = jnp.where(fits, pltpu.roll(decay, ROWS - shift, 0), 1.0)
                    flow = flow + decay * later
                    decay = decay * factor
                prod, grad = carry[owner]
                flow = flow + decay * grad
                decay = decay * prod
                last = row == ROWS - 1
                grad_ref[slot, at, :] = direct + jnp.where(last, grad, pltpu.roll(flow, ROWS - 1, 0))
                prod_ref[slot, at, :] = jnp.where(last, prod, pltpu.roll(decay, ROWS - 1, 0))
                out.append((decay[:1], flow[:1]))
            return tuple(out)

        carry = tuple(
            (jnp.ones((1, LANE), F32), jnp.zeros((1, LANE), F32)) for owner in range(GRP)
        )
        for part in (1, 0):
            carry = lax.fori_loop(0, tiles, partial(tile, part), carry)
        for owner in range(GRP):
            ends_ref[owner : owner + 1, :] = carry[owner][0]
            ends_ref[GRP + owner : GRP + owner + 1, :] = carry[owner][1]
        gain_sum = jnp.zeros((1, LANE), F32)
        for slot in range(8):
            gate = gate_ref[slot]
            gate_sig = jax.nn.sigmoid(gate)
            pull = back_ref[slot] * states_ref[slot]
            out_ref[slot] = (pull * gain_row * (gate_sig * (1.0 + gate * (1.0 - gate_sig)))).astype(BF16)
            gain_sum = gain_sum + jnp.sum(pull * (gate * gate_sig), axis=0, keepdims=True)
        sum_ref[...] = gain_sum

    block = pl.BlockSpec((8, half, LANE), lambda j: (0, 0, j))
    vector = pl.BlockSpec((1, LANE), lambda j: (0, j))
    rows = pl.BlockSpec((8, half, LANE), lambda j: (0, 0, 0))
    return call(
        body,
        "scan_backward",
        (own // LANE,),
        [rows, pl.BlockSpec((8, half, LANE), lambda j: (0, 0, 2 * j + 1)), block, vector, vector, block, block, rows],
        [block, block, pl.BlockSpec((2 * GRP, LANE), lambda j: (0, j)), block, vector],
        [
            shape((8, half, own), F32),
            shape((8, half, own), F32),
            shape((2 * GRP, own), F32),
            shape((8, half, own), BF16),
            shape((1, own), F32),
        ],
        (keep, proj, proj_gate, bias, gain, states, back, coupling),
    )


def finish_backward(info, keep, ends, prod, grad, proj, bias, states, enter, deps=()):
    _, half, own = prod.shape
    parts = ends.shape[0]

    def body(info_ref, keep_ref, ends_ref, prod_ref, grad_ref, proj_ref, bias_ref, states_ref, enter_ref, out_ref, sum_ref):
        entering = entering_state(info_ref, ends_ref, parts, True, True)
        first = lax.broadcasted_iota(jnp.int32, (half, LANE), 0) == 0
        bias_sum = jnp.zeros((1, LANE), F32)
        for owner in range(GRP):
            before = enter_ref[owner : owner + 1, :]
            for part in range(2):
                slot = 2 * owner + part
                states = states_ref[slot]
                previous = jnp.where(first, before, pltpu.roll(states, 1, 0))
                before = states[half - 1 :]
                total = grad_ref[slot] + prod_ref[slot] * entering[owner : owner + 1]
                enter = proj_ref[slot, :, :LANE]
                sig = jax.nn.sigmoid(proj_ref[slot, :, LANE:] + bias_ref[...])
                enter_sig = jax.nn.sigmoid(enter)
                grad_forget = total * (previous * keep_ref[slot] - enter * enter_sig)
                grad_proj = grad_forget * ((1.0 - LOWER) * sig * (1.0 - sig))
                forget = LOWER + (1.0 - LOWER) * sig
                out_ref[slot, :, :LANE] = (
                    total * (1.0 - forget) * (enter_sig * (1.0 + enter * (1.0 - enter_sig)))
                ).astype(BF16)
                out_ref[slot, :, LANE:] = grad_proj.astype(BF16)
                bias_sum = bias_sum + jnp.sum(grad_proj, axis=0, keepdims=True)
        sum_ref[...] = bias_sum

    block = pl.BlockSpec((8, half, LANE), lambda j: (0, 0, j))
    pair = pl.BlockSpec((8, half, 2 * LANE), lambda j: (0, 0, j))
    vector = pl.BlockSpec((1, LANE), lambda j: (0, j))
    return call(
        body,
        "finish_backward",
        (own // LANE,),
        [
            SMEM,
            pl.BlockSpec((8, half, LANE), lambda j: (0, 0, 0)),
            pl.BlockSpec((parts, 2 * GRP, LANE), lambda j: (0, 0, j)),
            block,
            block,
            pair,
            vector,
            block,
            pl.BlockSpec((GRP, LANE), lambda j: (0, j)),
        ],
        [pair, vector],
        [shape((8, half, 2 * own), BF16), shape((1, own), F32)],
        (info, keep, ends, prod, grad, proj, bias, states, enter),
        deps,
    )


def place_rows(mine, pieces, deps=()):
    rows, wide = pieces[0].shape
    if rows % 16:
        pieces = lay(pieces, deps).reshape(GRP, rows, wide)

        def from_laid(mine_ref, pieces_ref, out_ref):
            out_ref[0] = pieces_ref[mine_ref[0] ^ pl.program_id(0)].astype(F32)

        return call(
            from_laid,
            "place_rows",
            (GRP,),
            [SMEM, whole_block(pieces)],
            pl.BlockSpec((1, rows, wide), lambda j: (j, 0, 0)),
            shape((GRP, rows, wide), F32),
            (mine.reshape(1), pieces),
        ).reshape(GRP * rows, wide)

    step = math.gcd(rows, pieces[3].shape[0])
    tops = pieces[3].shape[0] // step

    def body(mine_ref, *refs):
        out_ref, held_ref = refs[5:]
        collect(refs, held_ref, 0, tops)
        for which in range(GRP):
            out_ref[which] = held_ref[mine_ref[0] ^ which].astype(F32)

    return call(
        body,
        "place_rows",
        (rows // step,),
        [SMEM] + piece_blocks(pieces, step, wide),
        pl.BlockSpec((GRP, step, wide), lambda i: (0, i, 0)),
        shape((GRP, rows, wide), F32),
        (mine.reshape(1),) + tuple(pieces),
        deps,
        [pltpu.VMEM((GRP, step, wide), BF16)],
    ).reshape(GRP * rows, wide)


def place_stacked(mine, pieces, first, own, deps=()):
    rows = pieces[0].shape[0]
    count = rows // GRP
    tops = pieces[3].shape[0] // count

    def body(mine_ref, *refs):
        out_ref, held_ref = refs[5:]
        collect(refs, held_ref, 0, tops)
        for which in range(GRP):
            out_ref[which * count : (which + 1) * count, :] = held_ref[mine_ref[0] ^ which].astype(F32)

    return call(
        body,
        "place_stacked",
        (GRP,),
        [SMEM] + piece_blocks(pieces, count, own, lambda i: first // own),
        pl.BlockSpec((rows, own), lambda j: (0, j)),
        shape((rows, GRP * own), F32),
        (mine.reshape(1),) + tuple(pieces),
        deps,
        [pltpu.VMEM((GRP, count, own), BF16)],
    )


def on_device(
    tokens,
    seq_lengths,
    cotangent,
    norm_gain,
    input_proj,
    forget_proj,
    forget_bias,
    gate_proj,
    state_gain,
    out_proj,
    mlp_gain,
    mlp_gate,
    mlp_up,
    mlp_down,
):
    tok_rows, width = tokens.shape
    half = tok_rows // 2
    plane = GRP * tok_rows
    parts = lax.axis_size("seq")
    mine, place = lax.axis_index("grp"), lax.axis_index("seq")
    own = width // GRP

    def own_rows(matrix):
        count = matrix.shape[0] // GRP
        return lax.dynamic_slice_in_dim(matrix, mine * count, count, 0)

    def own_features(vector):
        cut = vector.reshape(parts, GRP, -1)
        return lax.dynamic_index_in_dim(cut, mine, 1, False).reshape(1, -1)

    def all_features(vector):
        cut = vector.reshape(parts, 1, -1)
        spread = jnp.where(jnp.arange(GRP)[None, :, None] == mine, cut, 0.0)
        return spread.reshape(-1)

    def whole(rows):
        return lax.all_gather(rows, "seq", axis=0, tiled=True)

    def reduced(grads):
        return lax.psum_scatter(grads, "seq", scatter_dimension=0, tiled=True)

    starts = (jnp.cumsum(seq_lengths[0]) - seq_lengths[0]).astype(jnp.int32)
    starts = jnp.concatenate([(place * tok_rows).reshape(1).astype(jnp.int32), starts])
    info = place.reshape(1).astype(jnp.int32)
    bias = own_features(forget_bias)
    gain = own_features(state_gain)
    in_gain, mid_gain = norm_gain.reshape(1, -1), mlp_gain.reshape(1, -1)

    w_first = whole(pick_first(mine, input_proj, forget_proj, gate_proj, out_proj, parts))
    normed = norm_in(tokens, starts, in_gain, width)
    cot_held = start_gather(cotangent)
    held = start_gather(normed)
    ff_cols = pick_columns(mine, (mlp_gate, mlp_up), parts, True, (normed,))
    w_ff = whole(ff_cols)
    w_down = whole(own_rows(mlp_down))
    normed = end_gather(held, (ff_cols,))
    cot_pieces = second_step(cot_held)
    keep = normed[:, width:].astype(F32).reshape(8, half, LANE)

    proj = product("proj_pair", normed, w_first, width, 0, 2 * own, 256, cot_pieces).reshape(
        8, half, 2 * own
    )
    prod, state, ends = scan_forward(keep, proj, bias)
    ends, _ = all_ends(ends, parts)
    proj_gate = product("proj_gate", normed, w_first, width, 2 * own, own, 256, (prod,))
    proj_gate = proj_gate.reshape(8, half, own)
    states, mix, squares, enter = finish_forward(info, ends, prod, state, proj_gate, gain)
    mix, squares = mix.reshape(plane, own), squares.reshape(plane, LANE)
    w_stacked = w_first.reshape(parts, -1, 4 * own)
    to_x, to_y, kept = partial_sums(
        "mix", NN, (mix,), (w_stacked,), own, squares, stacked=(width, parts, 3 * own)
    )
    by_x, by_y = send_x(to_x), send_y(to_y)
    w_out = take_out(w_stacked, parts, own, (to_x,))
    cot = lay(cot_pieces, (w_out,))
    for_y, for_x = merge("mix_merge", kept, by_x, by_y, squares, (cot,))
    pieces = (kept, by_x, by_y, send_y(for_y), send_x(for_x), squares)
    middle, normed_mid, raw, scale_state, scale_mid = finish_mix(pieces, tokens, mid_gain, width)
    normed_mid = gather_rows(normed_mid)
    hidden, by_gate, by_up = feed_forward(normed_mid, w_ff)
    part_down = outer_sum("part_down", hidden, cot, hidden.shape[1], width, -512)
    sum_down = reduced(part_down)

    to_x, to_y, kept_out = partial_sums("down", NN, (hidden,), (w_down,), 256, deps=(part_down,))
    by_x_out, by_y_out = send_x(to_x), send_y(to_y)
    grad_ff = feed_back(cot, w_down, by_gate, by_up, (to_x,))
    to_x, to_y, kept = partial_sums("grad_mid", NT, (grad_ff,), (w_ff,), 256)
    by_x, by_y = send_x(to_x), send_y(to_y)
    part_ff = outer_sum("part_ff", normed_mid, grad_ff, width, grad_ff.shape[1], 256, (to_x,))
    sum_ff = reduced(part_ff)
    out_for_y, out_for_x = merge("down_merge", kept_out, by_x_out, by_y_out, None, (part_ff,))
    out_last_y, out_last_x = send_y(out_for_y), send_x(out_for_x)
    pieces_out = (kept_out, by_x_out, by_y_out, out_last_y, out_last_x)
    for_y, for_x = merge("grad_mid_merge", kept, by_x, by_y, deps=(out_for_y,))
    block_out = add_scattered(pieces_out, middle, BF16, width, (for_y,))
    pieces = (kept, by_x, by_y, send_y(for_y), send_x(for_x))
    grad_middle, scaled_mix, grad_mlp_gain = finish_mid(
        pieces,
        middle,
        cotangent,
        raw,
        scale_state,
        scale_mid,
        mid_gain,
        width,
        (block_out,),
    )
    held = start_gather(scaled_mix)
    grad_mix = end_gather(held)
    held_down = start_gather(after(sum_down, grad_mix))
    back, coupling = product_back("back", grad_mix, w_out, 256)
    after_prod, local, ends_back, grad_gate, gain_sum = scan_backward(
        keep,
        proj,
        proj_gate,
        bias,
        gain,
        states,
        back.reshape(8, half, own),
        coupling.reshape(8, half, LANE),
    )
    grad_gate = grad_gate.reshape(plane, own)
    part_gate_out, _ = outer_gate_out(
        normed,
        grad_gate,
        mix,
        grad_mix,
        parts,
        width,
        (after_prod,),
        lambda deps: (held_down[1], held_down[2]),
    )
    sum_gate_out = reduced(part_gate_out)
    ends_back = lax.all_gather(after(ends_back, part_gate_out), "seq")
    grad_pair, bias_sum = finish_backward(
        info, keep, ends_back, after_prod, local, proj, bias, states, enter, (part_gate_out,)
    )
    grad_pair = grad_pair.reshape(plane, 2 * own)
    held_ff = start_gather(after(sum_ff, part_gate_out))
    to_x, to_y, kept = partial_sums(
        "grad_in", NT, (grad_pair, grad_gate), (w_first, w_first), 256, firsts=(0, 2 * own)
    )
    by_x, by_y = send_x(to_x), send_y(to_y)
    down_pieces = second_step(held_down)
    part_pair = outer_sum(
        "part_pair", normed, grad_pair, width, 2 * own, 256, (to_x,) + down_pieces[3:] + held_ff[1:]
    )
    sum_pair = reduced(part_pair)
    grad_down = place_rows(mine, down_pieces, (part_pair, held_ff[1], held_ff[2]))
    for_y, for_x = merge("grad_in_merge", kept, by_x, by_y, deps=(grad_down,))
    last_y, last_x = send_y(for_y), send_x(for_x)
    pieces = (kept, by_x, by_y, last_y, last_x)
    held_go = start_gather(after(sum_gate_out, pieces[3], pieces[4]))
    ff_pieces = second_step(held_ff)
    grad_tokens, grad_norm_gain = finish_in(
        pieces, tokens, grad_middle, in_gain, width, ff_pieces[3:]
    )
    vectors = sum_everywhere(
        jnp.stack(
            [grad_norm_gain[0], all_features(bias_sum), all_features(gain_sum), grad_mlp_gain[0]]
        )
    )
    held_pair = start_gather(after(sum_pair, grad_tokens))
    grad_mlp_gate, grad_mlp_up = place_columns(
        mine, ff_pieces, parts, 2, w_ff.shape[1] // 2, True, (grad_tokens,)
    )
    gate_out_pieces = second_step(held_go, (grad_mlp_up,))
    (grad_gate_proj,) = place_columns(
        mine, gate_out_pieces, parts, 1, own, True, (grad_mlp_up,)
    )
    grad_out = place_stacked(mine, gate_out_pieces, own, own, (grad_gate_proj,))
    grad_input, grad_forget = place_columns(
        mine, second_step(held_pair, (grad_mlp_up,)), parts, 2, own, True, (grad_out,)
    )
    vectors = sum(after(vectors, grad_input))
    return (
        block_out,
        grad_tokens,
        vectors[0],
        grad_input,
        grad_forget,
        vectors[1],
        grad_gate_proj,
        vectors[2],
        grad_out,
        vectors[3],
        grad_mlp_gate,
        grad_mlp_up,
        grad_down,
    )


def solution(mesh):
    rows = P("seq", None)
    tokens = P(("grp", "seq"), None)
    return jax.shard_map(
        on_device,
        mesh=mesh,
        in_specs=(
            tokens,
            P("grp", None),
            tokens,
            P(),
            rows,
            rows,
            P(),
            rows,
            P(),
            rows,
            P(),
            rows,
            rows,
            rows,
        ),
        out_specs=(
            tokens,
            tokens,
            P(),
            rows,
            rows,
            P(),
            rows,
            P(),
            rows,
            P(),
            rows,
            rows,
            rows,
        ),
        check_vma=False,
    )
```
